32 devices in a mesh: section: 4 (over x, core), dom: 8 (over z, y).
Axes of the slice: x: 2, y: 2, z: 4, core: 2. Of those that a mesh axis runs over, the one named last changes fastest.
Arguments:
- initial_features: bfloat16 [12288, 384], P('dom'), may hold values from -16 to 16
- layer_weights: bfloat16 [8, 384, 384], P('section'), may hold values from -0.3125 to 0.3125
- adjacency_tiles: bfloat16 [96, 24, 128, 128], P('dom'), may hold values from -0.15625 to 0.15625
- tile_columns: int32 [96, 24], P('dom'), may hold values from 0 to 35, as said below
- send_blocks: int32 [8, 3, 8], P('dom'), may hold values from -1 to 3, as said below
- stale_imports: bfloat16 [8, 8, 16, 128, 384], P('section', 'dom'), may hold values from 0 to 1.5
Outputs:
- final_features: bfloat16 [12288, 384], P('dom', 'section')
The draws below stay inside these ranges and needn't reach their ends.
Inputs may be any that keep to these rules, and one draw needn't show every extreme that they name: send_blocks[q, h, p] is -1 when q equals p, else -1 or a block index of 0 to 3 within row group h. `tile_columns`: for a tile of partition p's local block r: a value j < 12 names p's own block j with j // 4 <= r // 4; a value 12 + h*8 + q names an import slot with send_blocks[q, h, p] >= 0.
All inputs are finite; a program needn't handle non-finite values.
Results may differ from the reference program's by a relative error of at most 0.011.
Values may be sent and summed in bfloat16 or wider, within the bound.
No kernel may reach another device: no remote copies, remote signals or barrier semaphores. Data moves between devices by JAX's collectives and lax.ppermute only.
A program may use at most 256 MiB of HBM per device.

```python
import jax
import jax.numpy as jnp
from jax import lax

D = 384
BLOCK = 128
TILES = 24
GROUPS = 3
GROUP_BLOCKS = 4
PARTITIONS = 8
LAYERS = 8
BLOCKS_DEV = 12
NBLK = 96
SLOTS = 24
STALE_SLOTS = 16
NODES = 12288


def graph_tables(key):
    base = jax.random.fold_in(key, 311)
    key_use, key_pick, key_score = jax.random.split(base, 3)
    usable = jax.random.randint(key_use, (PARTITIONS, GROUPS, PARTITIONS), 0, 5) < 3
    usable = usable.at[PARTITIONS - 1, GROUPS - 1, 0].set(True)
    picks = jax.random.randint(key_pick, (PARTITIONS, GROUPS, PARTITIONS), 0, GROUP_BLOCKS)
    diagonal = jnp.arange(PARTITIONS)[:, None, None] == jnp.arange(PARTITIONS)[None, None, :]
    sends = jnp.where(usable & ~diagonal, picks, -1).astype(jnp.int32)
    row_group = jnp.arange(BLOCKS_DEV) // GROUP_BLOCKS
    own_ok = jnp.arange(BLOCKS_DEV)[None, :] // GROUP_BLOCKS <= row_group[:, None]
    import_ok = (sends >= 0).transpose(2, 1, 0).reshape(PARTITIONS, SLOTS)
    own_full = jnp.broadcast_to(own_ok[None, :, :], (PARTITIONS, BLOCKS_DEV, BLOCKS_DEV))
    import_full = jnp.broadcast_to(import_ok[:, None, :], (PARTITIONS, BLOCKS_DEV, SLOTS))
    valid = jnp.concatenate([own_full, import_full], -1)
    total = BLOCKS_DEV + SLOTS
    scores = jax.random.randint(key_score, (PARTITIONS, BLOCKS_DEV, TILES, total), 0, 1 << 20) * 256
    scores = scores + jnp.arange(total, dtype=jnp.int32)[None, None, None, :]
    scores = jnp.where(valid[:, :, None, :], scores, -1)
    columns = jnp.argmax(scores, -1).astype(jnp.int32).reshape(NBLK, TILES)
    columns = columns.at[BLOCKS_DEV - 1, 0].set(total - 1)
    columns = columns.at[0, 0].set(0)
    return (sends, columns.astype(jnp.int32))


def draw_tile_columns(key, part):
    return graph_tables(key)[1]


def draw_send_blocks(key, part):
    return graph_tables(key)[0]


def block_scale(stream_key, dims, cuts, low, top_value):
    factor_of = 1.0
    for dim, parts in cuts:
        steps = jax.random.uniform(jax.random.fold_in(jax.random.fold_in(stream_key, 6), dim), (parts,), jnp.float32, low / len(cuts), top_value / len(cuts))
        factor_of = factor_of * jnp.repeat(jnp.exp(steps), dims[dim] // parts).reshape((-1,) + (1,) * (len(dims) - 1 - dim))
    return factor_of


def gaussian(key, shape, spread, reach, cuts=(), kind=jnp.bfloat16):
    drawn = jax.random.normal(key, shape, jnp.float32) * spread
    if len(cuts) > 0:
        drawn = block_scale(key, shape, cuts, -0.22, 0.18) * drawn
    return jnp.clip(drawn, min=-reach, max=reach).astype(kind)


def setup_inputs(seed: int = 0) -> dict:
    keys = jax.random.split(jax.random.key(seed), 7)
    initial_features = gaussian(keys[0], (NODES, D), 4.0, 16.0, ((0, 8),))
    layer_weights = gaussian(keys[1], (LAYERS, D, D), D ** -0.5, 0.3125, ((0, 4),))
    adjacency_tiles = gaussian(keys[2], (NBLK, TILES, BLOCK, BLOCK), (TILES * BLOCK // 2) ** -0.5, 0.15625, ((0, 8),))
    tile_columns = draw_tile_columns(jax.random.fold_in(keys[6], 71), 0)
    send_blocks = draw_send_blocks(jax.random.fold_in(keys[6], 71), 0)
    stale_imports = jnp.clip(1.5 * jax.random.uniform(keys[5], (LAYERS, PARTITIONS, STALE_SLOTS, BLOCK, D), jnp.float32) ** block_scale(keys[5], (LAYERS, PARTITIONS, STALE_SLOTS, BLOCK, D), ((0, 4), (1, 8)), -0.2, 0.2), 0.0, 1.5).astype(jnp.bfloat16)
    return dict(initial_features=initial_features, layer_weights=layer_weights, adjacency_tiles=adjacency_tiles, tile_columns=tile_columns, send_blocks=send_blocks, stale_imports=stale_imports)


alpha_mix = 0.1
lambda_decay = 0.5


def finish(summed, initial_rows, weight, beta_layer):
    mixed = ((1.0 - alpha_mix) * summed + alpha_mix * initial_rows.astype(jnp.float32)).astype(jnp.bfloat16)
    flat = mixed.reshape(-1, mixed.shape[-1])
    product = jnp.dot(flat, weight, preferred_element_type=jnp.float32).reshape(mixed.shape)
    return jax.nn.relu((1.0 - beta_layer) * mixed.astype(jnp.float32) + beta_layer * product).astype(jnp.bfloat16)


def reference(initial_features, layer_weights, adjacency_tiles, tile_columns, send_blocks, stale_imports):
    part_total = PARTITIONS
    initial = initial_features.reshape(part_total, BLOCKS_DEV, BLOCK, D)
    tile_blocks = adjacency_tiles.reshape(part_total, BLOCKS_DEV, TILES, BLOCK, BLOCK)
    column_blocks = tile_columns.reshape(part_total, BLOCKS_DEV, TILES)
    offsets = jnp.arange(GROUPS, dtype=jnp.int32)[None, :, None] * GROUP_BLOCKS
    source_rows = (jnp.maximum(send_blocks, 0) + offsets).astype(jnp.int32)
    present = send_blocks >= 0
    slot_group = jnp.arange(SLOTS, dtype=jnp.int32) // PARTITIONS
    part_ids = jnp.arange(part_total, dtype=jnp.int32)[:, None, None]

    def one_layer(features, inputs):
        weight, stale_layer, layer_index = inputs
        beta_layer = jnp.log(lambda_decay / (layer_index.astype(jnp.float32) + 1.0) + 1.0)
        picked = features[part_ids, source_rows]
        picked = jnp.where(present[..., None, None], picked, jnp.zeros_like(picked))
        fresh_all = picked.transpose(2, 1, 0, 3, 4).reshape(part_total, SLOTS, BLOCK, D)

        def per_part(pieces):
            own_blocks, fresh_part, stale_part, init_part, tile_part, column_part = pieces
            stale_full = jnp.concatenate([jnp.zeros((PARTITIONS, BLOCK, D), jnp.bfloat16), stale_part], 0)
            finished = []
            for group_index in range(GROUPS):
                imports = jnp.where((slot_group <= group_index)[:, None, None], fresh_part, stale_full)
                table = jnp.concatenate([own_blocks, imports], 0)
                low = group_index * GROUP_BLOCKS
                high = low + GROUP_BLOCKS
                gathered = table[column_part[low:high]]
                summed = jnp.einsum("rkij,rkjd->rid", tile_part[low:high].astype(jnp.float32), gathered.astype(jnp.float32))
                finished.append(finish(summed, init_part[low:high], weight, beta_layer))
            return jnp.concatenate(finished, 0)

        advanced = lax.map(per_part, (features, fresh_all, stale_layer, initial, tile_blocks, column_blocks))
        return advanced, None

    result, unused = lax.scan(one_layer, initial, (layer_weights, stale_imports, jnp.arange(LAYERS, dtype=jnp.int32)))
    return result.reshape(NODES, D)
```

```python
import functools
import math

import jax
import jax.numpy as jnp
from jax import lax
from jax.experimental import pallas as pl
from jax.experimental.pallas import tpu as pltpu
from jax.sharding import PartitionSpec as P

alpha_mix = 0.1
lambda_decay = 0.5
vmem_bytes = 48 * 1024 * 1024


def group_streams(groups):
    return [list(range(groups))]


def params():
    return pltpu.CompilerParams(vmem_limit_bytes=vmem_bytes)


def whole(shape):
    return pl.BlockSpec(shape, lambda i, *prefetched: (0,) * len(shape))


def pick_outgoing(picks, blocks_ref, outgoing_ref, stream, group_blocks, part_count):
    for local, group in enumerate(stream):

        def pick(dest, carry):
            chosen = jnp.maximum(picks[group * part_count + dest], 0)
            outgoing_ref[dest, local] = blocks_ref[local * group_blocks + chosen]
            return carry

        lax.fori_loop(0, part_count, pick, 0)


def prologue_kernel(streams, group_blocks, part_count, info, picks, rows_ref, *refs):
    own_refs = refs[: len(streams)]
    outgoing_refs = refs[len(streams) : 2 * len(streams)]
    turned = refs[-1]
    block = own_refs[0].shape[2]
    part_width = own_refs[0].shape[1]
    first = pl.multiple_of(info[0] * part_width, part_width)
    for stream, own_ref, outgoing_ref in zip(streams, own_refs, outgoing_refs):
        for local in range(len(stream) * group_blocks):
            row = (stream[0] * group_blocks + local) * block
            turned[local % 2] = rows_ref[row : row + block, :].T
            own_ref[local] = turned[local % 2, pl.ds(first, part_width), :]
        pick_outgoing(picks, own_ref, outgoing_ref, stream, group_blocks, part_count)


def prologue(initial_features, section, picks, streams, group_blocks, block, part_width, part_count):
    rows, width = initial_features.shape
    own_shapes = [(len(s) * group_blocks, part_width, block) for s in streams]
    out_shapes = [(part_count, len(s), part_width, block) for s in streams]
    return pl.pallas_call(
        functools.partial(prologue_kernel, streams, group_blocks, part_count),
        grid_spec=pltpu.PrefetchScalarGridSpec(
            num_scalar_prefetch=2,
            grid=(1,),
            in_specs=[whole((rows, width))],
            out_specs=[whole(s) for s in own_shapes + out_shapes],
            scratch_shapes=[pltpu.VMEM((2, width, block), jnp.bfloat16)],
        ),
        out_shape=[jax.ShapeDtypeStruct(s, jnp.bfloat16) for s in own_shapes + out_shapes],
        compiler_params=params(),
        name="prologue",
    )(section, picks, initial_features)


def turn_kernel(in_ref, out_ref):
    count = in_ref.shape[0]
    parts, part_width = out_ref.shape[0], out_ref.shape[2]
    for item in range(count):
        turned = in_ref[item].T
        for part in range(parts):
            out_ref[part, item] = turned[part * part_width : (part + 1) * part_width, :]


def turn_blocks(blocks, parts):
    count, block, width = blocks.shape
    step = 4 if count % 4 == 0 else 1
    part_width = width // parts
    return pl.pallas_call(
        turn_kernel,
        grid=(count // step,),
        in_specs=[pl.BlockSpec((step, block, width), lambda i: (i, 0, 0))],
        out_specs=pl.BlockSpec((parts, step, part_width, block), lambda i: (0, i, 0, 0)),
        out_shape=jax.ShapeDtypeStruct((parts, count, part_width, block), jnp.bfloat16),
        compiler_params=params(),
        name="turn",
    )(blocks)


def aggregate_kernel(plan, columns, initial_ref, tiles_ref, *refs):
    stream, group_blocks, fanout, sources, layer_slot = plan
    source_refs = refs[: len(sources)]
    mixed_ref, table, tiles, table_sem, tiles_sem = refs[len(sources) :]
    rows = len(stream) * group_blocks
    first_row = stream[0] * group_blocks

    def tile_copy(row):
        return pltpu.make_async_copy(tiles_ref.at[first_row + row], tiles.at[row], tiles_sem.at[row])

    copies = []
    for index, (kind, target, detail) in enumerate(sources):
        ref = source_refs[index]
        if kind == "own":
            source = ref
        elif kind == "import":
            source = ref.at[:, detail]
        else:
            source = ref.at[layer_slot]
        count = source.shape[0]
        copies.append(
            pltpu.make_async_copy(source, table.at[pl.ds(target, count)], table_sem.at[index])
        )
    for copy in copies:
        copy.start()
    for row in range(rows):
        tile_copy(row).start()
    for copy in copies:
        copy.wait()

    def one_row(row, carry):
        tile_copy(row).wait()
        base = (first_row + row) * fanout
        total = None
        for tile in range(0, fanout, 2):
            span = range(tile, min(tile + 2, fanout))
            left = jnp.concatenate([table[columns[base + t]] for t in span], 1)
            right = jnp.concatenate([tiles[row, t] for t in span], 1)
            term = lax.dot_general(
                left, right, (((1,), (1,)), ((), ())), preferred_element_type=jnp.float32
            )
            total = term if total is None else total + term
        mixed_ref[row] = (
            (1.0 - alpha_mix) * total + alpha_mix * initial_ref[row].astype(jnp.float32)
        ).astype(jnp.bfloat16)
        return carry

    lax.fori_loop(0, rows, one_row, 0)


def aggregate(columns, initial_blocks, tiles, own, imports, stale, layer_slot, stream, streams, group_blocks, part_count):
    rows, part_width, block = initial_blocks.shape
    blocks_dev, fanout = tiles.shape[:2]
    groups = blocks_dev // group_blocks
    sources, operands = [], []
    for other, own_blocks, imported in zip(streams, own, imports):
        if other[0] > stream[-1]:
            continue
        sources.append(("own", other[0] * group_blocks, None))
        operands.append(own_blocks)
        for local, group in enumerate(other):
            sources.append(("import", blocks_dev + group * part_count, local))
            operands.append(imported)
    if groups > 1 and stream[0] < groups - 1:
        sources.append(("stale", blocks_dev + groups * part_count, None))
        operands.append(stale)
    table_size = blocks_dev + (2 * groups - 1) * part_count
    plan = (stream, group_blocks, fanout, sources, layer_slot)
    flops = 2 * rows * fanout * block * block * part_width
    return pl.pallas_call(
        functools.partial(aggregate_kernel, plan),
        grid_spec=pltpu.PrefetchScalarGridSpec(
            num_scalar_prefetch=1,
            grid=(1,),
            in_specs=[whole(initial_blocks.shape)]
            + [pl.BlockSpec(memory_space=pl.ANY)] * (1 + len(operands)),
            out_specs=whole((rows, part_width, block)),
            scratch_shapes=[
                pltpu.VMEM((table_size, part_width, block), jnp.bfloat16),
                pltpu.VMEM((rows, fanout, block, block), jnp.bfloat16),
                pltpu.SemaphoreType.DMA((len(sources),)),
                pltpu.SemaphoreType.DMA((rows,)),
            ],
        ),
        out_shape=jax.ShapeDtypeStruct((rows, part_width, block), jnp.bfloat16),
        cost_estimate=pl.CostEstimate(
            flops=flops, bytes_accessed=rows * fanout * block * block * 2, transcendentals=0
        ),
        compiler_params=params(),
        name="aggregate",
    )(columns, initial_blocks, tiles, *operands)


def finish_kernel(plan, picks, mixed_ref, gathered_ref, weight_ref, *refs):
    beta_layer, stream, group_blocks, part_count, last = plan
    rows, part_width, block = mixed_ref.shape
    parts = gathered_ref.shape[0]
    weight = weight_ref[0]
    for row in range(0, rows, 2):
        span = range(row, min(row + 2, rows))
        right = jnp.concatenate(
            [jnp.concatenate([gathered_ref[p, r] for p in range(parts)], 0) for r in span], 1
        )
        product = jnp.dot(weight, right, preferred_element_type=jnp.float32)
        for place, r in enumerate(span):
            value = (1.0 - beta_layer) * mixed_ref[r].astype(jnp.float32) + beta_layer * product[
                :, place * block : (place + 1) * block
            ]
            value = jnp.maximum(value, 0.0).astype(jnp.bfloat16)
            if last:
                refs[0][r * block : (r + 1) * block, :] = value.T
            else:
                refs[0][r] = value
    if not last:
        pick_outgoing(picks, refs[0], refs[1], stream, group_blocks, part_count)


def finish(picks, mixed, gathered, weights, layer, stream, group_blocks, part_count, last):
    rows, part_width, block = mixed.shape
    width = weights.shape[2]
    beta_layer = math.log(lambda_decay / (layer + 1) + 1.0)
    plan = (beta_layer, stream, group_blocks, part_count, last)
    if last:
        shapes = [(rows * block, part_width)]
    else:
        shapes = [(rows, part_width, block), (part_count, len(stream), part_width, block)]
    return pl.pallas_call(
        functools.partial(finish_kernel, plan),
        grid_spec=pltpu.PrefetchScalarGridSpec(
            num_scalar_prefetch=1,
            grid=(1,),
            in_specs=[
                whole(mixed.shape),
                whole(gathered.shape),
                pl.BlockSpec((1, part_width, width), lambda i, *prefetched: (layer, 0, 0)),
            ],
            out_specs=[whole(s) for s in shapes],
        ),
        out_shape=[jax.ShapeDtypeStruct(s, jnp.bfloat16) for s in shapes],
        cost_estimate=pl.CostEstimate(
            flops=2 * rows * block * width * part_width,
            bytes_accessed=rows * block * width * 2,
            transcendentals=0,
        ),
        compiler_params=params(),
        name="finish",
    )(picks, mixed, gathered, weights)


def per_device(
    initial_features, layer_weights, adjacency_tiles, tile_columns, send_blocks, stale_imports
):
    section_count = lax.axis_size("section")
    part_count = lax.axis_size("dom")
    blocks_dev, fanout, block = adjacency_tiles.shape[:3]
    width = initial_features.shape[1]
    part_width = width // section_count
    groups = send_blocks.shape[1]
    group_blocks = blocks_dev // groups
    depth = layer_weights.shape[0]
    layers = depth * section_count
    streams = group_streams(groups)
    section = lax.axis_index("section").astype(jnp.int32).reshape(1)
    picks = send_blocks.reshape(-1)

    row_group = (jnp.arange(blocks_dev, dtype=jnp.int32) // group_blocks)[:, None]
    slot_group = (tile_columns - blocks_dev) // part_count
    is_stale = (tile_columns >= blocks_dev) & (slot_group > row_group)
    columns = jnp.where(
        is_stale, tile_columns + (groups - 1) * part_count, tile_columns
    ).reshape(-1)

    started = prologue(
        initial_features, section, picks, streams, group_blocks, block, part_width, part_count
    )
    own = started[: len(streams)]
    outgoing = started[len(streams) :]
    initial_blocks = own

    def exchange(value):
        return lax.all_to_all(value, "dom", split_axis=0, concat_axis=0, tiled=True)

    imports = [exchange(value) for value in outgoing]
    stale = [
        lax.all_to_all(
            turn_blocks(stale_imports[sub, 0], section_count),
            "section",
            split_axis=0,
            concat_axis=0,
            tiled=True,
        )
        for sub in range(depth)
    ]
    weights = lax.all_to_all(
        layer_weights.transpose(0, 2, 1).reshape(depth, section_count, part_width, width),
        "section",
        split_axis=1,
        concat_axis=0,
        tiled=True,
    ).reshape(layers, part_width, width)

    pieces = []
    for layer in range(layers):
        last = layer == layers - 1
        own_next, imports_next = [], []
        for index, stream in enumerate(streams):
            mixed = aggregate(
                columns,
                initial_blocks[index],
                adjacency_tiles,
                own,
                imports,
                stale[layer % depth],
                layer // depth,
                stream,
                streams,
                group_blocks,
                part_count,
            )
            gathered = lax.all_gather(mixed, "section", axis=0, tiled=False)
            result = finish(
                picks, mixed, gathered, weights, layer, stream, group_blocks, part_count, last
            )
            if last:
                pieces.append(result[0])
            else:
                own_next.append(result[0])
                imports_next.append(exchange(result[1]))
        own, imports = own_next, imports_next
    return jnp.concatenate(pieces, 0) if len(pieces) > 1 else pieces[0]


def solution(mesh):
    return jax.shard_map(
        per_device,
        mesh=mesh,
        in_specs=(
            P("dom", None),
            P("section", None, None),
            P("dom", None, None, None),
            P("dom", None),
            P("dom", None, None),
            P("section", "dom", None, None, None),
        ),
        out_specs=P("dom", "section"),
        check_vma=False,
    )
```

```python
import functools
import math

import jax
import jax.numpy as jnp
from jax import lax
from jax.experimental import pallas as pl
from jax.experimental.pallas import tpu as pltpu
from jax.sharding import PartitionSpec as P

alpha_mix = 0.1
lambda_decay = 0.5
vmem_bytes = 48 * 1024 * 1024


def group_streams(groups):
    return [[group] for group in range(groups)]


def params():
    return pltpu.CompilerParams(vmem_limit_bytes=vmem_bytes)


def whole(shape):
    return pl.BlockSpec(shape, lambda i, *prefetched: (0,) * len(shape))


def pick_outgoing(picks, blocks_ref, outgoing_ref, stream, group_blocks, part_count):
    for local, group in enumerate(stream):

        def pick(dest, carry):
            chosen = jnp.maximum(picks[group * part_count + dest], 0)
            outgoing_ref[dest, local] = blocks_ref[local * group_blocks + chosen]
            return carry

        lax.fori_loop(0, part_count, pick, 0)


def prologue_kernel(streams, group_blocks, part_count, info, picks, rows_ref, *refs):
    own_refs = refs[: len(streams)]
    outgoing_refs = refs[len(streams) : 2 * len(streams)]
    turned = refs[-1]
    block = own_refs[0].shape[2]
    part_width = own_refs[0].shape[1]
    first = pl.multiple_of(info[0] * part_width, part_width)
    for stream, own_ref, outgoing_ref in zip(streams, own_refs, outgoing_refs):
        for local in range(len(stream) * group_blocks):
            row = (stream[0] * group_blocks + local) * block
            turned[local % 2] = rows_ref[row : row + block, :].T
            own_ref[local] = turned[local % 2, pl.ds(first, part_width), :]
        pick_outgoing(picks, own_ref, outgoing_ref, stream, group_blocks, part_count)


def prologue(initial_features, section, picks, streams, group_blocks, block, part_width, part_count):
    rows, width = initial_features.shape
    own_shapes = [(len(s) * group_blocks, part_width, block) for s in streams]
    out_shapes = [(part_count, len(s), part_width, block) for s in streams]
    return pl.pallas_call(
        functools.partial(prologue_kernel, streams, group_blocks, part_count),
        grid_spec=pltpu.PrefetchScalarGridSpec(
            num_scalar_prefetch=2,
            grid=(1,),
            in_specs=[whole((rows, width))],
            out_specs=[whole(s) for s in own_shapes + out_shapes],
            scratch_shapes=[pltpu.VMEM((2, width, block), jnp.bfloat16)],
        ),
        out_shape=[jax.ShapeDtypeStruct(s, jnp.bfloat16) for s in own_shapes + out_shapes],
        compiler_params=params(),
        name="prologue",
    )(section, picks, initial_features)


def turn_kernel(in_ref, out_ref):
    count = in_ref.shape[0]
    parts, part_width = out_ref.shape[0], out_ref.shape[2]
    for item in range(count):
        turned = in_ref[item].T
        for part in range(parts):
            out_ref[part, item] = turned[part * part_width : (part + 1) * part_width, :]


def turn_blocks(blocks, parts):
    count, block, width = blocks.shape
    step = 4 if count % 4 == 0 else 1
    part_width = width // parts
    return pl.pallas_call(
        turn_kernel,
        grid=(count // step,),
        in_specs=[pl.BlockSpec((step, block, width), lambda i: (i, 0, 0))],
        out_specs=pl.BlockSpec((parts, step, part_width, block), lambda i: (0, i, 0, 0)),
        out_shape=jax.ShapeDtypeStruct((parts, count, part_width, block), jnp.bfloat16),
        compiler_params=params(),
        name="turn",
    )(blocks)


def aggregate_kernel(plan, columns, initial_ref, tiles_ref, *refs):
    stream, group_blocks, fanout, sources, layer_slot = plan
    source_refs = refs[: len(sources)]
    mixed_ref, table, tiles, table_sem, tiles_sem = refs[len(sources) :]
    rows = len(stream) * group_blocks
    first_row = stream[0] * group_blocks

    def tile_copy(row):
        return pltpu.make_async_copy(tiles_ref.at[first_row + row], tiles.at[row], tiles_sem.at[row])

    copies = []
    for index, (kind, target, detail) in enumerate(sources):
        ref = source_refs[index]
        if kind == "own":
            source = ref
        elif kind == "import":
            source = ref.at[:, detail]
        else:
            source = ref.at[layer_slot]
        count = source.shape[0]
        copies.append(
            pltpu.make_async_copy(source, table.at[pl.ds(target, count)], table_sem.at[index])
        )
    for copy in copies:
        copy.start()
    for row in range(rows):
        tile_copy(row).start()
    for copy in copies:
        copy.wait()

    def one_row(row, carry):
        tile_copy(row).wait()
        base = (first_row + row) * fanout
        total = None
        for tile in range(0, fanout, 2):
            span = range(tile, min(tile + 2, fanout))
            left = jnp.concatenate([table[columns[base + t]] for t in span], 1)
            right = jnp.concatenate([tiles[row, t] for t in span], 1)
            term = lax.dot_general(
                left, right, (((1,), (1,)), ((), ())), preferred_element_type=jnp.float32
            )
            total = term if total is None else total + term
        mixed_ref[row] = (
            (1.0 - alpha_mix) * total + alpha_mix * initial_ref[row].astype(jnp.float32)
        ).astype(jnp.bfloat16)
        return carry

    lax.fori_loop(0, rows, one_row, 0)


def aggregate(columns, initial_blocks, tiles, own, imports, stale, layer_slot, stream, streams, group_blocks, part_count):
    rows, part_width, block = initial_blocks.shape
    blocks_dev, fanout = tiles.shape[:2]
    groups = blocks_dev // group_blocks
    sources, operands = [], []
    for other, own_blocks, imported in zip(streams, own, imports):
        if other[0] > stream[-1]:
            continue
        sources.append(("own", other[0] * group_blocks, None))
        operands.append(own_blocks)
        for local, group in enumerate(other):
            sources.append(("import", blocks_dev + group * part_count, local))
            operands.append(imported)
    if groups > 1 and stream[0] < groups - 1:
        sources.append(("stale", blocks_dev + groups * part_count, None))
        operands.append(stale)
    table_size = blocks_dev + (2 * groups - 1) * part_count
    plan = (stream, group_blocks, fanout, sources, layer_slot)
    flops = 2 * rows * fanout * block * block * part_width
    return pl.pallas_call(
        functools.partial(aggregate_kernel, plan),
        grid_spec=pltpu.PrefetchScalarGridSpec(
            num_scalar_prefetch=1,
            grid=(1,),
            in_specs=[whole(initial_blocks.shape)]
            + [pl.BlockSpec(memory_space=pl.ANY)] * (1 + len(operands)),
            out_specs=whole((rows, part_width, block)),
            scratch_shapes=[
                pltpu.VMEM((table_size, part_width, block), jnp.bfloat16),
                pltpu.VMEM((rows, fanout, block, block), jnp.bfloat16),
                pltpu.SemaphoreType.DMA((len(sources),)),
                pltpu.SemaphoreType.DMA((rows,)),
            ],
        ),
        out_shape=jax.ShapeDtypeStruct((rows, part_width, block), jnp.bfloat16),
        cost_estimate=pl.CostEstimate(
            flops=flops, bytes_accessed=rows * fanout * block * block * 2, transcendentals=0
        ),
        compiler_params=params(),
        name="aggregate",
    )(columns, initial_blocks, tiles, *operands)


def finish_kernel(plan, picks, mixed_ref, gathered_ref, weight_ref, *refs):
    beta_layer, stream, group_blocks, part_count, last = plan
    *refs, held, held_sem = refs
    rows, part_width, block = mixed_ref.shape
    parts = gathered_ref.shape[0]
    spans = [(row, min(row + 2, rows)) for row in range(0, rows, 2)]
    copies = [
        pltpu.make_async_copy(
            gathered_ref.at[:, low:high], held.at[:, low:high], held_sem.at[index]
        )
        for index, (low, high) in enumerate(spans)
    ]
    for copy in copies:
        copy.start()
    weight = weight_ref[0]
    for copy, (low, high) in zip(copies, spans):
        copy.wait()
        span = range(low, high)
        right = jnp.concatenate(
            [jnp.concatenate([held[p, r] for p in range(parts)], 0) for r in span], 1
        )
        product = jnp.dot(weight, right, preferred_element_type=jnp.float32)
        for place, r in enumerate(span):
            value = (1.0 - beta_layer) * mixed_ref[r].astype(jnp.float32) + beta_layer * product[
                :, place * block : (place + 1) * block
            ]
            value = jnp.maximum(value, 0.0).astype(jnp.bfloat16)
            if last:
                refs[0][r * block : (r + 1) * block, :] = value.T
            else:
                refs[0][r] = value
    if not last:
        pick_outgoing(picks, refs[0], refs[1], stream, group_blocks, part_count)


def finish(picks, mixed, gathered, weights, layer, stream, group_blocks, part_count, last):
    rows, part_width, block = mixed.shape
    width = weights.shape[2]
    beta_layer = math.log(lambda_decay / (layer + 1) + 1.0)
    plan = (beta_layer, stream, group_blocks, part_count, last)
    if last:
        shapes = [(rows * block, part_width)]
    else:
        shapes = [(rows, part_width, block), (part_count, len(stream), part_width, block)]
    return pl.pallas_call(
        functools.partial(finish_kernel, plan),
        grid_spec=pltpu.PrefetchScalarGridSpec(
            num_scalar_prefetch=1,
            grid=(1,),
            in_specs=[
                whole(mixed.shape),
                pl.BlockSpec(memory_space=pl.ANY),
                pl.BlockSpec((1, part_width, width), lambda i, *prefetched: (layer, 0, 0)),
            ],
            out_specs=[whole(s) for s in shapes],
            scratch_shapes=[
                pltpu.VMEM(gathered.shape, jnp.bfloat16),
                pltpu.SemaphoreType.DMA(((rows + 1) // 2,)),
            ],
        ),
        out_shape=[jax.ShapeDtypeStruct(s, jnp.bfloat16) for s in shapes],
        cost_estimate=pl.CostEstimate(
            flops=2 * rows * block * width * part_width,
            bytes_accessed=rows * block * width * 2,
            transcendentals=0,
        ),
        compiler_params=params(),
        name="finish",
    )(picks, mixed, gathered, weights)


def per_device(
    initial_features, layer_weights, adjacency_tiles, tile_columns, send_blocks, stale_imports
):
    section_count = lax.axis_size("section")
    part_count = lax.axis_size("dom")
    blocks_dev, fanout, block = adjacency_tiles.shape[:3]
    width = initial_features.shape[1]
    part_width = width // section_count
    groups = send_blocks.shape[1]
    group_blocks = blocks_dev // groups
    depth = layer_weights.shape[0]
    layers = depth * section_count
    streams = group_streams(groups)
    section = lax.axis_index("section").astype(jnp.int32).reshape(1)
    picks = send_blocks.reshape(-1)

    row_group = (jnp.arange(blocks_dev, dtype=jnp.int32) // group_blocks)[:, None]
    slot_group = (tile_columns - blocks_dev) // part_count
    is_stale = (tile_columns >= blocks_dev) & (slot_group > row_group)
    columns = jnp.where(
        is_stale, tile_columns + (groups - 1) * part_count, tile_columns
    ).reshape(-1)

    started = prologue(
        initial_features, section, picks, streams, group_blocks, block, part_width, part_count
    )
    own = started[: len(streams)]
    outgoing = started[len(streams) :]
    initial_blocks = own

    def exchange(value):
        return lax.all_to_all(value, "dom", split_axis=0, concat_axis=0, tiled=True)

    imports = [exchange(value) for value in outgoing]
    stale = [
        lax.all_to_all(
            turn_blocks(stale_imports[sub, 0], section_count),
            "section",
            split_axis=0,
            concat_axis=0,
            tiled=True,
        )
        for sub in range(depth)
    ]
    weights = lax.all_to_all(
        layer_weights.transpose(0, 2, 1).reshape(depth, section_count, part_width, width),
        "section",
        split_axis=1,
        concat_axis=0,
        tiled=True,
    ).reshape(layers, part_width, width)

    pieces = []
    for layer in range(layers):
        last = layer == layers - 1
        own_next, imports_next = [], []
        for index, stream in enumerate(streams):
            mixed = aggregate(
                columns,
                initial_blocks[index],
                adjacency_tiles,
                own,
                imports,
                stale[layer % depth],
                layer // depth,
                stream,
                streams,
                group_blocks,
                part_count,
            )
            gathered = lax.all_gather(mixed, "section", axis=0, tiled=False)
            result = finish(
                picks, mixed, gathered, weights, layer, stream, group_blocks, part_count, last
            )
            if last:
                pieces.append(result[0])
            else:
                own_next.append(result[0])
                imports_next.append(exchange(result[1]))
        own, imports = own_next, imports_next
    return jnp.concatenate(pieces, 0) if len(pieces) > 1 else pieces[0]


def solution(mesh):
    return jax.shard_map(
        per_device,
        mesh=mesh,
        in_specs=(
            P("dom", None),
            P("section", None, None),
            P("dom", None, None, None),
            P("dom", None),
            P("dom", None, None),
            P("section", "dom", None, None, None),
        ),
        out_specs=P("dom", "section"),
        check_vma=False,
    )
```

```python
import functools
import math

import jax
import jax.numpy as jnp
from jax import lax
from jax.experimental import pallas as pl
from jax.experimental.pallas import tpu as pltpu
from jax.sharding import PartitionSpec as P

alpha_mix = 0.1
lambda_decay = 0.5
vmem_bytes = 24 * 1024 * 1024
anywhere = pl.BlockSpec(memory_space=pl.ANY)


def unit_of(tick, section, sections):
    group = (tick - section) % sections
    return group, tick - group


def start_when(condition, copy):
    pl.when(condition)(lambda: copy.start())


def wait_when(condition, copy):
    pl.when(condition)(lambda: copy.wait())


def tick_kernel(plan, info, columns, picks, *refs):
    tick, sections, parts, groups, depth, layers, history, moved_keys, sends, is_last = plan
    initial_ref, tiles_ref, stale_ref, weights_ref = refs[:4]
    refs = list(refs[4:])
    arrived = [[refs.pop(0) for _ in range(parts)] for _ in range(history)]
    moved = {key: (refs.pop(0), refs.pop(0)) for key in moved_keys}
    out_refs = [refs.pop(0) for _ in range(parts)] if sends else []
    final_refs = [refs.pop(0) for _ in range(sections)] if is_last else []
    table, tiles, stored_weight, initial, made, table_sem, tile_sem, other_sem, out_sem = refs
    fanout, block = tiles_ref.shape[1:3]
    blocks_dev = tiles_ref.shape[0]
    group_blocks = blocks_dev // groups
    width = initial_ref.shape[1]

    section, part = info[0], info[1]
    group = lax.rem(tick - section + 4 * sections, sections)
    layer = tick - group
    first_row = group * group_blocks
    computing = (group < groups) & (layer >= 0) & (layer < layers)
    passing = (group < groups) & (layer == -1)
    home = lax.div(jnp.maximum(layer, 0), depth)
    sub = lax.rem(jnp.maximum(layer, 0), depth)
    turn = lax.div(jnp.maximum(layer, 0), sections)

    first_initial = pl.multiple_of(first_row * block, block)
    initial_copy = pltpu.make_async_copy(
        initial_ref.at[pl.ds(first_initial, group_blocks * block)], initial, other_sem.at[0]
    )

    if history > 0:
        copies = []
        for back in range(history):
            known = computing & (group >= back)
            source_group = jnp.maximum(group - back, 0)
            sem = lambda index: table_sem.at[back * parts + index]
            copies.append(
                (
                    known,
                    pltpu.make_async_copy(
                        arrived[back][0],
                        table.at[pl.ds(source_group * group_blocks, group_blocks)],
                        sem(0),
                    ),
                )
            )
            for distance in range(1, parts):
                origin = lax.rem(part - distance + parts, parts)
                copies.append(
                    (
                        known,
                        pltpu.make_async_copy(
                            arrived[back][distance],
                            table.at[blocks_dev + source_group * parts + origin],
                            sem(distance),
                        ),
                    )
                )
        here = section == home
        sources = [(here, stale_ref.at[sub, 0], weights_ref.at[sub])]
        for (moved_turn, moved_sub), (moved_stale, moved_weight) in moved.items():
            chosen = jnp.logical_not(here) & (turn == moved_turn) & (sub == moved_sub)
            sources.append((chosen, moved_stale, moved_weight))
        for chosen, stale_source, weight_source in sources:
            for later in range(1, groups):
                copies.append(
                    (
                        computing & chosen & (group < later),
                        pltpu.make_async_copy(
                            stale_source.at[(later - 1) * parts : later * parts],
                            table.at[pl.ds(blocks_dev + later * parts, parts)],
                            other_sem.at[1 + later],
                        ),
                    )
                )
            copies.append(
                (
                    computing & chosen,
                    pltpu.make_async_copy(weight_source, stored_weight, other_sem.at[1]),
                )
            )

        def tile_copy(row):
            return pltpu.make_async_copy(
                tiles_ref.at[first_row + row], tiles.at[row], tile_sem.at[row]
            )

        for condition, copy in copies:
            start_when(condition, copy)

        @pl.when(computing)
        def _():
            for row in range(group_blocks):
                tile_copy(row).start()
            initial_copy.start()

        for condition, copy in copies:
            wait_when(condition, copy)

        @pl.when(computing)
        def _():
            initial_copy.wait()
            beta_layer = jnp.float32(0.0)
            for known_layer in range(max(tick - groups + 1, 0), min(tick, layers - 1) + 1):
                beta_layer = jnp.where(
                    layer == known_layer,
                    jnp.float32(math.log(lambda_decay / (known_layer + 1) + 1.0)),
                    beta_layer,
                )
            mixed_rows = []
            for row in range(group_blocks):
                tile_copy(row).wait()
                base = (first_row + row) * fanout
                total = None
                for tile in range(0, fanout, 2):
                    span = range(tile, min(tile + 2, fanout))
                    left = jnp.concatenate([tiles[row, t] for t in span], 1)
                    right = jnp.concatenate([table[columns[base + t]] for t in span], 0)
                    term = jnp.dot(left, right, preferred_element_type=jnp.float32)
                    total = term if total is None else total + term
                start = initial[row * block : (row + 1) * block].astype(jnp.float32)
                mixed = ((1.0 - alpha_mix) * total + alpha_mix * start).astype(jnp.bfloat16)
                product = jnp.dot(mixed, stored_weight[...], preferred_element_type=jnp.float32)
                value = (1.0 - beta_layer) * mixed.astype(jnp.float32) + beta_layer * product
                made[row] = jnp.maximum(value, 0.0).astype(jnp.bfloat16)

    if tick < groups - 1:

        @pl.when(passing)
        def _():
            initial_copy.start()
            initial_copy.wait()
            for row in range(group_blocks):
                made[row] = initial[row * block : (row + 1) * block]

    if sends:
        sending = passing | (computing & (layer < layers - 1))

        @pl.when(sending)
        def _():
            out_copies = [pltpu.make_async_copy(made, out_refs[0], out_sem.at[0])]
            for distance in range(1, parts):
                dest = lax.rem(part + distance, parts)
                chosen = jnp.maximum(picks[group * parts + dest], 0)
                out_copies.append(
                    pltpu.make_async_copy(
                        made.at[chosen], out_refs[distance], out_sem.at[distance]
                    )
                )
            for copy in out_copies:
                copy.start()
            for copy in out_copies:
                copy.wait()

    if is_last:

        @pl.when(computing & (layer == layers - 1))
        def _():
            piece = width // sections
            for index, final_ref in enumerate(final_refs):
                for row in range(group_blocks):
                    final_ref[row * block : (row + 1) * block, :] = made[row][
                        :, index * piece : (index + 1) * piece
                    ]


def run_tick(tick, scalars, arrays, arrived, moved, sizes):
    sections, parts, groups, depth, layers = sizes
    initial_features, tiles = arrays[:2]
    width = initial_features.shape[1]
    blocks_dev, fanout, block = tiles.shape[:3]
    group_blocks = blocks_dev // groups
    sends = tick < layers + groups - 2
    is_last = tick >= layers - 1
    units = [unit_of(tick, s, sections) for s in range(sections)]
    units = [(g, l) for g, l in units if g < groups and 0 <= l < layers]
    moved_keys = sorted(
        {(l // sections, l % depth) for g, l in units if l // depth != l % sections}
    )
    plan = (
        tick, sections, parts, groups, depth, layers, len(arrived), moved_keys, sends, is_last,
    )
    operands = list(arrays)
    for back in arrived:
        operands += back
    for key in moved_keys:
        operands += list(moved[key])
    out_shape, out_specs = [], []
    if sends:
        shapes = [(group_blocks, block, width)] + [(block, width)] * (parts - 1)
        out_shape += [jax.ShapeDtypeStruct(s, jnp.bfloat16) for s in shapes]
        out_specs += [anywhere] * parts
    if is_last:
        shape = (group_blocks * block, width // sections)
        out_shape += [jax.ShapeDtypeStruct(shape, jnp.bfloat16)] * sections
        out_specs += [pl.BlockSpec(shape, lambda i, *prefetched: (0, 0))] * sections
    work = group_blocks if units else 0
    results = pl.pallas_call(
        functools.partial(tick_kernel, plan),
        grid_spec=pltpu.PrefetchScalarGridSpec(
            num_scalar_prefetch=3,
            grid=(1,),
            in_specs=[anywhere] * len(operands),
            out_specs=out_specs,
            scratch_shapes=[
                pltpu.VMEM((blocks_dev + groups * parts, block, width), jnp.bfloat16),
                pltpu.VMEM((group_blocks, fanout, block, block), jnp.bfloat16),
                pltpu.VMEM((width, width), jnp.bfloat16),
                pltpu.VMEM((group_blocks * block, width), jnp.bfloat16),
                pltpu.VMEM((group_blocks, block, width), jnp.bfloat16),
                pltpu.SemaphoreType.DMA((groups * parts,)),
                pltpu.SemaphoreType.DMA((group_blocks,)),
                pltpu.SemaphoreType.DMA((groups + 1,)),
                pltpu.SemaphoreType.DMA((parts,)),
            ],
        ),
        out_shape=out_shape,
        cost_estimate=pl.CostEstimate(
            flops=2 * work * block * width * (fanout * block + width) + 1,
            bytes_accessed=work * fanout * block * (block + width) * 2 + 1,
            transcendentals=0,
        ),
        compiler_params=pltpu.CompilerParams(vmem_limit_bytes=vmem_bytes),
        name="tick",
    )(*scalars, *operands)
    return (results[:parts] if sends else []), (results[-sections:] if is_last else [])


def per_device(
    initial_features, layer_weights, adjacency_tiles, tile_columns, send_blocks, stale_imports
):
    sections = lax.axis_size("section")
    parts = lax.axis_size("dom")
    groups = send_blocks.shape[1]
    depth = layer_weights.shape[0]
    layers = depth * sections
    section = lax.axis_index("section").astype(jnp.int32)
    part = lax.axis_index("dom").astype(jnp.int32)
    scalars = (jnp.stack([section, part]), tile_columns.reshape(-1), send_blocks.reshape(-1))
    arrays = (initial_features, adjacency_tiles, stale_imports, layer_weights)
    sizes = (sections, parts, groups, depth, layers)

    def move(value, pairs, distance):
        routes = [
            (a * parts + q, b * parts + (q + distance) % parts) for a, b in pairs for q in range(parts)
        ]
        return lax.ppermute(value, ("section", "dom"), routes)

    routes = {}
    for layer in range(layers):
        if layer // depth != layer % sections:
            key = (layer // sections, layer % depth)
            routes.setdefault(key, []).append((layer // depth, layer % sections))
    moved = {
        key: (move(stale_imports[key[1], 0], pairs, 0), move(layer_weights[key[1]], pairs, 0))
        for key, pairs in sorted(routes.items())
    }

    arrived = []
    pieces = []
    for tick in range(-1, layers + groups - 1):
        outgoing, final = run_tick(tick, scalars, arrays, arrived, moved, sizes)
        senders = []
        for s in range(sections):
            group, layer = unit_of(tick, s, sections)
            if group < groups and -1 <= layer < layers - 1:
                senders.append((s, (s + 1) % sections))
        if outgoing:
            received = [move(value, senders, distance) for distance, value in enumerate(outgoing)]
            arrived = [received] + arrived[: groups - 1]
        if final:
            last = (layers - 1) % sections
            piece = final[last]
            for s in range(sections):
                if s != last:
                    piece = jnp.where(section == s, move(final[s], [(last, s)], 0), piece)
            pieces.append(piece)
    return jnp.concatenate(pieces, 0)


def solution(mesh):
    return jax.shard_map(
        per_device,
        mesh=mesh,
        in_specs=(
            P("dom", None),
            P("section", None, None),
            P("dom", None, None, None),
            P("dom", None),
            P("dom", None, None),
            P("section", "dom", None, None, None),
        ),
        out_specs=P("dom", "section"),
        check_vma=False,
    )
```

```python
import functools
import math

import jax
import jax.numpy as jnp
from jax import lax
from jax.experimental import pallas as pl
from jax.experimental.pallas import tpu as pltpu
from jax.sharding import PartitionSpec as P

alpha_mix = 0.1
lambda_decay = 0.5
vmem_bytes = 24 * 1024 * 1024
anywhere = pl.BlockSpec(memory_space=pl.ANY)


def unit_of(tick, section, sections):
    group = (tick - section) % sections
    return group, tick - group


def start_when(condition, copy):
    pl.when(condition)(lambda: copy.start())


def wait_when(condition, copy):
    pl.when(condition)(lambda: copy.wait())


def tick_kernel(plan, info, columns, picks, *refs):
    tick, sections, parts, groups, depth, layers, history, moved_keys, sends, is_last = plan
    initial_ref, tiles_ref, stale_ref, weights_ref = refs[:4]
    refs = list(refs[4:])
    arrived = [[refs.pop(0) for _ in range(parts)] for _ in range(history)]
    moved = {key: (refs.pop(0), refs.pop(0)) for key in moved_keys}
    out_refs = [refs.pop(0) for _ in range(parts)] if sends else []
    final_refs = [refs.pop(0) for _ in range(sections)] if is_last else []
    table, tiles, stored_weight, initial, made, table_sem, tile_sem, other_sem, out_sem = refs
    fanout, block = tiles_ref.shape[1:3]
    blocks_dev = tiles_ref.shape[0]
    group_blocks = blocks_dev // groups
    width = initial_ref.shape[1]

    section, part = info[0], info[1]
    group = lax.rem(tick - section + 4 * sections, sections)
    layer = tick - group
    first_row = group * group_blocks
    computing = (group < groups) & (layer >= 0) & (layer < layers)
    passing = (group < groups) & (layer == -1)
    home = lax.div(jnp.maximum(layer, 0), depth)
    sub = lax.rem(jnp.maximum(layer, 0), depth)
    turn = lax.div(jnp.maximum(layer, 0), sections)

    first_initial = pl.multiple_of(first_row * block, block)
    initial_copy = pltpu.make_async_copy(
        initial_ref.at[pl.ds(first_initial, group_blocks * block)], initial, other_sem.at[0]
    )

    if history > 0:
        copies = []
        for back in range(history):
            known = computing & (group >= back)
            source_group = jnp.maximum(group - back, 0)
            sem = lambda index: table_sem.at[back * parts + index]
            copies.append(
                (
                    known,
                    pltpu.make_async_copy(
                        arrived[back][0],
                        table.at[pl.ds(source_group * group_blocks, group_blocks)],
                        sem(0),
                    ),
                )
            )
            for distance in range(1, parts):
                origin = lax.rem(part - distance + parts, parts)
                copies.append(
                    (
                        known,
                        pltpu.make_async_copy(
                            arrived[back][distance],
                            table.at[blocks_dev + source_group * parts + origin],
                            sem(distance),
                        ),
                    )
                )
        here = section == home
        sources = [(here, stale_ref.at[sub, 0], weights_ref.at[sub])]
        for (moved_turn, moved_sub), (moved_stale, moved_weight) in moved.items():
            chosen = jnp.logical_not(here) & (turn == moved_turn) & (sub == moved_sub)
            sources.append((chosen, moved_stale, moved_weight))
        for chosen, stale_source, weight_source in sources:
            for later in range(1, groups):
                copies.append(
                    (
                        computing & chosen & (group < later),
                        pltpu.make_async_copy(
                            stale_source.at[(later - 1) * parts : later * parts],
                            table.at[pl.ds(blocks_dev + later * parts, parts)],
                            other_sem.at[1 + later],
                        ),
                    )
                )
            copies.append(
                (
                    computing & chosen,
                    pltpu.make_async_copy(weight_source, stored_weight, other_sem.at[1]),
                )
            )

        def tile_copy(row):
            return pltpu.make_async_copy(
                tiles_ref.at[first_row + row], tiles.at[row], tile_sem.at[row]
            )

        for condition, copy in copies:
            start_when(condition, copy)

        @pl.when(computing)
        def _():
            for row in range(group_blocks):
                tile_copy(row).start()
            initial_copy.start()

        for condition, copy in copies:
            wait_when(condition, copy)

        @pl.when(computing)
        def _():
            initial_copy.wait()
            beta_layer = jnp.float32(0.0)
            for known_layer in range(max(tick - groups + 1, 0), min(tick, layers - 1) + 1):
                beta_layer = jnp.where(
                    layer == known_layer,
                    jnp.float32(math.log(lambda_decay / (known_layer + 1) + 1.0)),
                    beta_layer,
                )
            mixed_rows = []
            for row in range(group_blocks):
                tile_copy(row).wait()
                base = (first_row + row) * fanout
                left = jnp.concatenate([tiles[row, t] for t in range(fanout)], 1)
                right = jnp.concatenate([table[columns[base + t]] for t in range(fanout)], 0)
                total = jnp.dot(left, right, preferred_element_type=jnp.float32)
                start = initial[row * block : (row + 1) * block].astype(jnp.float32)
                mixed = ((1.0 - alpha_mix) * total + alpha_mix * start).astype(jnp.bfloat16)
                product = jnp.dot(mixed, stored_weight[...], preferred_element_type=jnp.float32)
                value = (1.0 - beta_layer) * mixed.astype(jnp.float32) + beta_layer * product
                made[row] = jnp.maximum(value, 0.0).astype(jnp.bfloat16)

    if tick < groups - 1:

        @pl.when(passing)
        def _():
            initial_copy.start()
            initial_copy.wait()
            for row in range(group_blocks):
                made[row] = initial[row * block : (row + 1) * block]

    if sends:
        sending = passing | (computing & (layer < layers - 1))

        @pl.when(sending)
        def _():
            out_copies = [pltpu.make_async_copy(made, out_refs[0], out_sem.at[0])]
            for distance in range(1, parts):
                dest = lax.rem(part + distance, parts)
                chosen = jnp.maximum(picks[group * parts + dest], 0)
                out_copies.append(
                    pltpu.make_async_copy(
                        made.at[chosen], out_refs[distance], out_sem.at[distance]
                    )
                )
            for copy in out_copies:
                copy.start()
            for copy in out_copies:
                copy.wait()

    if is_last:

        @pl.when(computing & (layer == layers - 1))
        def _():
            piece = width // sections
            for index, final_ref in enumerate(final_refs):
                for row in range(group_blocks):
                    final_ref[row * block : (row + 1) * block, :] = made[row][
                        :, index * piece : (index + 1) * piece
                    ]


def run_tick(tick, scalars, arrays, arrived, moved, sizes):
    sections, parts, groups, depth, layers = sizes
    initial_features, tiles = arrays[:2]
    width = initial_features.shape[1]
    blocks_dev, fanout, block = tiles.shape[:3]
    group_blocks = blocks_dev // groups
    sends = tick < layers + groups - 2
    is_last = tick >= layers - 1
    units = [unit_of(tick, s, sections) for s in range(sections)]
    units = [(g, l) for g, l in units if g < groups and 0 <= l < layers]
    moved_keys = sorted(
        {(l // sections, l % depth) for g, l in units if l // depth != l % sections}
    )
    plan = (
        tick, sections, parts, groups, depth, layers, len(arrived), moved_keys, sends, is_last,
    )
    operands = list(arrays)
    for back in arrived:
        operands += back
    for key in moved_keys:
        operands += list(moved[key])
    out_shape, out_specs = [], []
    if sends:
        shapes = [(group_blocks, block, width)] + [(block, width)] * (parts - 1)
        out_shape += [jax.ShapeDtypeStruct(s, jnp.bfloat16) for s in shapes]
        out_specs += [anywhere] * parts
    if is_last:
        shape = (group_blocks * block, width // sections)
        out_shape += [jax.ShapeDtypeStruct(shape, jnp.bfloat16)] * sections
        out_specs += [pl.BlockSpec(shape, lambda i, *prefetched: (0, 0))] * sections
    work = group_blocks if units else 0
    results = pl.pallas_call(
        functools.partial(tick_kernel, plan),
        grid_spec=pltpu.PrefetchScalarGridSpec(
            num_scalar_prefetch=3,
            grid=(1,),
            in_specs=[anywhere] * len(operands),
            out_specs=out_specs,
            scratch_shapes=[
                pltpu.VMEM((blocks_dev + groups * parts, block, width), jnp.bfloat16),
                pltpu.VMEM((group_blocks, fanout, block, block), jnp.bfloat16),
                pltpu.VMEM((width, width), jnp.bfloat16),
                pltpu.VMEM((group_blocks * block, width), jnp.bfloat16),
                pltpu.VMEM((group_blocks, block, width), jnp.bfloat16),
                pltpu.SemaphoreType.DMA((groups * parts,)),
                pltpu.SemaphoreType.DMA((group_blocks,)),
                pltpu.SemaphoreType.DMA((groups + 1,)),
                pltpu.SemaphoreType.DMA((parts,)),
            ],
        ),
        out_shape=out_shape,
        cost_estimate=pl.CostEstimate(
            flops=2 * work * block * width * (fanout * block + width) + 1,
            bytes_accessed=work * fanout * block * (block + width) * 2 + 1,
            transcendentals=0,
        ),
        compiler_params=pltpu.CompilerParams(vmem_limit_bytes=vmem_bytes),
        name="tick",
    )(*scalars, *operands)
    return (results[:parts] if sends else []), (results[-sections:] if is_last else [])


def per_device(
    initial_features, layer_weights, adjacency_tiles, tile_columns, send_blocks, stale_imports
):
    sections = lax.axis_size("section")
    parts = lax.axis_size("dom")
    groups = send_blocks.shape[1]
    depth = layer_weights.shape[0]
    layers = depth * sections
    section = lax.axis_index("section").astype(jnp.int32)
    part = lax.axis_index("dom").astype(jnp.int32)
    scalars = (jnp.stack([section, part]), tile_columns.reshape(-1), send_blocks.reshape(-1))
    arrays = (initial_features, adjacency_tiles, stale_imports, layer_weights)
    sizes = (sections, parts, groups, depth, layers)

    def move(value, pairs, distance):
        routes = [
            (a * parts + q, b * parts + (q + distance) % parts) for a, b in pairs for q in range(parts)
        ]
        idle_from = [s for s in range(sections) if s not in [a for a, b in pairs]]
        idle_to = [s for s in range(sections) if s not in [b for a, b in pairs]]
        both = [s for s in idle_from if s in idle_to]
        fill = [(s, s) for s in both] + list(
            zip([s for s in idle_from if s not in both], [s for s in idle_to if s not in both])
        )
        routes += [(a * parts + q, b * parts + q) for a, b in fill for q in range(parts)]
        return lax.ppermute(value, ("section", "dom"), routes)

    routes = {}
    for layer in range(layers):
        if layer // depth != layer % sections:
            key = (layer // sections, layer % depth)
            routes.setdefault(key, []).append((layer // depth, layer % sections))
    moved = {
        key: (move(stale_imports[key[1], 0], pairs, 0), move(layer_weights[key[1]], pairs, 0))
        for key, pairs in sorted(routes.items())
    }

    arrived = []
    pieces = []
    for tick in range(-1, layers + groups - 1):
        outgoing, final = run_tick(tick, scalars, arrays, arrived, moved, sizes)
        senders = []
        for s in range(sections):
            group, layer = unit_of(tick, s, sections)
            if group < groups and -1 <= layer < layers - 1:
                senders.append((s, (s + 1) % sections))
        if outgoing:
            received = [move(value, senders, distance) for distance, value in enumerate(outgoing)]
            arrived = [received] + arrived[: groups - 1]
        if final:
            last = (layers - 1) % sections
            piece = final[last]
            for s in range(sections):
                if s != last:
                    piece = jnp.where(section == s, move(final[s], [(last, s)], 0), piece)
            pieces.append(piece)
    return jnp.concatenate(pieces, 0)


def solution(mesh):
    return jax.shard_map(
        per_device,
        mesh=mesh,
        in_specs=(
            P("dom", None),
            P("section", None, None),
            P("dom", None, None, None),
            P("dom", None),
            P("dom", None, None),
            P("section", "dom", None, None, None),
        ),
        out_specs=P("dom", "section"),
        check_vma=False,
    )
```

```python
import functools
import math

import jax
import jax.numpy as jnp
from jax import lax
from jax.experimental import pallas as pl
from jax.experimental.pallas import tpu as pltpu
from jax.sharding import PartitionSpec as P

alpha_mix = 0.1
lambda_decay = 0.5
vmem_bytes = 20 * 1024 * 1024


def group_streams(groups):
    return [list(range(groups - 1)), [groups - 1]]


def params():
    return pltpu.CompilerParams(vmem_limit_bytes=vmem_bytes)


def whole(shape):
    return pl.BlockSpec(shape, lambda i, *prefetched: (0,) * len(shape))


def pick_outgoing(picks, blocks_ref, outgoing_ref, stream, group_blocks, part_count):
    for local, group in enumerate(stream):

        def pick(dest, carry):
            chosen = jnp.maximum(picks[group * part_count + dest], 0)
            outgoing_ref[dest, local] = blocks_ref[local * group_blocks + chosen]
            return carry

        lax.fori_loop(0, part_count, pick, 0)


def prologue_kernel(streams, group_blocks, part_count, info, picks, rows_ref, *refs):
    own_refs = refs[: len(streams)]
    outgoing_refs = refs[len(streams) : 2 * len(streams)]
    turned = refs[-1]
    block = own_refs[0].shape[2]
    part_width = own_refs[0].shape[1]
    first = pl.multiple_of(info[0] * part_width, part_width)
    for stream, own_ref, outgoing_ref in zip(streams, own_refs, outgoing_refs):
        for local in range(len(stream) * group_blocks):
            row = (stream[0] * group_blocks + local) * block
            turned[local % 2] = rows_ref[row : row + block, :].T
            own_ref[local] = turned[local % 2, pl.ds(first, part_width), :]
        pick_outgoing(picks, own_ref, outgoing_ref, stream, group_blocks, part_count)


def prologue(initial_features, section, picks, streams, group_blocks, block, part_width, part_count):
    rows, width = initial_features.shape
    own_shapes = [(len(s) * group_blocks, part_width, block) for s in streams]
    out_shapes = [(part_count, len(s), part_width, block) for s in streams]
    return pl.pallas_call(
        functools.partial(prologue_kernel, streams, group_blocks, part_count),
        grid_spec=pltpu.PrefetchScalarGridSpec(
            num_scalar_prefetch=2,
            grid=(1,),
            in_specs=[whole((rows, width))],
            out_specs=[whole(s) for s in own_shapes + out_shapes],
            scratch_shapes=[pltpu.VMEM((2, width, block), jnp.bfloat16)],
        ),
        out_shape=[jax.ShapeDtypeStruct(s, jnp.bfloat16) for s in own_shapes + out_shapes],
        compiler_params=params(),
        name="prologue",
    )(section, picks, initial_features)


def turn_kernel(in_ref, out_ref):
    count = in_ref.shape[0]
    parts, part_width = out_ref.shape[0], out_ref.shape[2]
    for item in range(count):
        turned = in_ref[item].T
        for part in range(parts):
            out_ref[part, item] = turned[part * part_width : (part + 1) * part_width, :]


def turn_blocks(blocks, parts):
    count, block, width = blocks.shape
    step = 4 if count % 4 == 0 else 1
    part_width = width // parts
    return pl.pallas_call(
        turn_kernel,
        grid=(count // step,),
        in_specs=[pl.BlockSpec((step, block, width), lambda i: (i, 0, 0))],
        out_specs=pl.BlockSpec((parts, step, part_width, block), lambda i: (0, i, 0, 0)),
        out_shape=jax.ShapeDtypeStruct((parts, count, part_width, block), jnp.bfloat16),
        compiler_params=params(),
        name="turn",
    )(blocks)


def aggregate_kernel(plan, columns, initial_ref, tiles_ref, *refs):
    stream, group_blocks, fanout, sources, layer_slot = plan
    source_refs = refs[: len(sources)]
    mixed_ref, table, tiles, table_sem, tiles_sem = refs[len(sources) :]
    rows = len(stream) * group_blocks
    first_row = stream[0] * group_blocks

    def tile_copy(row):
        return pltpu.make_async_copy(tiles_ref.at[first_row + row], tiles.at[row], tiles_sem.at[row])

    copies = []
    for index, (kind, target, detail) in enumerate(sources):
        ref = source_refs[index]
        if kind == "own":
            source = ref
        elif kind == "import":
            source = ref.at[:, detail]
        else:
            source = ref.at[layer_slot]
        count = source.shape[0]
        copies.append(
            pltpu.make_async_copy(source, table.at[pl.ds(target, count)], table_sem.at[index])
        )
    for copy in copies:
        copy.start()
    for row in range(rows):
        tile_copy(row).start()
    for copy in copies:
        copy.wait()

    def one_row(row, carry):
        tile_copy(row).wait()
        base = (first_row + row) * fanout
        total = None
        for tile in range(0, fanout, 2):
            span = range(tile, min(tile + 2, fanout))
            left = jnp.concatenate([table[columns[base + t]] for t in span], 1)
            right = jnp.concatenate([tiles[row, t] for t in span], 1)
            term = lax.dot_general(
                left, right, (((1,), (1,)), ((), ())), preferred_element_type=jnp.float32
            )
            total = term if total is None else total + term
        mixed_ref[row] = (
            (1.0 - alpha_mix) * total + alpha_mix * initial_ref[row].astype(jnp.float32)
        ).astype(jnp.bfloat16)
        return carry

    lax.fori_loop(0, rows, one_row, 0)


def aggregate(columns, initial_blocks, tiles, own, imports, stale, layer_slot, stream, streams, group_blocks, part_count):
    rows, part_width, block = initial_blocks.shape
    blocks_dev, fanout = tiles.shape[:2]
    groups = blocks_dev // group_blocks
    sources, operands = [], []
    for other, own_blocks, imported in zip(streams, own, imports):
        if other[0] > stream[-1]:
            continue
        sources.append(("own", other[0] * group_blocks, None))
        operands.append(own_blocks)
        for local, group in enumerate(other):
            sources.append(("import", blocks_dev + group * part_count, local))
            operands.append(imported)
    if groups > 1 and stream[0] < groups - 1:
        sources.append(("stale", blocks_dev + groups * part_count, None))
        operands.append(stale)
    table_size = blocks_dev + (2 * groups - 1) * part_count
    plan = (stream, group_blocks, fanout, sources, layer_slot)
    flops = 2 * rows * fanout * block * block * part_width
    return pl.pallas_call(
        functools.partial(aggregate_kernel, plan),
        grid_spec=pltpu.PrefetchScalarGridSpec(
            num_scalar_prefetch=1,
            grid=(1,),
            in_specs=[whole(initial_blocks.shape)]
            + [pl.BlockSpec(memory_space=pl.ANY)] * (1 + len(operands)),
            out_specs=whole((rows, part_width, block)),
            scratch_shapes=[
                pltpu.VMEM((table_size, part_width, block), jnp.bfloat16),
                pltpu.VMEM((rows, fanout, block, block), jnp.bfloat16),
                pltpu.SemaphoreType.DMA((len(sources),)),
                pltpu.SemaphoreType.DMA((rows,)),
            ],
        ),
        out_shape=jax.ShapeDtypeStruct((rows, part_width, block), jnp.bfloat16),
        cost_estimate=pl.CostEstimate(
            flops=flops, bytes_accessed=rows * fanout * block * block * 2, transcendentals=0
        ),
        compiler_params=params(),
        name="aggregate",
    )(columns, initial_blocks, tiles, *operands)


def finish_kernel(plan, picks, mixed_ref, gathered_ref, weight_ref, *refs):
    beta_layer, stream, group_blocks, part_count, last = plan
    *refs, held, held_sem = refs
    rows, part_width, block = mixed_ref.shape
    parts = gathered_ref.shape[0]
    spans = [(row, min(row + 2, rows)) for row in range(0, rows, 2)]
    copies = [
        pltpu.make_async_copy(
            gathered_ref.at[:, low:high], held.at[:, low:high], held_sem.at[index]
        )
        for index, (low, high) in enumerate(spans)
    ]
    for copy in copies:
        copy.start()
    weight = weight_ref[0]
    for copy, (low, high) in zip(copies, spans):
        copy.wait()
        span = range(low, high)
        right = jnp.concatenate(
            [jnp.concatenate([held[p, r] for p in range(parts)], 0) for r in span], 1
        )
        product = jnp.dot(weight, right, preferred_element_type=jnp.float32)
        for place, r in enumerate(span):
            value = (1.0 - beta_layer) * mixed_ref[r].astype(jnp.float32) + beta_layer * product[
                :, place * block : (place + 1) * block
            ]
            value = jnp.maximum(value, 0.0).astype(jnp.bfloat16)
            if last:
                refs[0][r * block : (r + 1) * block, :] = value.T
            else:
                refs[0][r] = value
    if not last:
        pick_outgoing(picks, refs[0], refs[1], stream, group_blocks, part_count)


def finish(picks, mixed, gathered, weights, layer, stream, group_blocks, part_count, last):
    rows, part_width, block = mixed.shape
    width = weights.shape[2]
    beta_layer = math.log(lambda_decay / (layer + 1) + 1.0)
    plan = (beta_layer, stream, group_blocks, part_count, last)
    if last:
        shapes = [(rows * block, part_width)]
    else:
        shapes = [(rows, part_width, block), (part_count, len(stream), part_width, block)]
    return pl.pallas_call(
        functools.partial(finish_kernel, plan),
        grid_spec=pltpu.PrefetchScalarGridSpec(
            num_scalar_prefetch=1,
            grid=(1,),
            in_specs=[
                whole(mixed.shape),
                pl.BlockSpec(memory_space=pl.ANY),
                pl.BlockSpec((1, part_width, width), lambda i, *prefetched: (layer, 0, 0)),
            ],
            out_specs=[whole(s) for s in shapes],
            scratch_shapes=[
                pltpu.VMEM(gathered.shape, jnp.bfloat16),
                pltpu.SemaphoreType.DMA(((rows + 1) // 2,)),
            ],
        ),
        out_shape=[jax.ShapeDtypeStruct(s, jnp.bfloat16) for s in shapes],
        cost_estimate=pl.CostEstimate(
            flops=2 * rows * block * width * part_width,
            bytes_accessed=rows * block * width * 2,
            transcendentals=0,
        ),
        compiler_params=params(),
        name="finish",
    )(picks, mixed, gathered, weights)


def per_device(
    initial_features, layer_weights, adjacency_tiles, tile_columns, send_blocks, stale_imports
):
    section_count = lax.axis_size("section")
    part_count = lax.axis_size("dom")
    blocks_dev, fanout, block = adjacency_tiles.shape[:3]
    width = initial_features.shape[1]
    part_width = width // section_count
    groups = send_blocks.shape[1]
    group_blocks = blocks_dev // groups
    depth = layer_weights.shape[0]
    layers = depth * section_count
    streams = group_streams(groups)
    section = lax.axis_index("section").astype(jnp.int32).reshape(1)
    picks = send_blocks.reshape(-1)

    row_group = (jnp.arange(blocks_dev, dtype=jnp.int32) // group_blocks)[:, None]
    slot_group = (tile_columns - blocks_dev) // part_count
    is_stale = (tile_columns >= blocks_dev) & (slot_group > row_group)
    columns = jnp.where(
        is_stale, tile_columns + (groups - 1) * part_count, tile_columns
    ).reshape(-1)

    started = prologue(
        initial_features, section, picks, streams, group_blocks, block, part_width, part_count
    )
    own = started[: len(streams)]
    outgoing = started[len(streams) :]
    initial_blocks = own

    def exchange(value):
        return lax.all_to_all(value, "dom", split_axis=0, concat_axis=0, tiled=True)

    imports = [exchange(value) for value in outgoing]
    stale = [
        lax.all_to_all(
            turn_blocks(stale_imports[sub, 0], section_count),
            "section",
            split_axis=0,
            concat_axis=0,
            tiled=True,
        )
        for sub in range(depth)
    ]
    weights = lax.all_to_all(
        layer_weights.transpose(0, 2, 1).reshape(depth, section_count, part_width, width),
        "section",
        split_axis=1,
        concat_axis=0,
        tiled=True,
    ).reshape(layers, part_width, width)

    pieces = []
    for layer in range(layers):
        last = layer == layers - 1
        own_next, imports_next = [], []
        for index, stream in enumerate(streams):
            mixed = aggregate(
                columns,
                initial_blocks[index],
                adjacency_tiles,
                own,
                imports,
                stale[layer % depth],
                layer // depth,
                stream,
                streams,
                group_blocks,
                part_count,
            )
            gathered = lax.all_gather(mixed, "section", axis=0, tiled=False)
            result = finish(
                picks, mixed, gathered, weights, layer, stream, group_blocks, part_count, last
            )
            if last:
                pieces.append(result[0])
            else:
                own_next.append(result[0])
                imports_next.append(exchange(result[1]))
        own, imports = own_next, imports_next
    return jnp.concatenate(pieces, 0) if len(pieces) > 1 else pieces[0]


def solution(mesh):
    return jax.shard_map(
        per_device,
        mesh=mesh,
        in_specs=(
            P("dom", None),
            P("section", None, None),
            P("dom", None, None, None),
            P("dom", None),
            P("dom", None, None),
            P("section", "dom", None, None, None),
        ),
        out_specs=P("dom", "section"),
        check_vma=False,
    )
```

```python
import functools
import math

import jax
import jax.numpy as jnp
from jax import lax
from jax.experimental import pallas as pl
from jax.experimental.pallas import tpu as pltpu
from jax.sharding import PartitionSpec as P

alpha_mix = 0.1
lambda_decay = 0.5
vmem_bytes = 48 * 1024 * 1024


def group_streams(groups):
    return [list(range(groups - 1)), [groups - 1]]


def params():
    return pltpu.CompilerParams(vmem_limit_bytes=vmem_bytes)


def whole(shape):
    return pl.BlockSpec(shape, lambda i, *prefetched: (0,) * len(shape))


def pick_outgoing(picks, blocks_ref, outgoing_ref, stream, group_blocks, part_count):
    for local, group in enumerate(stream):

        def pick(dest, carry):
            chosen = jnp.maximum(picks[group * part_count + dest], 0)
            outgoing_ref[dest, local] = blocks_ref[local * group_blocks + chosen]
            return carry

        lax.fori_loop(0, part_count, pick, 0)


def prologue_kernel(streams, group_blocks, part_count, info, picks, rows_ref, *refs):
    own_refs = refs[: len(streams)]
    outgoing_refs = refs[len(streams) : 2 * len(streams)]
    turned = refs[-1]
    block = own_refs[0].shape[2]
    part_width = own_refs[0].shape[1]
    first = pl.multiple_of(info[0] * part_width, part_width)
    for stream, own_ref, outgoing_ref in zip(streams, own_refs, outgoing_refs):
        for local in range(len(stream) * group_blocks):
            row = (stream[0] * group_blocks + local) * block
            turned[local % 2] = rows_ref[row : row + block, :].T
            own_ref[local] = turned[local % 2, pl.ds(first, part_width), :]
        pick_outgoing(picks, own_ref, outgoing_ref, stream, group_blocks, part_count)


def prologue(initial_features, section, picks, streams, group_blocks, block, part_width, part_count):
    rows, width = initial_features.shape
    own_shapes = [(len(s) * group_blocks, part_width, block) for s in streams]
    out_shapes = [(part_count, len(s), part_width, block) for s in streams]
    return pl.pallas_call(
        functools.partial(prologue_kernel, streams, group_blocks, part_count),
        grid_spec=pltpu.PrefetchScalarGridSpec(
            num_scalar_prefetch=2,
            grid=(1,),
            in_specs=[whole((rows, width))],
            out_specs=[whole(s) for s in own_shapes + out_shapes],
            scratch_shapes=[pltpu.VMEM((2, width, block), jnp.bfloat16)],
        ),
        out_shape=[jax.ShapeDtypeStruct(s, jnp.bfloat16) for s in own_shapes + out_shapes],
        compiler_params=params(),
        name="prologue",
    )(section, picks, initial_features)


def turn_kernel(in_ref, out_ref):
    count = in_ref.shape[0]
    parts, part_width = out_ref.shape[0], out_ref.shape[2]
    for item in range(count):
        turned = in_ref[item].T
        for part in range(parts):
            out_ref[part, item] = turned[part * part_width : (part + 1) * part_width, :]


def turn_blocks(blocks, parts):
    count, block, width = blocks.shape
    step = 4 if count % 4 == 0 else 1
    part_width = width // parts
    return pl.pallas_call(
        turn_kernel,
        grid=(count // step,),
        in_specs=[pl.BlockSpec((step, block, width), lambda i: (i, 0, 0))],
        out_specs=pl.BlockSpec((parts, step, part_width, block), lambda i: (0, i, 0, 0)),
        out_shape=jax.ShapeDtypeStruct((parts, count, part_width, block), jnp.bfloat16),
        compiler_params=params(),
        name="turn",
    )(blocks)


def aggregate_kernel(plan, columns, initial_ref, tiles_ref, *refs):
    stream, group_blocks, fanout, sources, layer_slot = plan
    source_refs = refs[: len(sources)]
    mixed_ref, table, tiles, table_sem, tiles_sem = refs[-5:]
    rows = len(stream) * group_blocks
    first_row = stream[0] * group_blocks

    def tile_copy(row):
        return pltpu.make_async_copy(tiles_ref.at[first_row + row], tiles.at[row], tiles_sem.at[row])

    copies = []
    for index, (kind, target, detail) in enumerate(sources):
        ref = source_refs[index]
        if kind == "own":
            source = ref
        elif kind == "import":
            source = ref.at[:, detail]
        else:
            source = ref.at[layer_slot]
        count = source.shape[0]
        copies.append(
            pltpu.make_async_copy(source, table.at[pl.ds(target, count)], table_sem.at[index])
        )
    for copy in copies:
        copy.start()
    for row in range(rows):
        tile_copy(row).start()
    for copy in copies:
        copy.wait()

    def one_row(row, carry):
        tile_copy(row).wait()
        base = (first_row + row) * fanout
        total = None
        for tile in range(0, fanout, 2):
            span = range(tile, min(tile + 2, fanout))
            left = jnp.concatenate([table[columns[base + t]] for t in span], 1)
            right = jnp.concatenate([tiles[row, t] for t in span], 1)
            term = lax.dot_general(
                left, right, (((1,), (1,)), ((), ())), preferred_element_type=jnp.float32
            )
            total = term if total is None else total + term
        mixed_ref[row] = (
            (1.0 - alpha_mix) * total + alpha_mix * initial_ref[row].astype(jnp.float32)
        ).astype(jnp.bfloat16)
        return carry

    lax.fori_loop(0, rows, one_row, 0)


def aggregate(columns, initial_blocks, tiles, own, imports, stale, layer_slot, stream, streams, group_blocks, part_count, after):
    rows, part_width, block = initial_blocks.shape
    blocks_dev, fanout = tiles.shape[:2]
    groups = blocks_dev // group_blocks
    sources, operands = [], []
    for other, own_blocks, imported in zip(streams, own, imports):
        if other[0] > stream[-1]:
            continue
        sources.append(("own", other[0] * group_blocks, None))
        operands.append(own_blocks)
        for local, group in enumerate(other):
            sources.append(("import", blocks_dev + group * part_count, local))
            operands.append(imported)
    if groups > 1 and stream[0] < groups - 1:
        sources.append(("stale", blocks_dev + groups * part_count, None))
        operands.append(stale)
    operands += after
    table_size = blocks_dev + (2 * groups - 1) * part_count
    plan = (stream, group_blocks, fanout, sources, layer_slot)
    flops = 2 * rows * fanout * block * block * part_width
    return pl.pallas_call(
        functools.partial(aggregate_kernel, plan),
        grid_spec=pltpu.PrefetchScalarGridSpec(
            num_scalar_prefetch=1,
            grid=(1,),
            in_specs=[whole(initial_blocks.shape)]
            + [pl.BlockSpec(memory_space=pl.ANY)] * (1 + len(operands)),
            out_specs=whole((rows, part_width, block)),
            scratch_shapes=[
                pltpu.VMEM((table_size, part_width, block), jnp.bfloat16),
                pltpu.VMEM((rows, fanout, block, block), jnp.bfloat16),
                pltpu.SemaphoreType.DMA((len(sources),)),
                pltpu.SemaphoreType.DMA((rows,)),
            ],
        ),
        out_shape=jax.ShapeDtypeStruct((rows, part_width, block), jnp.bfloat16),
        cost_estimate=pl.CostEstimate(
            flops=flops, bytes_accessed=rows * fanout * block * block * 2, transcendentals=0
        ),
        compiler_params=params(),
        name="aggregate",
    )(columns, initial_blocks, tiles, *operands)


def finish_kernel(plan, picks, mixed_ref, gathered_ref, weight_ref, *refs):
    beta_layer, stream, group_blocks, part_count, last = plan
    *refs, held, held_sem = refs
    rows, part_width, block = mixed_ref.shape
    parts = gathered_ref.shape[0]
    spans = [(row, min(row + 2, rows)) for row in range(0, rows, 2)]
    copies = [
        pltpu.make_async_copy(
            gathered_ref.at[:, low:high], held.at[:, low:high], held_sem.at[index]
        )
        for index, (low, high) in enumerate(spans)
    ]
    for copy in copies:
        copy.start()
    weight = weight_ref[0]
    for copy, (low, high) in zip(copies, spans):
        copy.wait()
        span = range(low, high)
        right = jnp.concatenate(
            [jnp.concatenate([held[p, r] for p in range(parts)], 0) for r in span], 1
        )
        product = jnp.dot(weight, right, preferred_element_type=jnp.float32)
        for place, r in enumerate(span):
            value = (1.0 - beta_layer) * mixed_ref[r].astype(jnp.float32) + beta_layer * product[
                :, place * block : (place + 1) * block
            ]
            value = jnp.maximum(value, 0.0).astype(jnp.bfloat16)
            if last:
                refs[0][r * block : (r + 1) * block, :] = value.T
            else:
                refs[0][r] = value
    if not last:
        pick_outgoing(picks, refs[0], refs[1], stream, group_blocks, part_count)


def finish(picks, mixed, gathered, weights, layer, stream, group_blocks, part_count, last):
    rows, part_width, block = mixed.shape
    width = weights.shape[2]
    beta_layer = math.log(lambda_decay / (layer + 1) + 1.0)
    plan = (beta_layer, stream, group_blocks, part_count, last)
    if last:
        shapes = [(rows * block, part_width)]
    else:
        shapes = [(rows, part_width, block), (part_count, len(stream), part_width, block)]
    return pl.pallas_call(
        functools.partial(finish_kernel, plan),
        grid_spec=pltpu.PrefetchScalarGridSpec(
            num_scalar_prefetch=1,
            grid=(1,),
            in_specs=[
                whole(mixed.shape),
                pl.BlockSpec(memory_space=pl.ANY),
                pl.BlockSpec((1, part_width, width), lambda i, *prefetched: (layer, 0, 0)),
            ],
            out_specs=[whole(s) for s in shapes],
            scratch_shapes=[
                pltpu.VMEM(gathered.shape, jnp.bfloat16),
                pltpu.SemaphoreType.DMA(((rows + 1) // 2,)),
            ],
        ),
        out_shape=[jax.ShapeDtypeStruct(s, jnp.bfloat16) for s in shapes],
        cost_estimate=pl.CostEstimate(
            flops=2 * rows * block * width * part_width,
            bytes_accessed=rows * block * width * 2,
            transcendentals=0,
        ),
        compiler_params=params(),
        name="finish",
    )(picks, mixed, gathered, weights)


def per_device(
    initial_features, layer_weights, adjacency_tiles, tile_columns, send_blocks, stale_imports
):
    section_count = lax.axis_size("section")
    part_count = lax.axis_size("dom")
    blocks_dev, fanout, block = adjacency_tiles.shape[:3]
    width = initial_features.shape[1]
    part_width = width // section_count
    groups = send_blocks.shape[1]
    group_blocks = blocks_dev // groups
    depth = layer_weights.shape[0]
    layers = depth * section_count
    streams = group_streams(groups)
    section = lax.axis_index("section").astype(jnp.int32).reshape(1)
    picks = send_blocks.reshape(-1)

    row_group = (jnp.arange(blocks_dev, dtype=jnp.int32) // group_blocks)[:, None]
    slot_group = (tile_columns - blocks_dev) // part_count
    is_stale = (tile_columns >= blocks_dev) & (slot_group > row_group)
    columns = jnp.where(
        is_stale, tile_columns + (groups - 1) * part_count, tile_columns
    ).reshape(-1)

    started = prologue(
        initial_features, section, picks, streams, group_blocks, block, part_width, part_count
    )
    own = started[: len(streams)]
    outgoing = started[len(streams) :]
    initial_blocks = own

    def exchange(value):
        return lax.all_to_all(value, "dom", split_axis=0, concat_axis=0, tiled=True)

    imports = [exchange(value) for value in outgoing]
    stale = [
        lax.all_to_all(
            turn_blocks(stale_imports[sub, 0], section_count),
            "section",
            split_axis=0,
            concat_axis=0,
            tiled=True,
        )
        for sub in range(depth)
    ]
    weights = lax.all_to_all(
        layer_weights.transpose(0, 2, 1).reshape(depth, section_count, part_width, width),
        "section",
        split_axis=1,
        concat_axis=0,
        tiled=True,
    ).reshape(layers, part_width, width)

    pieces = []
    after = []
    for layer in range(layers):
        last = layer == layers - 1
        own_next, imports_next = [], []
        for index, stream in enumerate(streams):
            mixed = aggregate(
                columns,
                initial_blocks[index],
                adjacency_tiles,
                own,
                imports,
                stale[layer % depth],
                layer // depth,
                stream,
                streams,
                group_blocks,
                part_count,
                after,
            )
            gathered = lax.all_gather(mixed, "section", axis=0, tiled=False)
            result = finish(
                picks, mixed, gathered, weights, layer, stream, group_blocks, part_count, last
            )
            if last:
                pieces.append(result[0])
            else:
                after = [result[1]]
                own_next.append(result[0])
                imports_next.append(exchange(result[1]))
        own, imports = own_next, imports_next
    return jnp.concatenate(pieces, 0) if len(pieces) > 1 else pieces[0]


def solution(mesh):
    return jax.shard_map(
        per_device,
        mesh=mesh,
        in_specs=(
            P("dom", None),
            P("section", None, None),
            P("dom", None, None, None),
            P("dom", None),
            P("dom", None, None),
            P("section", "dom", None, None, None),
        ),
        out_specs=P("dom", "section"),
        check_vma=False,
    )
```

```python
import functools
import math

import jax
import jax.numpy as jnp
from jax import lax
from jax.experimental import pallas as pl
from jax.experimental.pallas import tpu as pltpu
from jax.sharding import PartitionSpec as P

alpha_mix = 0.1
lambda_decay = 0.5
vmem_bytes = 48 * 1024 * 1024


def group_streams(groups):
    return [list(range(groups - 1)), [groups - 1]]


def params():
    return pltpu.CompilerParams(vmem_limit_bytes=vmem_bytes)


def in_hbm(shape):
    return pltpu.HBM(shape, jnp.bfloat16)


def start_all(copies):
    for condition, copy in copies:
        if condition is None:
            copy.start()
        else:
            pl.when(condition)(copy.start)


def wait_all(copies):
    for condition, copy in copies:
        if condition is None:
            copy.wait()
        else:
            pl.when(condition)(copy.wait)


def whole(shape):
    return pl.BlockSpec(shape, lambda i, *prefetched: (0,) * len(shape))


def pick_outgoing(picks, blocks_ref, outgoing_ref, stream, group_blocks, part_count):
    for local, group in enumerate(stream):

        def pick(dest, carry):
            chosen = jnp.maximum(picks[group * part_count + dest], 0)
            outgoing_ref[dest, local] = blocks_ref[local * group_blocks + chosen]
            return carry

        lax.fori_loop(0, part_count, pick, 0)


def prologue_kernel(streams, group_blocks, part_count, info, picks, rows_ref, *refs):
    own_refs = refs[: len(streams)]
    outgoing_refs = refs[len(streams) : 2 * len(streams)]
    turned = refs[-1]
    block = own_refs[0].shape[2]
    part_width = own_refs[0].shape[1]
    first = pl.multiple_of(info[0] * part_width, part_width)
    for stream, own_ref, outgoing_ref in zip(streams, own_refs, outgoing_refs):
        for local in range(len(stream) * group_blocks):
            row = (stream[0] * group_blocks + local) * block
            turned[local % 2] = rows_ref[row : row + block, :].T
            own_ref[local] = turned[local % 2, pl.ds(first, part_width), :]
        pick_outgoing(picks, own_ref, outgoing_ref, stream, group_blocks, part_count)


def prologue(initial_features, section, picks, streams, group_blocks, block, part_width, part_count):
    rows, width = initial_features.shape
    own_shapes = [(len(s) * group_blocks, part_width, block) for s in streams]
    out_shapes = [(part_count, len(s), part_width, block) for s in streams]
    return pl.pallas_call(
        functools.partial(prologue_kernel, streams, group_blocks, part_count),
        grid_spec=pltpu.PrefetchScalarGridSpec(
            num_scalar_prefetch=2,
            grid=(1,),
            in_specs=[whole((rows, width))],
            out_specs=[whole(s) for s in own_shapes + out_shapes],
            scratch_shapes=[pltpu.VMEM((2, width, block), jnp.bfloat16)],
        ),
        out_shape=[jax.ShapeDtypeStruct(s, jnp.bfloat16) for s in own_shapes + out_shapes],
        compiler_params=params(),
        name="prologue",
    )(section, picks, initial_features)


def turn_kernel(info, in_ref, *refs):
    *out_refs, turned = refs
    count = in_ref.shape[-3]
    sections, part_width = len(out_refs), out_refs[0].shape[1]
    for item in range(count):
        turned[item % 2] = in_ref[0, item].T if len(in_ref.shape) == 4 else in_ref[0, 0, item].T
        for distance, out_ref in enumerate(out_refs):
            owner = lax.rem(info[0] + distance, sections)
            first = pl.multiple_of(owner * part_width, part_width)
            out_ref[item] = turned[item % 2, pl.ds(first, part_width), :]


def turn_blocks(section, blocks, lead, sections):
    count, rows, width = blocks.shape[-3:]
    step = 8 if count % 8 == 0 else count
    part_width = width // sections
    block_shape = (1,) * (len(blocks.shape) - 3) + (step, rows, width)
    out_spec = pl.BlockSpec((step, part_width, rows), lambda i, *prefetched: (i, 0, 0))
    return pl.pallas_call(
        turn_kernel,
        grid_spec=pltpu.PrefetchScalarGridSpec(
            num_scalar_prefetch=1,
            grid=(count // step,),
            in_specs=[pl.BlockSpec(block_shape, lambda i, *prefetched: lead + (i, 0, 0))],
            out_specs=[out_spec] * sections,
            scratch_shapes=[pltpu.VMEM((2, width, rows), jnp.bfloat16)],
        ),
        out_shape=[in_hbm((count, part_width, rows))] * sections,
        compiler_params=params(),
        name="turn",
    )(section, blocks)


def aggregate_kernel(plan, columns, info, initial_ref, tiles_ref, *refs):
    stream, group_blocks, fanout, sources, home, sections = plan
    source_refs = refs[: len(sources)]
    mixed_ref, table, tiles, initial, table_sem, tiles_sem, initial_sem = refs[-7:]
    rows = len(stream) * group_blocks
    first_row = stream[0] * group_blocks

    def tile_copy(row):
        return pltpu.make_async_copy(tiles_ref.at[first_row + row], tiles.at[row], tiles_sem.at[row])

    initial_copy = pltpu.make_async_copy(initial_ref, initial, initial_sem)
    copies = []
    for index, (kind, target, detail) in enumerate(sources):
        ref = source_refs[index]
        source = ref.at[:, detail] if kind == "import" else ref
        condition = None
        if kind == "stale":
            condition = lax.rem(info[0] - home + 2 * sections, sections) == detail
        copies.append(
            (
                condition,
                pltpu.make_async_copy(
                    source, table.at[pl.ds(target, source.shape[0])], table_sem.at[index]
                ),
            )
        )
    start_all(copies)
    for row in range(min(2, rows)):
        tile_copy(row).start()
    initial_copy.start()
    wait_all(copies)

    for row in range(rows):
        tile_copy(row).wait()
        if row + 2 < rows:
            tile_copy(row + 2).start()
        if row == 0:
            initial_copy.wait()
        base = (first_row + row) * fanout
        total = None
        for tile in range(0, fanout, 2):
            span = range(tile, min(tile + 2, fanout))
            left = jnp.concatenate([table[columns[base + t]] for t in span], 1)
            right = jnp.concatenate([tiles[row, t] for t in span], 1)
            term = lax.dot_general(
                left, right, (((1,), (1,)), ((), ())), preferred_element_type=jnp.float32
            )
            total = term if total is None else total + term
        mixed_ref[row] = (
            (1.0 - alpha_mix) * total + alpha_mix * initial[row].astype(jnp.float32)
        ).astype(jnp.bfloat16)


def aggregate(columns, section, initial_blocks, tiles, own, imports, stale, home, stream, streams, group_blocks, part_count, after):
    rows, part_width, block = initial_blocks.shape
    blocks_dev, fanout = tiles.shape[:2]
    groups = blocks_dev // group_blocks
    sources, operands = [], []
    for other, own_blocks, imported in zip(streams, own, imports):
        if other[0] > stream[-1]:
            continue
        sources.append(("own", other[0] * group_blocks, None))
        operands.append(own_blocks)
        for local, group in enumerate(other):
            sources.append(("import", blocks_dev + group * part_count, local))
            operands.append(imported)
    if groups > 1 and stream[0] < groups - 1:
        for distance, stale_blocks in enumerate(stale):
            sources.append(("stale", blocks_dev + groups * part_count, distance))
            operands.append(stale_blocks)
    operands += after
    table_size = blocks_dev + (2 * groups - 1) * part_count
    plan = (stream, group_blocks, fanout, sources, home, len(stale))
    flops = 2 * rows * fanout * block * block * part_width
    return pl.pallas_call(
        functools.partial(aggregate_kernel, plan),
        grid_spec=pltpu.PrefetchScalarGridSpec(
            num_scalar_prefetch=2,
            grid=(1,),
            in_specs=[pl.BlockSpec(memory_space=pl.ANY)] * (2 + len(operands)),
            out_specs=whole((rows, part_width, block)),
            scratch_shapes=[
                pltpu.VMEM((table_size, part_width, block), jnp.bfloat16),
                pltpu.VMEM((rows, fanout, block, block), jnp.bfloat16),
                pltpu.VMEM(initial_blocks.shape, jnp.bfloat16),
                pltpu.SemaphoreType.DMA((len(sources),)),
                pltpu.SemaphoreType.DMA((rows,)),
                pltpu.SemaphoreType.DMA,
            ],
        ),
        out_shape=jax.ShapeDtypeStruct((rows, part_width, block), jnp.bfloat16),
        cost_estimate=pl.CostEstimate(
            flops=flops, bytes_accessed=rows * fanout * block * block * 2, transcendentals=0
        ),
        compiler_params=params(),
        name="aggregate",
    )(columns, section, initial_blocks, tiles, *operands)


def finish_kernel(plan, picks, info, mixed_ref, gathered_ref, *refs):
    beta_layer, stream, group_blocks, part_count, sub, home, last = plan
    rows, part_width, block = mixed_ref.shape
    parts = gathered_ref.shape[0]
    weight_refs = refs[:parts]
    weight, weight_sem = refs[-2:]
    refs = refs[parts:-2]
    copies = [
        (
            lax.rem(info[0] - home + 2 * parts, parts) == distance,
            pltpu.make_async_copy(weight_ref.at[sub], weight, weight_sem.at[distance]),
        )
        for distance, weight_ref in enumerate(weight_refs)
    ]
    start_all(copies)
    wait_all(copies)
    for row in range(0, rows, 2):
        span = range(row, min(row + 2, rows))
        right = jnp.concatenate(
            [jnp.concatenate([gathered_ref[p, r] for p in range(parts)], 0) for r in span], 1
        )
        product = jnp.dot(weight[...], right, preferred_element_type=jnp.float32)
        for place, r in enumerate(span):
            value = (1.0 - beta_layer) * mixed_ref[r].astype(jnp.float32) + beta_layer * product[
                :, place * block : (place + 1) * block
            ]
            value = jnp.maximum(value, 0.0).astype(jnp.bfloat16)
            if last:
                refs[0][r * block : (r + 1) * block, :] = value.T
            else:
                refs[0][r] = value
    if not last:
        pick_outgoing(picks, refs[0], refs[1], stream, group_blocks, part_count)
        refs[2][...] = jnp.zeros_like(refs[2])


def finish(picks, section, mixed, gathered, weights, layer, depth, stream, group_blocks, part_count, last):
    rows, part_width, block = mixed.shape
    width = weights[0].shape[2]
    beta_layer = math.log(lambda_decay / (layer + 1) + 1.0)
    plan = (
        beta_layer, stream, group_blocks, part_count, layer % depth, layer // depth, last,
    )
    if last:
        shapes = [(rows * block, part_width)]
        out_shape = [jax.ShapeDtypeStruct(shapes[0], jnp.bfloat16)]
    else:
        outgoing = (part_count, len(stream), part_width, block)
        shapes = [(rows, part_width, block), outgoing, (16, 128)]
        out_shape = [
            in_hbm(shapes[0]),
            jax.ShapeDtypeStruct(outgoing, jnp.bfloat16),
            jax.ShapeDtypeStruct((16, 128), jnp.bfloat16),
        ]
    return pl.pallas_call(
        functools.partial(finish_kernel, plan),
        grid_spec=pltpu.PrefetchScalarGridSpec(
            num_scalar_prefetch=2,
            grid=(1,),
            in_specs=[whole(mixed.shape), whole(gathered.shape)]
            + [pl.BlockSpec(memory_space=pl.ANY)] * len(weights),
            out_specs=[whole(s) for s in shapes],
            scratch_shapes=[
                pltpu.VMEM((part_width, width), jnp.bfloat16),
                pltpu.SemaphoreType.DMA((len(weights),)),
            ],
        ),
        out_shape=out_shape,
        cost_estimate=pl.CostEstimate(
            flops=2 * rows * block * width * part_width,
            bytes_accessed=rows * block * width * 2,
            transcendentals=0,
        ),
        compiler_params=params(),
        name="finish",
    )(picks, section, mixed, gathered, *weights)


def per_device(
    initial_features, layer_weights, adjacency_tiles, tile_columns, send_blocks, stale_imports
):
    section_count = lax.axis_size("section")
    part_count = lax.axis_size("dom")
    blocks_dev, fanout, block = adjacency_tiles.shape[:3]
    width = initial_features.shape[1]
    part_width = width // section_count
    groups = send_blocks.shape[1]
    group_blocks = blocks_dev // groups
    depth = layer_weights.shape[0]
    layers = depth * section_count
    streams = group_streams(groups)
    section = lax.axis_index("section").astype(jnp.int32).reshape(1)
    picks = send_blocks.reshape(-1)

    row_group = (jnp.arange(blocks_dev, dtype=jnp.int32) // group_blocks)[:, None]
    slot_group = (tile_columns - blocks_dev) // part_count
    is_stale = (tile_columns >= blocks_dev) & (slot_group > row_group)
    columns = jnp.where(
        is_stale, tile_columns + (groups - 1) * part_count, tile_columns
    ).reshape(-1)

    started = prologue(
        initial_features, section, picks, streams, group_blocks, block, part_width, part_count
    )
    own = started[: len(streams)]
    outgoing = started[len(streams) :]
    initial_blocks = own

    def exchange(value):
        return lax.all_to_all(value, "dom", split_axis=0, concat_axis=0, tiled=True)

    def spread(pieces):
        ring = range(section_count)
        return [pieces[0]] + [
            lax.ppermute(
                pieces[distance], "section", [(s, (s + distance) % section_count) for s in ring]
            )
            for distance in range(1, section_count)
        ]

    imports = [exchange(value) for value in outgoing]
    stale = [
        spread(turn_blocks(section, stale_imports, (sub, 0), section_count))
        for sub in range(depth)
    ]
    weights = spread(turn_blocks(section, layer_weights[None], (0,), section_count))

    pieces = []
    after = []
    for layer in range(layers):
        last = layer == layers - 1
        own_next, imports_next = [], []
        for index, stream in enumerate(streams):
            mixed = aggregate(
                columns,
                section,
                initial_blocks[index],
                adjacency_tiles,
                own,
                imports,
                stale[layer % depth],
                layer // depth,
                stream,
                streams,
                group_blocks,
                part_count,
                after,
            )
            gathered = lax.all_gather(mixed, "section", axis=0, tiled=False)
            result = finish(
                picks, section, mixed, gathered, weights, layer, depth, stream, group_blocks,
                part_count, last,
            )
            if last:
                pieces.append(result[0])
            else:
                after = [result[2]]
                own_next.append(result[0])
                imports_next.append(exchange(result[1]))
        own, imports = own_next, imports_next
    return jnp.concatenate(pieces, 0) if len(pieces) > 1 else pieces[0]


def solution(mesh):
    return jax.shard_map(
        per_device,
        mesh=mesh,
        in_specs=(
            P("dom", None),
            P("section", None, None),
            P("dom", None, None, None),
            P("dom", None),
            P("dom", None, None),
            P("section", "dom", None, None, None),
        ),
        out_specs=P("dom", "section"),
        check_vma=False,
    )
```

```python
import functools
import math

import jax
import jax.numpy as jnp
from jax import lax
from jax.experimental import pallas as pl
from jax.experimental.pallas import tpu as pltpu
from jax.sharding import PartitionSpec as P

alpha_mix = 0.1
lambda_decay = 0.5
vmem_bytes = 48 * 1024 * 1024


def group_streams(groups):
    return [list(range(groups - 1)), [groups - 1]]


def params():
    return pltpu.CompilerParams(vmem_limit_bytes=vmem_bytes)


def in_hbm(shape):
    return pltpu.HBM(shape, jnp.bfloat16)


hbm = pl.BlockSpec(memory_space=pltpu.HBM)
anywhere = pl.BlockSpec(memory_space=pl.ANY)


def pinned(value):
    return pltpu.with_memory_space_constraint(value, pltpu.HBM)


def start_all(copies):
    for condition, copy in copies:
        if condition is None:
            copy.start()
        else:
            pl.when(condition)(copy.start)


def wait_all(copies):
    for condition, copy in copies:
        if condition is None:
            copy.wait()
        else:
            pl.when(condition)(copy.wait)


def whole(shape):
    return pl.BlockSpec(shape, lambda i, *prefetched: (0,) * len(shape))


def pick_outgoing(picks, blocks_ref, outgoing_ref, stream, group_blocks, part_count):
    for local, group in enumerate(stream):

        def pick(dest, carry):
            chosen = jnp.maximum(picks[group * part_count + dest], 0)
            outgoing_ref[dest, local] = blocks_ref[local * group_blocks + chosen]
            return carry

        lax.fori_loop(0, part_count, pick, 0)


def prologue_kernel(streams, group_blocks, part_count, info, picks, rows_ref, unused, *refs):
    own_refs = refs[: len(streams)]
    outgoing_refs = refs[len(streams) : 2 * len(streams)]
    turned = refs[-1]
    block = own_refs[0].shape[2]
    part_width = own_refs[0].shape[1]
    first = pl.multiple_of(info[0] * part_width, part_width)
    for stream, own_ref, outgoing_ref in zip(streams, own_refs, outgoing_refs):
        for local in range(len(stream) * group_blocks):
            row = (stream[0] * group_blocks + local) * block
            turned[local % 2] = rows_ref[row : row + block, :].T
            own_ref[local] = turned[local % 2, pl.ds(first, part_width), :]
        pick_outgoing(picks, own_ref, outgoing_ref, stream, group_blocks, part_count)


def prologue(initial_features, section, picks, after, streams, group_blocks, block, part_width, part_count):
    rows, width = initial_features.shape
    own_shapes = [(len(s) * group_blocks, part_width, block) for s in streams]
    out_shapes = [(part_count, len(s), part_width, block) for s in streams]
    return pl.pallas_call(
        functools.partial(prologue_kernel, streams, group_blocks, part_count),
        grid_spec=pltpu.PrefetchScalarGridSpec(
            num_scalar_prefetch=2,
            grid=(1,),
            in_specs=[whole((rows, width)), hbm],
            out_specs=[whole(s) for s in own_shapes + out_shapes],
            scratch_shapes=[pltpu.VMEM((2, width, block), jnp.bfloat16)],
        ),
        out_shape=[in_hbm(s) for s in own_shapes]
        + [jax.ShapeDtypeStruct(s, jnp.bfloat16) for s in out_shapes],
        compiler_params=params(),
        name="prologue",
    )(section, picks, pinned(initial_features), pinned(after))


def turn_kernel(info, in_ref, *refs):
    *out_refs, turned = refs
    count = in_ref.shape[-3]
    sections, part_width = len(out_refs), out_refs[0].shape[1]
    for item in range(count):
        turned[item % 2] = in_ref[0, item].T if len(in_ref.shape) == 4 else in_ref[0, 0, item].T
        for distance, out_ref in enumerate(out_refs):
            owner = lax.rem(info[0] + distance, sections)
            first = pl.multiple_of(owner * part_width, part_width)
            out_ref[item] = turned[item % 2, pl.ds(first, part_width), :]


def turn_blocks(section, blocks, lead, sections):
    count, rows, width = blocks.shape[-3:]
    step = 8 if count % 8 == 0 else count
    part_width = width // sections
    block_shape = (1,) * (len(blocks.shape) - 3) + (step, rows, width)
    out_spec = pl.BlockSpec((step, part_width, rows), lambda i, *prefetched: (i, 0, 0))
    return pl.pallas_call(
        turn_kernel,
        grid_spec=pltpu.PrefetchScalarGridSpec(
            num_scalar_prefetch=1,
            grid=(count // step,),
            in_specs=[pl.BlockSpec(block_shape, lambda i, *prefetched: lead + (i, 0, 0))],
            out_specs=[out_spec] * sections,
            scratch_shapes=[pltpu.VMEM((2, width, rows), jnp.bfloat16)],
        ),
        out_shape=[in_hbm((count, part_width, rows))] * sections,
        compiler_params=params(),
        name="turn",
    )(section, pinned(blocks))


def aggregate_kernel(plan, columns, info, initial_ref, tiles_ref, *refs):
    stream, group_blocks, fanout, sources, home, sections = plan
    source_refs = refs[: len(sources)]
    mixed_ref, table, tiles, initial, table_sem, tiles_sem, initial_sem = refs[-7:]
    rows = len(stream) * group_blocks
    first_row = stream[0] * group_blocks

    def tile_copy(row):
        return pltpu.make_async_copy(tiles_ref.at[first_row + row], tiles.at[row], tiles_sem.at[row])

    initial_copy = pltpu.make_async_copy(initial_ref, initial, initial_sem)
    copies = []
    for index, (kind, target, detail) in enumerate(sources):
        ref = source_refs[index]
        source = ref.at[:, detail] if kind == "import" else ref
        condition = None
        if kind == "stale":
            condition = lax.rem(info[0] - home + 2 * sections, sections) == detail
        copies.append(
            (
                condition,
                pltpu.make_async_copy(
                    source, table.at[pl.ds(target, source.shape[0])], table_sem.at[index]
                ),
            )
        )
    start_all(copies)
    initial_copy.start()
    for row in range(rows):
        tile_copy(row).start()
    wait_all(copies)
    initial_copy.wait()

    def one_row(row, carry):
        tile_copy(row).wait()
        base = (first_row + row) * fanout
        total = None
        for tile in range(0, fanout, 2):
            span = range(tile, min(tile + 2, fanout))
            left = jnp.concatenate([table[columns[base + t]] for t in span], 1)
            right = jnp.concatenate([tiles[row, t] for t in span], 1)
            term = lax.dot_general(
                left, right, (((1,), (1,)), ((), ())), preferred_element_type=jnp.float32
            )
            total = term if total is None else total + term
        mixed_ref[row] = (
            (1.0 - alpha_mix) * total + alpha_mix * initial[row].astype(jnp.float32)
        ).astype(jnp.bfloat16)
        return carry

    lax.fori_loop(0, rows, one_row, 0)


def aggregate(columns, section, initial_blocks, tiles, own, imports, stale, home, stream, streams, group_blocks, part_count, after):
    rows, part_width, block = initial_blocks.shape
    blocks_dev, fanout = tiles.shape[:2]
    groups = blocks_dev // group_blocks
    sources, operands, specs = [], [], []
    for other, own_blocks, imported in zip(streams, own, imports):
        if other[0] > stream[-1]:
            continue
        sources.append(("own", other[0] * group_blocks, None))
        operands.append(pinned(own_blocks))
        specs.append(hbm)
        for local, group in enumerate(other):
            sources.append(("import", blocks_dev + group * part_count, local))
            operands.append(imported)
            specs.append(anywhere)
    if groups > 1 and stream[0] < groups - 1:
        for distance, stale_blocks in enumerate(stale):
            sources.append(("stale", blocks_dev + groups * part_count, distance))
            operands.append(pinned(stale_blocks))
            specs.append(hbm)
    operands += after
    specs += [anywhere] * len(after)
    table_size = blocks_dev + (2 * groups - 1) * part_count
    plan = (stream, group_blocks, fanout, sources, home, len(stale))
    flops = 2 * rows * fanout * block * block * part_width
    return pl.pallas_call(
        functools.partial(aggregate_kernel, plan),
        grid_spec=pltpu.PrefetchScalarGridSpec(
            num_scalar_prefetch=2,
            grid=(1,),
            in_specs=[hbm, hbm] + specs,
            out_specs=whole((rows, part_width, block)),
            scratch_shapes=[
                pltpu.VMEM((table_size, part_width, block), jnp.bfloat16),
                pltpu.VMEM((rows, fanout, block, block), jnp.bfloat16),
                pltpu.VMEM(initial_blocks.shape, jnp.bfloat16),
                pltpu.SemaphoreType.DMA((len(sources),)),
                pltpu.SemaphoreType.DMA((rows,)),
                pltpu.SemaphoreType.DMA,
            ],
        ),
        out_shape=jax.ShapeDtypeStruct((rows, part_width, block), jnp.bfloat16),
        cost_estimate=pl.CostEstimate(
            flops=flops, bytes_accessed=rows * fanout * block * block * 2, transcendentals=0
        ),
        compiler_params=params(),
        name="aggregate",
    )(columns, section, pinned(initial_blocks), pinned(tiles), *operands)


def finish_kernel(plan, picks, info, mixed_ref, gathered_ref, *refs):
    beta_layer, stream, group_blocks, part_count, sub, home, last = plan
    rows, part_width, block = mixed_ref.shape
    parts = gathered_ref.shape[0]
    weight_refs = refs[:parts]
    weight, weight_sem = refs[-2:]
    refs = refs[parts:-2]
    copies = [
        (
            lax.rem(info[0] - home + 2 * parts, parts) == distance,
            pltpu.make_async_copy(weight_ref.at[sub], weight, weight_sem.at[distance]),
        )
        for distance, weight_ref in enumerate(weight_refs)
    ]
    start_all(copies)
    wait_all(copies)
    for row in range(0, rows, 2):
        span = range(row, min(row + 2, rows))
        right = jnp.concatenate(
            [jnp.concatenate([gathered_ref[p, r] for p in range(parts)], 0) for r in span], 1
        )
        product = jnp.dot(weight[...], right, preferred_element_type=jnp.float32)
        for place, r in enumerate(span):
            value = (1.0 - beta_layer) * mixed_ref[r].astype(jnp.float32) + beta_layer * product[
                :, place * block : (place + 1) * block
            ]
            value = jnp.maximum(value, 0.0).astype(jnp.bfloat16)
            if last:
                refs[0][r * block : (r + 1) * block, :] = value.T
            else:
                refs[0][r] = value
    if not last:
        pick_outgoing(picks, refs[0], refs[1], stream, group_blocks, part_count)
        refs[2][...] = jnp.zeros_like(refs[2])


def finish(picks, section, mixed, gathered, weights, layer, depth, stream, group_blocks, part_count, last):
    rows, part_width, block = mixed.shape
    width = weights[0].shape[2]
    beta_layer = math.log(lambda_decay / (layer + 1) + 1.0)
    plan = (
        beta_layer, stream, group_blocks, part_count, layer % depth, layer // depth, last,
    )
    if last:
        shapes = [(rows * block, part_width)]
        out_shape = [jax.ShapeDtypeStruct(shapes[0], jnp.bfloat16)]
    else:
        outgoing = (part_count, len(stream), part_width, block)
        shapes = [(rows, part_width, block), outgoing, (16, 128)]
        out_shape = [
            in_hbm(shapes[0]),
            jax.ShapeDtypeStruct(outgoing, jnp.bfloat16),
            jax.ShapeDtypeStruct((16, 128), jnp.bfloat16),
        ]
    return pl.pallas_call(
        functools.partial(finish_kernel, plan),
        grid_spec=pltpu.PrefetchScalarGridSpec(
            num_scalar_prefetch=2,
            grid=(1,),
            in_specs=[whole(mixed.shape), whole(gathered.shape)]
            + [hbm] * len(weights),
            out_specs=[whole(s) for s in shapes],
            scratch_shapes=[
                pltpu.VMEM((part_width, width), jnp.bfloat16),
                pltpu.SemaphoreType.DMA((len(weights),)),
            ],
        ),
        out_shape=out_shape,
        cost_estimate=pl.CostEstimate(
            flops=2 * rows * block * width * part_width,
            bytes_accessed=rows * block * width * 2,
            transcendentals=0,
        ),
        compiler_params=params(),
        name="finish",
    )(picks, section, mixed, gathered, *[pinned(w) for w in weights])


def per_device(
    initial_features, layer_weights, adjacency_tiles, tile_columns, send_blocks, stale_imports
):
    section_count = lax.axis_size("section")
    part_count = lax.axis_size("dom")
    blocks_dev, fanout, block = adjacency_tiles.shape[:3]
    width = initial_features.shape[1]
    part_width = width // section_count
    groups = send_blocks.shape[1]
    group_blocks = blocks_dev // groups
    depth = layer_weights.shape[0]
    layers = depth * section_count
    streams = group_streams(groups)
    section = lax.axis_index("section").astype(jnp.int32).reshape(1)
    picks = send_blocks.reshape(-1)

    row_group = (jnp.arange(blocks_dev, dtype=jnp.int32) // group_blocks)[:, None]
    slot_group = (tile_columns - blocks_dev) // part_count
    is_stale = (tile_columns >= blocks_dev) & (slot_group > row_group)
    columns = jnp.where(
        is_stale, tile_columns + (groups - 1) * part_count, tile_columns
    ).reshape(-1)

    turned = [
        turn_blocks(section, stale_imports, (sub, 0), section_count) for sub in range(depth)
    ]
    started = prologue(
        initial_features, section, picks, turned[0][0], streams, group_blocks, block, part_width, part_count
    )
    own = started[: len(streams)]
    outgoing = started[len(streams) :]
    initial_blocks = own

    def exchange(value):
        return lax.all_to_all(value, "dom", split_axis=0, concat_axis=0, tiled=True)

    def spread(pieces):
        ring = range(section_count)
        return [pieces[0]] + [
            lax.ppermute(
                pieces[distance], "section", [(s, (s + distance) % section_count) for s in ring]
            )
            for distance in range(1, section_count)
        ]

    imports = [exchange(value) for value in outgoing]
    stale = [spread(pieces) for pieces in turned]
    weights = spread(turn_blocks(section, layer_weights[None], (0,), section_count))

    pieces = []
    after = []
    for layer in range(layers):
        last = layer == layers - 1
        own_next, imports_next = [], []
        for index, stream in enumerate(streams):
            mixed = aggregate(
                columns,
                section,
                initial_blocks[index],
                adjacency_tiles,
                own,
                imports,
                stale[layer % depth],
                layer // depth,
                stream,
                streams,
                group_blocks,
                part_count,
                after,
            )
            gathered = lax.all_gather(mixed, "section", axis=0, tiled=False)
            result = finish(
                picks, section, mixed, gathered, weights, layer, depth, stream, group_blocks,
                part_count, last,
            )
            if last:
                pieces.append(result[0])
            else:
                after = [result[2]]
                own_next.append(result[0])
                imports_next.append(exchange(result[1]))
        own, imports = own_next, imports_next
    return jnp.concatenate(pieces, 0) if len(pieces) > 1 else pieces[0]


def solution(mesh):
    return jax.shard_map(
        per_device,
        mesh=mesh,
        in_specs=(
            P("dom", None),
            P("section", None, None),
            P("dom", None, None, None),
            P("dom", None),
            P("dom", None, None),
            P("section", "dom", None, None, None),
        ),
        out_specs=P("dom", "section"),
        check_vma=False,
    )
```

```python
import functools
import math

import jax
import jax.numpy as jnp
from jax import lax
from jax.experimental import pallas as pl
from jax.experimental.pallas import tpu as pltpu
from jax.sharding import PartitionSpec as P

alpha_mix = 0.1
lambda_decay = 0.5
vmem_bytes = 48 * 1024 * 1024


def group_streams(groups):
    return [list(range(groups - 1)), [groups - 1]]


def params():
    return pltpu.CompilerParams(vmem_limit_bytes=vmem_bytes)


def in_hbm(shape):
    return pltpu.HBM(shape, jnp.bfloat16)


hbm = pl.BlockSpec(memory_space=pltpu.HBM)
anywhere = pl.BlockSpec(memory_space=pl.ANY)


def pinned(value):
    return pltpu.with_memory_space_constraint(value, pltpu.HBM)


def start_all(copies):
    for condition, copy in copies:
        if condition is None:
            copy.start()
        else:
            pl.when(condition)(copy.start)


def wait_all(copies):
    for condition, copy in copies:
        if condition is None:
            copy.wait()
        else:
            pl.when(condition)(copy.wait)


def whole(shape):
    return pl.BlockSpec(shape, lambda i, *prefetched: (0,) * len(shape))


def pick_outgoing(picks, blocks_ref, outgoing_ref, stream, group_blocks, part_count):
    for local, group in enumerate(stream):

        def pick(dest, carry):
            chosen = jnp.maximum(picks[group * part_count + dest], 0)
            outgoing_ref[dest, local] = blocks_ref[local * group_blocks + chosen]
            return carry

        lax.fori_loop(0, part_count, pick, 0)


def prologue_kernel(streams, group_blocks, part_count, info, picks, rows_ref, unused, *refs):
    own_refs = refs[: len(streams)]
    outgoing_refs = refs[len(streams) : 2 * len(streams)]
    turned = refs[-1]
    block = own_refs[0].shape[2]
    part_width = own_refs[0].shape[1]
    first = pl.multiple_of(info[0] * part_width, part_width)
    for stream, own_ref, outgoing_ref in zip(streams, own_refs, outgoing_refs):
        for local in range(len(stream) * group_blocks):
            row = (stream[0] * group_blocks + local) * block
            turned[local % 2] = rows_ref[row : row + block, :].T
            own_ref[local] = turned[local % 2, pl.ds(first, part_width), :]
        pick_outgoing(picks, own_ref, outgoing_ref, stream, group_blocks, part_count)


def prologue(initial_features, section, picks, after, streams, group_blocks, block, part_width, part_count):
    rows, width = initial_features.shape
    own_shapes = [(len(s) * group_blocks, part_width, block) for s in streams]
    out_shapes = [(part_count, len(s), part_width, block) for s in streams]
    return pl.pallas_call(
        functools.partial(prologue_kernel, streams, group_blocks, part_count),
        grid_spec=pltpu.PrefetchScalarGridSpec(
            num_scalar_prefetch=2,
            grid=(1,),
            in_specs=[whole((rows, width)), hbm],
            out_specs=[whole(s) for s in own_shapes + out_shapes],
            scratch_shapes=[pltpu.VMEM((2, width, block), jnp.bfloat16)],
        ),
        out_shape=[in_hbm(s) for s in own_shapes]
        + [jax.ShapeDtypeStruct(s, jnp.bfloat16) for s in out_shapes],
        compiler_params=params(),
        name="prologue",
    )(section, picks, pinned(initial_features), pinned(after))


def turn_kernel(info, in_ref, *refs):
    *out_refs, turned = refs
    count = in_ref.shape[-3]
    sections, part_width = len(out_refs), out_refs[0].shape[1]
    for item in range(count):
        turned[item % 2] = in_ref[0, item].T if len(in_ref.shape) == 4 else in_ref[0, 0, item].T
        for distance, out_ref in enumerate(out_refs):
            owner = lax.rem(info[0] + distance, sections)
            first = pl.multiple_of(owner * part_width, part_width)
            out_ref[item] = turned[item % 2, pl.ds(first, part_width), :]


def turn_blocks(section, blocks, lead, sections):
    count, rows, width = blocks.shape[-3:]
    step = 8 if count % 8 == 0 else count
    part_width = width // sections
    block_shape = (1,) * (len(blocks.shape) - 3) + (step, rows, width)
    out_spec = pl.BlockSpec((step, part_width, rows), lambda i, *prefetched: (i, 0, 0))
    return pl.pallas_call(
        turn_kernel,
        grid_spec=pltpu.PrefetchScalarGridSpec(
            num_scalar_prefetch=1,
            grid=(count // step,),
            in_specs=[pl.BlockSpec(block_shape, lambda i, *prefetched: lead + (i, 0, 0))],
            out_specs=[out_spec] * sections,
            scratch_shapes=[pltpu.VMEM((2, width, rows), jnp.bfloat16)],
        ),
        out_shape=[in_hbm((count, part_width, rows))] * sections,
        compiler_params=params(),
        name="turn",
    )(section, pinned(blocks))


def aggregate_kernel(plan, columns, info, initial_ref, tiles_ref, *refs):
    stream, group_blocks, fanout, sources, home, sections = plan
    source_refs = refs[: len(sources)]
    mixed_ref, table, tiles, initial, table_sem, tiles_sem, initial_sem = refs[-7:]
    rows = len(stream) * group_blocks
    first_row = stream[0] * group_blocks

    def tile_copy(row):
        return pltpu.make_async_copy(tiles_ref.at[first_row + row], tiles.at[row], tiles_sem.at[row])

    initial_copy = pltpu.make_async_copy(initial_ref, initial, initial_sem)
    copies = []
    for index, (kind, target, detail) in enumerate(sources):
        ref = source_refs[index]
        source = ref.at[:, detail] if kind == "import" else ref
        condition = None
        if kind == "stale":
            condition = lax.rem(info[0] - home + 2 * sections, sections) == detail
        copies.append(
            (
                condition,
                pltpu.make_async_copy(
                    source, table.at[pl.ds(target, source.shape[0])], table_sem.at[index]
                ),
            )
        )
    start_all(copies)
    tile_copy(0).start()
    wait_all(copies)
    initial_copy.start()
    for row in range(1, rows):
        tile_copy(row).start()
    initial_copy.wait()

    def one_row(row, carry):
        tile_copy(row).wait()
        base = (first_row + row) * fanout
        total = None
        for tile in range(0, fanout, 2):
            span = range(tile, min(tile + 2, fanout))
            left = jnp.concatenate([table[columns[base + t]] for t in span], 1)
            right = jnp.concatenate([tiles[row, t] for t in span], 1)
            term = lax.dot_general(
                left, right, (((1,), (1,)), ((), ())), preferred_element_type=jnp.float32
            )
            total = term if total is None else total + term
        mixed_ref[row] = (
            (1.0 - alpha_mix) * total + alpha_mix * initial[row].astype(jnp.float32)
        ).astype(jnp.bfloat16)
        return carry

    lax.fori_loop(0, rows, one_row, 0)


def aggregate(columns, section, initial_blocks, tiles, own, imports, stale, home, stream, streams, group_blocks, part_count, after):
    rows, part_width, block = initial_blocks.shape
    blocks_dev, fanout = tiles.shape[:2]
    groups = blocks_dev // group_blocks
    sources, operands, specs = [], [], []
    for other, own_blocks, imported in zip(streams, own, imports):
        if other[0] > stream[-1]:
            continue
        sources.append(("own", other[0] * group_blocks, None))
        operands.append(pinned(own_blocks))
        specs.append(hbm)
        for local, group in enumerate(other):
            sources.append(("import", blocks_dev + group * part_count, local))
            operands.append(imported)
            specs.append(anywhere)
    if groups > 1 and stream[0] < groups - 1:
        for distance, stale_blocks in enumerate(stale):
            sources.append(("stale", blocks_dev + groups * part_count, distance))
            operands.append(pinned(stale_blocks))
            specs.append(hbm)
    operands += [pinned(value) for value in after]
    specs += [hbm] * len(after)
    table_size = blocks_dev + (2 * groups - 1) * part_count
    plan = (stream, group_blocks, fanout, sources, home, len(stale))
    flops = 2 * rows * fanout * block * block * part_width
    return pl.pallas_call(
        functools.partial(aggregate_kernel, plan),
        grid_spec=pltpu.PrefetchScalarGridSpec(
            num_scalar_prefetch=2,
            grid=(1,),
            in_specs=[hbm, hbm] + specs,
            out_specs=whole((rows, part_width, block)),
            scratch_shapes=[
                pltpu.VMEM((table_size, part_width, block), jnp.bfloat16),
                pltpu.VMEM((rows, fanout, block, block), jnp.bfloat16),
                pltpu.VMEM(initial_blocks.shape, jnp.bfloat16),
                pltpu.SemaphoreType.DMA((len(sources),)),
                pltpu.SemaphoreType.DMA((rows,)),
                pltpu.SemaphoreType.DMA,
            ],
        ),
        out_shape=jax.ShapeDtypeStruct((rows, part_width, block), jnp.bfloat16),
        cost_estimate=pl.CostEstimate(
            flops=flops, bytes_accessed=rows * fanout * block * block * 2, transcendentals=0
        ),
        compiler_params=params(),
        name="aggregate",
    )(columns, section, pinned(initial_blocks), pinned(tiles), *operands)


def finish_kernel(plan, picks, info, mixed_ref, gathered_ref, *refs):
    beta_layer, stream, group_blocks, part_count, sub, home, last = plan
    rows, part_width, block = mixed_ref.shape
    parts = gathered_ref.shape[0]
    weight_refs = refs[:parts]
    weight, weight_sem = refs[-2:]
    refs = refs[parts:-2]
    copies = [
        (
            lax.rem(info[0] - home + 2 * parts, parts) == distance,
            pltpu.make_async_copy(weight_ref.at[sub], weight, weight_sem.at[distance]),
        )
        for distance, weight_ref in enumerate(weight_refs)
    ]
    start_all(copies)
    wait_all(copies)
    for row in range(0, rows, 2):
        span = range(row, min(row + 2, rows))
        right = jnp.concatenate(
            [jnp.concatenate([gathered_ref[p, r] for p in range(parts)], 0) for r in span], 1
        )
        product = jnp.dot(weight[...], right, preferred_element_type=jnp.float32)
        for place, r in enumerate(span):
            value = (1.0 - beta_layer) * mixed_ref[r].astype(jnp.float32) + beta_layer * product[
                :, place * block : (place + 1) * block
            ]
            value = jnp.maximum(value, 0.0).astype(jnp.bfloat16)
            if last:
                refs[0][r * block : (r + 1) * block, :] = value.T
            else:
                refs[0][r] = value
    if not last:
        pick_outgoing(picks, refs[0], refs[1], stream, group_blocks, part_count)
        refs[2][...] = jnp.zeros_like(refs[2])


def finish(picks, section, mixed, gathered, weights, layer, depth, stream, group_blocks, part_count, last):
    rows, part_width, block = mixed.shape
    width = weights[0].shape[2]
    beta_layer = math.log(lambda_decay / (layer + 1) + 1.0)
    plan = (
        beta_layer, stream, group_blocks, part_count, layer % depth, layer // depth, last,
    )
    if last:
        shapes = [(rows * block, part_width)]
        out_shape = [jax.ShapeDtypeStruct(shapes[0], jnp.bfloat16)]
    else:
        outgoing = (part_count, len(stream), part_width, block)
        shapes = [(rows, part_width, block), outgoing, (16, 128)]
        out_shape = [
            in_hbm(shapes[0]),
            jax.ShapeDtypeStruct(outgoing, jnp.bfloat16),
            in_hbm((16, 128)),
        ]
    return pl.pallas_call(
        functools.partial(finish_kernel, plan),
        grid_spec=pltpu.PrefetchScalarGridSpec(
            num_scalar_prefetch=2,
            grid=(1,),
            in_specs=[whole(mixed.shape), whole(gathered.shape)]
            + [anywhere] * len(weights),
            out_specs=[whole(s) for s in shapes],
            scratch_shapes=[
                pltpu.VMEM((part_width, width), jnp.bfloat16),
                pltpu.SemaphoreType.DMA((len(weights),)),
            ],
        ),
        out_shape=out_shape,
        cost_estimate=pl.CostEstimate(
            flops=2 * rows * block * width * part_width,
            bytes_accessed=rows * block * width * 2,
            transcendentals=0,
        ),
        compiler_params=params(),
        name="finish",
    )(picks, section, mixed, gathered, *weights)


def per_device(
    initial_features, layer_weights, adjacency_tiles, tile_columns, send_blocks, stale_imports
):
    section_count = lax.axis_size("section")
    part_count = lax.axis_size("dom")
    blocks_dev, fanout, block = adjacency_tiles.shape[:3]
    width = initial_features.shape[1]
    part_width = width // section_count
    groups = send_blocks.shape[1]
    group_blocks = blocks_dev // groups
    depth = layer_weights.shape[0]
    layers = depth * section_count
    streams = group_streams(groups)
    section = lax.axis_index("section").astype(jnp.int32).reshape(1)
    picks = send_blocks.reshape(-1)

    row_group = (jnp.arange(blocks_dev, dtype=jnp.int32) // group_blocks)[:, None]
    slot_group = (tile_columns - blocks_dev) // part_count
    is_stale = (tile_columns >= blocks_dev) & (slot_group > row_group)
    columns = jnp.where(
        is_stale, tile_columns + (groups - 1) * part_count, tile_columns
    ).reshape(-1)

    turned = [
        turn_blocks(section, stale_imports, (sub, 0), section_count) for sub in range(depth)
    ]
    started = prologue(
        initial_features, section, picks, turned[0][0], streams, group_blocks, block, part_width, part_count
    )
    own = started[: len(streams)]
    outgoing = started[len(streams) :]
    initial_blocks = own

    def exchange(value):
        return lax.all_to_all(value, "dom", split_axis=0, concat_axis=0, tiled=True)

    def spread(pieces):
        ring = range(section_count)
        return [pieces[0]] + [
            lax.ppermute(
                pieces[distance], "section", [(s, (s + distance) % section_count) for s in ring]
            )
            for distance in range(1, section_count)
        ]

    imports = [exchange(value) for value in outgoing]
    stale = [spread(pieces) for pieces in turned]
    weights = spread(turn_blocks(section, layer_weights[None], (0,), section_count))

    pieces = []
    after = [pieces[0] for pieces in turned[1:]]
    for layer in range(layers):
        last = layer == layers - 1
        own_next, imports_next = [], []
        for index, stream in enumerate(streams):
            mixed = aggregate(
                columns,
                section,
                initial_blocks[index],
                adjacency_tiles,
                own,
                imports,
                stale[layer % depth],
                layer // depth,
                stream,
                streams,
                group_blocks,
                part_count,
                after,
            )
            if last:
                after = [mixed[0]]
            gathered = lax.all_gather(mixed, "section", axis=0, tiled=False)
            result = finish(
                picks, section, mixed, gathered, weights, layer, depth, stream, group_blocks,
                part_count, last,
            )
            if last:
                pieces.append(result[0])
            else:
                after = [result[2]]
                own_next.append(result[0])
                imports_next.append(exchange(result[1]))
        own, imports = own_next, imports_next
    return jnp.concatenate(pieces, 0) if len(pieces) > 1 else pieces[0]


def solution(mesh):
    return jax.shard_map(
        per_device,
        mesh=mesh,
        in_specs=(
            P("dom", None),
            P("section", None, None),
            P("dom", None, None, None),
            P("dom", None),
            P("dom", None, None),
            P("section", "dom", None, None, None),
        ),
        out_specs=P("dom", "section"),
        check_vma=False,
    )
```

```python
import functools
import math

import jax
import jax.numpy as jnp
from jax import lax
from jax.experimental import pallas as pl
from jax.experimental.pallas import tpu as pltpu
from jax.sharding import PartitionSpec as P

alpha_mix = 0.1
lambda_decay = 0.5
vmem_bytes = 48 * 1024 * 1024


def group_streams(groups):
    return [list(range(groups - 1)), [groups - 1]]


def params():
    return pltpu.CompilerParams(vmem_limit_bytes=vmem_bytes)


def in_hbm(shape):
    return pltpu.HBM(shape, jnp.bfloat16)


hbm = pl.BlockSpec(memory_space=pltpu.HBM)
anywhere = pl.BlockSpec(memory_space=pl.ANY)


def pinned(value):
    return pltpu.with_memory_space_constraint(value, pltpu.HBM)


def start_all(copies):
    for condition, copy in copies:
        if condition is None:
            copy.start()
        else:
            pl.when(condition)(copy.start)


def wait_all(copies):
    for condition, copy in copies:
        if condition is None:
            copy.wait()
        else:
            pl.when(condition)(copy.wait)


def whole(shape):
    return pl.BlockSpec(shape, lambda i, *prefetched: (0,) * len(shape))


def pick_outgoing(picks, blocks_ref, outgoing_ref, stream, group_blocks, part_count):
    for local, group in enumerate(stream):

        def pick(dest, carry):
            chosen = jnp.maximum(picks[group * part_count + dest], 0)
            outgoing_ref[dest, local] = blocks_ref[local * group_blocks + chosen]
            return carry

        lax.fori_loop(0, part_count, pick, 0)


def prologue_kernel(streams, group_blocks, part_count, info, picks, rows_ref, unused, *refs):
    own_refs = refs[: len(streams)]
    outgoing_refs = refs[len(streams) : 2 * len(streams)]
    turned = refs[-1]
    block = own_refs[0].shape[2]
    part_width = own_refs[0].shape[1]
    first = pl.multiple_of(info[0] * part_width, part_width)
    for stream, own_ref, outgoing_ref in zip(streams, own_refs, outgoing_refs):
        for local in range(len(stream) * group_blocks):
            row = (stream[0] * group_blocks + local) * block
            turned[local % 2] = rows_ref[row : row + block, :].T
            own_ref[local] = turned[local % 2, pl.ds(first, part_width), :]
        pick_outgoing(picks, own_ref, outgoing_ref, stream, group_blocks, part_count)


def prologue(initial_features, section, picks, after, streams, group_blocks, block, part_width, part_count):
    rows, width = initial_features.shape
    own_shapes = [(len(s) * group_blocks, part_width, block) for s in streams]
    out_shapes = [(part_count, len(s), part_width, block) for s in streams]
    return pl.pallas_call(
        functools.partial(prologue_kernel, streams, group_blocks, part_count),
        grid_spec=pltpu.PrefetchScalarGridSpec(
            num_scalar_prefetch=2,
            grid=(1,),
            in_specs=[whole((rows, width)), hbm],
            out_specs=[whole(s) for s in own_shapes + out_shapes],
            scratch_shapes=[pltpu.VMEM((2, width, block), jnp.bfloat16)],
        ),
        out_shape=[in_hbm(s) for s in own_shapes]
        + [jax.ShapeDtypeStruct(s, jnp.bfloat16) for s in out_shapes],
        compiler_params=params(),
        name="prologue",
    )(section, picks, pinned(initial_features), pinned(after))


def turn_kernel(info, in_ref, *refs):
    *out_refs, turned = refs
    count = in_ref.shape[-3]
    sections, part_width = len(out_refs), out_refs[0].shape[1]
    for item in range(count):
        turned[item % 2] = in_ref[0, item].T if len(in_ref.shape) == 4 else in_ref[0, 0, item].T
        for distance, out_ref in enumerate(out_refs):
            owner = lax.rem(info[0] + distance, sections)
            first = pl.multiple_of(owner * part_width, part_width)
            out_ref[item] = turned[item % 2, pl.ds(first, part_width), :]


def turn_blocks(section, blocks, lead, sections):
    count, rows, width = blocks.shape[-3:]
    step = 8 if count % 8 == 0 else count
    part_width = width // sections
    block_shape = (1,) * (len(blocks.shape) - 3) + (step, rows, width)
    out_spec = pl.BlockSpec((step, part_width, rows), lambda i, *prefetched: (i, 0, 0))
    return pl.pallas_call(
        turn_kernel,
        grid_spec=pltpu.PrefetchScalarGridSpec(
            num_scalar_prefetch=1,
            grid=(count // step,),
            in_specs=[pl.BlockSpec(block_shape, lambda i, *prefetched: lead + (i, 0, 0))],
            out_specs=[out_spec] * sections,
            scratch_shapes=[pltpu.VMEM((2, width, rows), jnp.bfloat16)],
        ),
        out_shape=[in_hbm((count, part_width, rows))] * sections,
        compiler_params=params(),
        name="turn",
    )(section, pinned(blocks))


def aggregate_kernel(plan, columns, info, initial_ref, tiles_ref, *refs):
    stream, group_blocks, fanout, sources, home, sections = plan
    source_refs = refs[: len(sources)]
    mixed_ref, table, tiles, initial, table_sem, tiles_sem, initial_sem = refs[-7:]
    rows = len(stream) * group_blocks
    first_row = stream[0] * group_blocks

    def tile_copy(row):
        return pltpu.make_async_copy(tiles_ref.at[first_row + row], tiles.at[row], tiles_sem.at[row])

    initial_copy = pltpu.make_async_copy(initial_ref, initial, initial_sem)
    copies = []
    for index, (kind, target, detail) in enumerate(sources):
        ref = source_refs[index]
        source = ref.at[:, detail] if kind == "import" else ref
        condition = None
        if kind == "stale":
            condition = lax.rem(info[0] - home + 2 * sections, sections) == detail
        copies.append(
            (
                condition,
                pltpu.make_async_copy(
                    source, table.at[pl.ds(target, source.shape[0])], table_sem.at[index]
                ),
            )
        )
    start_all(copies)
    ahead = min(3, rows)
    for row in range(ahead):
        tile_copy(row).start()
    initial_copy.start()
    wait_all(copies)
    initial_copy.wait()

    def one_row(row, carry):
        tile_copy(row).wait()

        @pl.when(row + ahead < rows)
        def _():
            tile_copy(row + ahead).start()

        base = (first_row + row) * fanout
        total = None
        for tile in range(0, fanout, 2):
            span = range(tile, min(tile + 2, fanout))
            left = jnp.concatenate([table[columns[base + t]] for t in span], 1)
            right = jnp.concatenate([tiles[row, t] for t in span], 1)
            term = lax.dot_general(
                left, right, (((1,), (1,)), ((), ())), preferred_element_type=jnp.float32
            )
            total = term if total is None else total + term
        mixed_ref[row] = (
            (1.0 - alpha_mix) * total + alpha_mix * initial[row].astype(jnp.float32)
        ).astype(jnp.bfloat16)
        return carry

    lax.fori_loop(0, rows, one_row, 0)


def aggregate(columns, section, initial_blocks, tiles, own, imports, stale, home, stream, streams, group_blocks, part_count, after):
    rows, part_width, block = initial_blocks.shape
    blocks_dev, fanout = tiles.shape[:2]
    groups = blocks_dev // group_blocks
    sources, operands, specs = [], [], []
    for other, own_blocks, imported in zip(streams, own, imports):
        if other[0] > stream[-1]:
            continue
        sources.append(("own", other[0] * group_blocks, None))
        operands.append(pinned(own_blocks))
        specs.append(hbm)
        for local, group in enumerate(other):
            sources.append(("import", blocks_dev + group * part_count, local))
            operands.append(imported)
            specs.append(anywhere)
    if groups > 1 and stream[0] < groups - 1:
        for distance, stale_blocks in enumerate(stale):
            sources.append(("stale", blocks_dev + groups * part_count, distance))
            operands.append(pinned(stale_blocks))
            specs.append(hbm)
    operands += [pinned(value) for value in after]
    specs += [hbm] * len(after)
    table_size = blocks_dev + (2 * groups - 1) * part_count
    plan = (stream, group_blocks, fanout, sources, home, len(stale))
    flops = 2 * rows * fanout * block * block * part_width
    return pl.pallas_call(
        functools.partial(aggregate_kernel, plan),
        grid_spec=pltpu.PrefetchScalarGridSpec(
            num_scalar_prefetch=2,
            grid=(1,),
            in_specs=[hbm, hbm] + specs,
            out_specs=whole((rows, part_width, block)),
            scratch_shapes=[
                pltpu.VMEM((table_size, part_width, block), jnp.bfloat16),
                pltpu.VMEM((rows, fanout, block, block), jnp.bfloat16),
                pltpu.VMEM(initial_blocks.shape, jnp.bfloat16),
                pltpu.SemaphoreType.DMA((len(sources),)),
                pltpu.SemaphoreType.DMA((rows,)),
                pltpu.SemaphoreType.DMA,
            ],
        ),
        out_shape=jax.ShapeDtypeStruct((rows, part_width, block), jnp.bfloat16),
        cost_estimate=pl.CostEstimate(
            flops=flops, bytes_accessed=rows * fanout * block * block * 2, transcendentals=0
        ),
        compiler_params=params(),
        name="aggregate",
    )(columns, section, pinned(initial_blocks), pinned(tiles), *operands)


def finish_kernel(plan, picks, info, mixed_ref, gathered_ref, *refs):
    beta_layer, stream, group_blocks, part_count, sub, home, last = plan
    rows, part_width, block = mixed_ref.shape
    parts = gathered_ref.shape[0]
    weight_refs = refs[:parts]
    weight, weight_sem = refs[-2:]
    refs = refs[parts:-2]
    copies = [
        (
            lax.rem(info[0] - home + 2 * parts, parts) == distance,
            pltpu.make_async_copy(weight_ref.at[sub], weight, weight_sem.at[distance]),
        )
        for distance, weight_ref in enumerate(weight_refs)
    ]
    start_all(copies)
    wait_all(copies)
    for row in range(0, rows, 2):
        span = range(row, min(row + 2, rows))
        right = jnp.concatenate(
            [jnp.concatenate([gathered_ref[p, r] for p in range(parts)], 0) for r in span], 1
        )
        product = jnp.dot(weight[...], right, preferred_element_type=jnp.float32)
        for place, r in enumerate(span):
            value = (1.0 - beta_layer) * mixed_ref[r].astype(jnp.float32) + beta_layer * product[
                :, place * block : (place + 1) * block
            ]
            value = jnp.maximum(value, 0.0).astype(jnp.bfloat16)
            if last:
                refs[0][r * block : (r + 1) * block, :] = value.T
            else:
                refs[0][r] = value
    if not last:
        pick_outgoing(picks, refs[0], refs[1], stream, group_blocks, part_count)
        refs[2][...] = jnp.zeros_like(refs[2])


def finish(picks, section, mixed, gathered, weights, layer, depth, stream, group_blocks, part_count, last):
    rows, part_width, block = mixed.shape
    width = weights[0].shape[2]
    beta_layer = math.log(lambda_decay / (layer + 1) + 1.0)
    plan = (
        beta_layer, stream, group_blocks, part_count, layer % depth, layer // depth, last,
    )
    if last:
        shapes = [(rows * block, part_width)]
        out_shape = [jax.ShapeDtypeStruct(shapes[0], jnp.bfloat16)]
    else:
        outgoing = (part_count, len(stream), part_width, block)
        shapes = [(rows, part_width, block), outgoing, (16, 128)]
        out_shape = [
            in_hbm(shapes[0]),
            jax.ShapeDtypeStruct(outgoing, jnp.bfloat16),
            in_hbm((16, 128)),
        ]
    return pl.pallas_call(
        functools.partial(finish_kernel, plan),
        grid_spec=pltpu.PrefetchScalarGridSpec(
            num_scalar_prefetch=2,
            grid=(1,),
            in_specs=[whole(mixed.shape), whole(gathered.shape)]
            + [anywhere] * len(weights),
            out_specs=[whole(s) for s in shapes],
            scratch_shapes=[
                pltpu.VMEM((part_width, width), jnp.bfloat16),
                pltpu.SemaphoreType.DMA((len(weights),)),
            ],
        ),
        out_shape=out_shape,
        cost_estimate=pl.CostEstimate(
            flops=2 * rows * block * width * part_width,
            bytes_accessed=rows * block * width * 2,
            transcendentals=0,
        ),
        compiler_params=params(),
        name="finish",
    )(picks, section, mixed, gathered, *weights)


def per_device(
    initial_features, layer_weights, adjacency_tiles, tile_columns, send_blocks, stale_imports
):
    section_count = lax.axis_size("section")
    part_count = lax.axis_size("dom")
    blocks_dev, fanout, block = adjacency_tiles.shape[:3]
    width = initial_features.shape[1]
    part_width = width // section_count
    groups = send_blocks.shape[1]
    group_blocks = blocks_dev // groups
    depth = layer_weights.shape[0]
    layers = depth * section_count
    streams = group_streams(groups)
    section = lax.axis_index("section").astype(jnp.int32).reshape(1)
    picks = send_blocks.reshape(-1)

    row_group = (jnp.arange(blocks_dev, dtype=jnp.int32) // group_blocks)[:, None]
    slot_group = (tile_columns - blocks_dev) // part_count
    is_stale = (tile_columns >= blocks_dev) & (slot_group > row_group)
    columns = jnp.where(
        is_stale, tile_columns + (groups - 1) * part_count, tile_columns
    ).reshape(-1)

    turned = [
        turn_blocks(section, stale_imports, (sub, 0), section_count) for sub in range(depth)
    ]
    started = prologue(
        initial_features, section, picks, turned[0][0], streams, group_blocks, block, part_width, part_count
    )
    own = started[: len(streams)]
    outgoing = started[len(streams) :]
    initial_blocks = own

    def exchange(value):
        return lax.all_to_all(value, "dom", split_axis=0, concat_axis=0, tiled=True)

    def spread(pieces):
        ring = range(section_count)
        return [pieces[0]] + [
            lax.ppermute(
                pieces[distance], "section", [(s, (s + distance) % section_count) for s in ring]
            )
            for distance in range(1, section_count)
        ]

    imports = [exchange(value) for value in outgoing]
    stale = [spread(pieces) for pieces in turned]
    weights = spread(turn_blocks(section, layer_weights[None], (0,), section_count))

    pieces = []
    after = [pieces[0] for pieces in turned[1:]] + weights[1:]
    for layer in range(layers):
        last = layer == layers - 1
        own_next, imports_next = [], []
        for index, stream in enumerate(streams):
            mixed = aggregate(
                columns,
                section,
                initial_blocks[index],
                adjacency_tiles,
                own,
                imports,
                stale[layer % depth],
                layer // depth,
                stream,
                streams,
                group_blocks,
                part_count,
                after,
            )
            if last:
                after = [mixed[0]]
            gathered = lax.all_gather(mixed, "section", axis=0, tiled=False)
            result = finish(
                picks, section, mixed, gathered, weights, layer, depth, stream, group_blocks,
                part_count, last,
            )
            if last:
                pieces.append(result[0])
            else:
                after = [result[2]]
                own_next.append(result[0])
                imports_next.append(exchange(result[1]))
        own, imports = own_next, imports_next
    return jnp.concatenate(pieces, 0) if len(pieces) > 1 else pieces[0]


def solution(mesh):
    return jax.shard_map(
        per_device,
        mesh=mesh,
        in_specs=(
            P("dom", None),
            P("section", None, None),
            P("dom", None, None, None),
            P("dom", None),
            P("dom", None, None),
            P("section", "dom", None, None, None),
        ),
        out_specs=P("dom", "section"),
        check_vma=False,
    )
```

```python
import functools
import math

import jax
import jax.numpy as jnp
from jax import lax
from jax.experimental import pallas as pl
from jax.experimental.pallas import tpu as pltpu
from jax.sharding import PartitionSpec as P

alpha_mix = 0.1
lambda_decay = 0.5
vmem_bytes = 48 * 1024 * 1024


def group_streams(groups):
    return [list(range(groups - 1)), [groups - 1]]


def params():
    return pltpu.CompilerParams(vmem_limit_bytes=vmem_bytes)


def in_hbm(shape):
    return pltpu.HBM(shape, jnp.bfloat16)


hbm = pl.BlockSpec(memory_space=pltpu.HBM)
anywhere = pl.BlockSpec(memory_space=pl.ANY)


def pinned(value):
    return pltpu.with_memory_space_constraint(value, pltpu.HBM)


def start_all(copies):
    for condition, copy in copies:
        if condition is None:
            copy.start()
        else:
            pl.when(condition)(copy.start)


def wait_all(copies):
    for condition, copy in copies:
        if condition is None:
            copy.wait()
        else:
            pl.when(condition)(copy.wait)


def whole(shape):
    return pl.BlockSpec(shape, lambda i, *prefetched: (0,) * len(shape))


def pick_outgoing(picks, blocks_ref, outgoing_ref, stream, group_blocks, part_count):
    for local, group in enumerate(stream):

        def pick(dest, carry):
            chosen = jnp.maximum(picks[group * part_count + dest], 0)
            outgoing_ref[dest, local] = blocks_ref[local * group_blocks + chosen]
            return carry

        lax.fori_loop(0, part_count, pick, 0)


def prologue_kernel(streams, group_blocks, part_count, info, picks, rows_ref, unused, *refs):
    own_refs = refs[: len(streams)]
    outgoing_refs = refs[len(streams) : 2 * len(streams)]
    turned = refs[-1]
    block = own_refs[0].shape[2]
    part_width = own_refs[0].shape[1]
    first = pl.multiple_of(info[0] * part_width, part_width)
    for stream, own_ref, outgoing_ref in zip(streams, own_refs, outgoing_refs):
        for local in range(len(stream) * group_blocks):
            row = (stream[0] * group_blocks + local) * block
            turned[local % 2] = rows_ref[row : row + block, :].T
            own_ref[local] = turned[local % 2, pl.ds(first, part_width), :]
        pick_outgoing(picks, own_ref, outgoing_ref, stream, group_blocks, part_count)


def prologue(initial_features, section, picks, after, streams, group_blocks, block, part_width, part_count):
    rows, width = initial_features.shape
    own_shapes = [(len(s) * group_blocks, part_width, block) for s in streams]
    out_shapes = [(part_count, len(s), part_width, block) for s in streams]
    return pl.pallas_call(
        functools.partial(prologue_kernel, streams, group_blocks, part_count),
        grid_spec=pltpu.PrefetchScalarGridSpec(
            num_scalar_prefetch=2,
            grid=(1,),
            in_specs=[whole((rows, width)), hbm],
            out_specs=[whole(s) for s in own_shapes + out_shapes],
            scratch_shapes=[pltpu.VMEM((2, width, block), jnp.bfloat16)],
        ),
        out_shape=[in_hbm(s) for s in own_shapes]
        + [jax.ShapeDtypeStruct(s, jnp.bfloat16) for s in out_shapes],
        compiler_params=params(),
        name="prologue",
    )(section, picks, pinned(initial_features), pinned(after))


def turn_kernel(info, in_ref, *refs):
    *out_refs, turned = refs
    count = in_ref.shape[-3]
    sections, part_width = len(out_refs), out_refs[0].shape[1]
    for item in range(count):
        turned[item % 2] = in_ref[0, item].T if len(in_ref.shape) == 4 else in_ref[0, 0, item].T
        for distance, out_ref in enumerate(out_refs):
            owner = lax.rem(info[0] + distance, sections)
            first = pl.multiple_of(owner * part_width, part_width)
            out_ref[item] = turned[item % 2, pl.ds(first, part_width), :]


def turn_blocks(section, blocks, lead, sections):
    count, rows, width = blocks.shape[-3:]
    step = 8 if count % 8 == 0 else count
    part_width = width // sections
    block_shape = (1,) * (len(blocks.shape) - 3) + (step, rows, width)
    out_spec = pl.BlockSpec((step, part_width, rows), lambda i, *prefetched: (i, 0, 0))
    return pl.pallas_call(
        turn_kernel,
        grid_spec=pltpu.PrefetchScalarGridSpec(
            num_scalar_prefetch=1,
            grid=(count // step,),
            in_specs=[pl.BlockSpec(block_shape, lambda i, *prefetched: lead + (i, 0, 0))],
            out_specs=[out_spec] * sections,
            scratch_shapes=[pltpu.VMEM((2, width, rows), jnp.bfloat16)],
        ),
        out_shape=[in_hbm((count, part_width, rows))] * sections,
        compiler_params=params(),
        name="turn",
    )(section, pinned(blocks))


class Aggregate:
    def __init__(self, plan, columns, info, initial_ref, tiles_ref, source_refs, mixed_ref, scratch):
        self.stream, self.group_blocks, self.fanout, sources, home, sections = plan
        self.columns, self.tiles_ref, self.mixed_ref = columns, tiles_ref, mixed_ref
        self.table, self.tiles, self.initial, table_sem, self.tiles_sem, initial_sem = scratch
        self.rows = len(self.stream) * self.group_blocks
        self.first_row = self.stream[0] * self.group_blocks
        self.ahead = min(3, self.rows)
        self.initial_copy = pltpu.make_async_copy(initial_ref, self.initial, initial_sem)
        self.copies = []
        for index, (kind, target, detail) in enumerate(sources):
            ref = source_refs[index]
            source = ref.at[:, detail] if kind == "import" else ref
            condition = None
            if kind == "stale":
                condition = lax.rem(info[0] - home + 2 * sections, sections) == detail
            part = self.table.at[pl.ds(target, source.shape[0])]
            copy = pltpu.make_async_copy(source, part, table_sem.at[index])
            self.copies.append((condition, copy))

    def tile_copy(self, row):
        return pltpu.make_async_copy(
            self.tiles_ref.at[self.first_row + row], self.tiles.at[row], self.tiles_sem.at[row]
        )

    def begin(self):
        start_all(self.copies)
        for row in range(self.ahead):
            self.tile_copy(row).start()
        self.initial_copy.start()

    def run(self):
        wait_all(self.copies)
        self.initial_copy.wait()

        def one_row(row, carry):
            self.tile_copy(row).wait()

            @pl.when(row + self.ahead < self.rows)
            def _():
                self.tile_copy(row + self.ahead).start()

            base = (self.first_row + row) * self.fanout
            total = None
            for tile in range(0, self.fanout, 2):
                span = range(tile, min(tile + 2, self.fanout))
                left = jnp.concatenate([self.table[self.columns[base + t]] for t in span], 1)
                right = jnp.concatenate([self.tiles[row, t] for t in span], 1)
                term = lax.dot_general(
                    left, right, (((1,), (1,)), ((), ())), preferred_element_type=jnp.float32
                )
                total = term if total is None else total + term
            start = self.initial[row].astype(jnp.float32)
            self.mixed_ref[row] = ((1.0 - alpha_mix) * total + alpha_mix * start).astype(
                jnp.bfloat16
            )
            return carry

        lax.fori_loop(0, self.rows, one_row, 0)


def aggregate_kernel(plan, columns, info, initial_ref, tiles_ref, *refs):
    count = len(plan[3])
    work = Aggregate(plan, columns, info, initial_ref, tiles_ref, refs[:count], refs[-7], refs[-6:])
    work.begin()
    work.run()


def both_kernel(finish_plan, aggregate_plan, columns, picks, info, mixed_ref, gathered_ref, *refs):
    parts = gathered_ref.shape[0]
    count = len(aggregate_plan[3])
    weight_refs, refs = refs[:parts], refs[parts:]
    initial_ref, tiles_ref = refs[:2]
    source_refs, refs = refs[2 : 2 + count], refs[2 + count :]
    own_ref, outgoing_ref, next_ref = refs[:3]
    weight, weight_sem = refs[3:5]
    work = Aggregate(
        aggregate_plan, columns, info, initial_ref, tiles_ref, source_refs, next_ref, refs[5:]
    )
    work.begin()
    finish_body(
        finish_plan, picks, info, mixed_ref, gathered_ref, weight_refs, [own_ref, outgoing_ref],
        weight, weight_sem,
    )
    work.run()


def aggregate_parts(section, initial_blocks, tiles, own, imports, stale, home, stream, streams, group_blocks, part_count):
    rows, part_width, block = initial_blocks.shape
    blocks_dev, fanout = tiles.shape[:2]
    groups = blocks_dev // group_blocks
    sources, operands, specs = [], [], []
    for other, own_blocks, imported in zip(streams, own, imports):
        if other[0] > stream[-1]:
            continue
        sources.append(("own", other[0] * group_blocks, None))
        operands.append(pinned(own_blocks))
        specs.append(hbm)
        for local, group in enumerate(other):
            sources.append(("import", blocks_dev + group * part_count, local))
            operands.append(imported)
            specs.append(anywhere)
    if groups > 1 and stream[0] < groups - 1:
        for distance, stale_blocks in enumerate(stale):
            sources.append(("stale", blocks_dev + groups * part_count, distance))
            operands.append(pinned(stale_blocks))
            specs.append(hbm)
    table_size = blocks_dev + (2 * groups - 1) * part_count
    plan = (stream, group_blocks, fanout, sources, home, len(stale))
    scratch = [
        pltpu.VMEM((table_size, part_width, block), jnp.bfloat16),
        pltpu.VMEM((rows, fanout, block, block), jnp.bfloat16),
        pltpu.VMEM(initial_blocks.shape, jnp.bfloat16),
        pltpu.SemaphoreType.DMA((len(sources),)),
        pltpu.SemaphoreType.DMA((rows,)),
        pltpu.SemaphoreType.DMA,
    ]
    operands = [pinned(initial_blocks), pinned(tiles)] + operands
    return plan, operands, [hbm, hbm] + specs, scratch


def estimate(rows, fanout, block, part_width, width):
    return pl.CostEstimate(
        flops=2 * rows * block * part_width * (fanout * block + width),
        bytes_accessed=rows * fanout * block * block * 2,
        transcendentals=0,
    )


def aggregate(columns, section, parts, shape, after):
    plan, operands, specs, scratch = parts
    operands = operands + [pinned(value) for value in after]
    return pl.pallas_call(
        functools.partial(aggregate_kernel, plan),
        grid_spec=pltpu.PrefetchScalarGridSpec(
            num_scalar_prefetch=2,
            grid=(1,),
            in_specs=specs + [hbm] * len(after),
            out_specs=whole(shape),
            scratch_shapes=scratch,
        ),
        out_shape=jax.ShapeDtypeStruct(shape, jnp.bfloat16),
        cost_estimate=estimate(shape[0], plan[2], shape[2], shape[1], 0),
        compiler_params=params(),
        name="aggregate",
    )(columns, section, *operands)


def finish_and_aggregate(columns, picks, section, mixed, gathered, weights, layer, depth, stream, group_blocks, part_count, parts, shape):
    aggregate_plan, operands, specs, scratch = parts
    rows, part_width, block = mixed.shape
    width = weights[0].shape[2]
    beta_layer = math.log(lambda_decay / (layer + 1) + 1.0)
    plan = (beta_layer, stream, group_blocks, part_count, layer % depth, layer // depth, False)
    outgoing = (part_count, len(stream), part_width, block)
    return pl.pallas_call(
        functools.partial(both_kernel, plan, aggregate_plan),
        grid_spec=pltpu.PrefetchScalarGridSpec(
            num_scalar_prefetch=3,
            grid=(1,),
            in_specs=[whole(mixed.shape), whole(gathered.shape)] + [anywhere] * len(weights) + specs,
            out_specs=[whole(mixed.shape), whole(outgoing), whole(shape)],
            scratch_shapes=[
                pltpu.VMEM((part_width, width), jnp.bfloat16),
                pltpu.SemaphoreType.DMA((len(weights),)),
            ]
            + scratch,
        ),
        out_shape=[
            in_hbm(mixed.shape),
            jax.ShapeDtypeStruct(outgoing, jnp.bfloat16),
            jax.ShapeDtypeStruct(shape, jnp.bfloat16),
        ],
        cost_estimate=estimate(shape[0], aggregate_plan[2], block, part_width, width),
        compiler_params=params(),
        name="finish_aggregate",
    )(columns, picks, section, mixed, gathered, *weights, *operands)


def finish_kernel(plan, picks, info, mixed_ref, gathered_ref, *refs):
    parts = gathered_ref.shape[0]
    out_refs = refs[parts:-2]
    finish_body(
        plan, picks, info, mixed_ref, gathered_ref, refs[:parts], out_refs, refs[-2], refs[-1]
    )
    if len(out_refs) > 2:
        out_refs[2][...] = jnp.zeros_like(out_refs[2])


def finish_body(plan, picks, info, mixed_ref, gathered_ref, weight_refs, refs, weight, weight_sem):
    beta_layer, stream, group_blocks, part_count, sub, home, last = plan
    rows, part_width, block = mixed_ref.shape
    parts = gathered_ref.shape[0]
    copies = [
        (
            lax.rem(info[0] - home + 2 * parts, parts) == distance,
            pltpu.make_async_copy(weight_ref.at[sub], weight, weight_sem.at[distance]),
        )
        for distance, weight_ref in enumerate(weight_refs)
    ]
    start_all(copies)
    wait_all(copies)
    for row in range(0, rows, 2):
        span = range(row, min(row + 2, rows))
        right = jnp.concatenate(
            [jnp.concatenate([gathered_ref[p, r] for p in range(parts)], 0) for r in span], 1
        )
        product = jnp.dot(weight[...], right, preferred_element_type=jnp.float32)
        for place, r in enumerate(span):
            value = (1.0 - beta_layer) * mixed_ref[r].astype(jnp.float32) + beta_layer * product[
                :, place * block : (place + 1) * block
            ]
            value = jnp.maximum(value, 0.0).astype(jnp.bfloat16)
            if last:
                refs[0][r * block : (r + 1) * block, :] = value.T
            else:
                refs[0][r] = value
    if not last:
        pick_outgoing(picks, refs[0], refs[1], stream, group_blocks, part_count)


def finish(picks, section, mixed, gathered, weights, layer, depth, stream, group_blocks, part_count, last):
    rows, part_width, block = mixed.shape
    width = weights[0].shape[2]
    beta_layer = math.log(lambda_decay / (layer + 1) + 1.0)
    plan = (
        beta_layer, stream, group_blocks, part_count, layer % depth, layer // depth, last,
    )
    if last:
        shapes = [(rows * block, part_width)]
        out_shape = [jax.ShapeDtypeStruct(shapes[0], jnp.bfloat16)]
    else:
        outgoing = (part_count, len(stream), part_width, block)
        shapes = [(rows, part_width, block), outgoing, (16, 128)]
        out_shape = [
            in_hbm(shapes[0]),
            jax.ShapeDtypeStruct(outgoing, jnp.bfloat16),
            in_hbm((16, 128)),
        ]
    return pl.pallas_call(
        functools.partial(finish_kernel, plan),
        grid_spec=pltpu.PrefetchScalarGridSpec(
            num_scalar_prefetch=2,
            grid=(1,),
            in_specs=[whole(mixed.shape), whole(gathered.shape)]
            + [anywhere] * len(weights),
            out_specs=[whole(s) for s in shapes],
            scratch_shapes=[
                pltpu.VMEM((part_width, width), jnp.bfloat16),
                pltpu.SemaphoreType.DMA((len(weights),)),
            ],
        ),
        out_shape=out_shape,
        cost_estimate=pl.CostEstimate(
            flops=2 * rows * block * width * part_width,
            bytes_accessed=rows * block * width * 2,
            transcendentals=0,
        ),
        compiler_params=params(),
        name="finish",
    )(picks, section, mixed, gathered, *weights)


def per_device(
    initial_features, layer_weights, adjacency_tiles, tile_columns, send_blocks, stale_imports
):
    section_count = lax.axis_size("section")
    part_count = lax.axis_size("dom")
    blocks_dev, fanout, block = adjacency_tiles.shape[:3]
    width = initial_features.shape[1]
    part_width = width // section_count
    groups = send_blocks.shape[1]
    group_blocks = blocks_dev // groups
    depth = layer_weights.shape[0]
    layers = depth * section_count
    streams = group_streams(groups)
    section = lax.axis_index("section").astype(jnp.int32).reshape(1)
    picks = send_blocks.reshape(-1)

    row_group = (jnp.arange(blocks_dev, dtype=jnp.int32) // group_blocks)[:, None]
    slot_group = (tile_columns - blocks_dev) // part_count
    is_stale = (tile_columns >= blocks_dev) & (slot_group > row_group)
    columns = jnp.where(
        is_stale, tile_columns + (groups - 1) * part_count, tile_columns
    ).reshape(-1)

    turned = [
        turn_blocks(section, stale_imports, (sub, 0), section_count) for sub in range(depth)
    ]
    started = prologue(
        initial_features, section, picks, turned[0][0], streams, group_blocks, block, part_width, part_count
    )
    own = started[: len(streams)]
    outgoing = started[len(streams) :]
    initial_blocks = own

    def exchange(value):
        return lax.all_to_all(value, "dom", split_axis=0, concat_axis=0, tiled=True)

    def spread(pieces):
        ring = range(section_count)
        return [pieces[0]] + [
            lax.ppermute(
                pieces[distance], "section", [(s, (s + distance) % section_count) for s in ring]
            )
            for distance in range(1, section_count)
        ]

    imports = [exchange(value) for value in outgoing]
    stale = [spread(pieces) for pieces in turned]
    weights = spread(turn_blocks(section, layer_weights[None], (0,), section_count))

    front, back = streams
    turned_late = [pieces[0] for pieces in turned[1:]]

    def parts_of(index, layer):
        return aggregate_parts(
            section, initial_blocks[index], adjacency_tiles, own, imports, stale[layer % depth],
            layer // depth, streams[index], streams, group_blocks, part_count,
        )

    own, imports = list(own), list(imports)
    shapes = [value.shape for value in initial_blocks]
    mixed_front = aggregate(columns, section, parts_of(0, 0), shapes[0], turned_late)
    for layer in range(layers):
        last = layer == layers - 1
        gathered = lax.all_gather(mixed_front, "section", axis=0, tiled=False)
        front_result = finish(
            picks, section, mixed_front, gathered, weights, layer, depth, front, group_blocks,
            part_count, last,
        )
        after = [mixed_front[0]] if last else [front_result[2]]
        mixed_back = aggregate(columns, section, parts_of(1, layer), shapes[1], after)
        gathered = lax.all_gather(mixed_back, "section", axis=0, tiled=False)
        if last:
            back_result = finish(
                picks, section, mixed_back, gathered, weights, layer, depth, back, group_blocks,
                part_count, last,
            )
            return jnp.concatenate([front_result[0], back_result[0]], 0)
        own[0], imports[0] = front_result[0], exchange(front_result[1])
        own[1], outgoing, mixed_front = finish_and_aggregate(
            columns, picks, section, mixed_back, gathered, weights, layer, depth, back,
            group_blocks, part_count, parts_of(0, layer + 1), shapes[0],
        )
        imports[1] = exchange(outgoing)


def solution(mesh):
    return jax.shard_map(
        per_device,
        mesh=mesh,
        in_specs=(
            P("dom", None),
            P("section", None, None),
            P("dom", None, None, None),
            P("dom", None),
            P("dom", None, None),
            P("section", "dom", None, None, None),
        ),
        out_specs=P("dom", "section"),
        check_vma=False,
    )
```

```python
import functools
import math

import jax
import jax.numpy as jnp
from jax import lax
from jax.experimental import pallas as pl
from jax.experimental.pallas import tpu as pltpu
from jax.sharding import PartitionSpec as P

alpha_mix = 0.1
lambda_decay = 0.5
vmem_bytes = 48 * 1024 * 1024


def group_streams(groups):
    return [list(range(groups - 1)), [groups - 1]]


def params():
    return pltpu.CompilerParams(vmem_limit_bytes=vmem_bytes)


def in_hbm(shape):
    return pltpu.HBM(shape, jnp.bfloat16)


hbm = pl.BlockSpec(memory_space=pltpu.HBM)
anywhere = pl.BlockSpec(memory_space=pl.ANY)


def pinned(value):
    return pltpu.with_memory_space_constraint(value, pltpu.HBM)


def start_all(copies):
    for condition, copy in copies:
        if condition is None:
            copy.start()
        else:
            pl.when(condition)(copy.start)


def wait_all(copies):
    for condition, copy in copies:
        if condition is None:
            copy.wait()
        else:
            pl.when(condition)(copy.wait)


def whole(shape):
    return pl.BlockSpec(shape, lambda i, *prefetched: (0,) * len(shape))


def pick_outgoing(picks, blocks_ref, outgoing_ref, stream, group_blocks, part_count):
    for local, group in enumerate(stream):

        def pick(dest, carry):
            chosen = jnp.maximum(picks[group * part_count + dest], 0)
            outgoing_ref[dest, local] = blocks_ref[local * group_blocks + chosen]
            return carry

        lax.fori_loop(0, part_count, pick, 0)


def prologue_kernel(streams, group_blocks, part_count, info, picks, rows_ref, unused, *refs):
    own_refs = refs[: len(streams)]
    outgoing_refs = refs[len(streams) : 2 * len(streams)]
    turned = refs[-1]
    block = own_refs[0].shape[2]
    part_width = own_refs[0].shape[1]
    first = pl.multiple_of(info[0] * part_width, part_width)
    for stream, own_ref, outgoing_ref in zip(streams, own_refs, outgoing_refs):
        for local in range(len(stream) * group_blocks):
            row = (stream[0] * group_blocks + local) * block
            turned[local % 2] = rows_ref[row : row + block, :].T
            own_ref[local] = turned[local % 2, pl.ds(first, part_width), :]
        pick_outgoing(picks, own_ref, outgoing_ref, stream, group_blocks, part_count)


def prologue(initial_features, section, picks, after, streams, group_blocks, block, part_width, part_count):
    rows, width = initial_features.shape
    own_shapes = [(len(s) * group_blocks, part_width, block) for s in streams]
    out_shapes = [(part_count, len(s), part_width, block) for s in streams]
    return pl.pallas_call(
        functools.partial(prologue_kernel, streams, group_blocks, part_count),
        grid_spec=pltpu.PrefetchScalarGridSpec(
            num_scalar_prefetch=2,
            grid=(1,),
            in_specs=[whole((rows, width)), hbm],
            out_specs=[whole(s) for s in own_shapes + out_shapes],
            scratch_shapes=[pltpu.VMEM((2, width, block), jnp.bfloat16)],
        ),
        out_shape=[in_hbm(s) for s in own_shapes]
        + [jax.ShapeDtypeStruct(s, jnp.bfloat16) for s in out_shapes],
        compiler_params=params(),
        name="prologue",
    )(section, picks, pinned(initial_features), pinned(after))


def turn_kernel(info, in_ref, *refs):
    *out_refs, turned = refs
    count = in_ref.shape[-3]
    sections, part_width = len(out_refs), out_refs[0].shape[1]
    for item in range(count):
        turned[item % 2] = in_ref[0, item].T if len(in_ref.shape) == 4 else in_ref[0, 0, item].T
        for distance, out_ref in enumerate(out_refs):
            owner = lax.rem(info[0] + distance, sections)
            first = pl.multiple_of(owner * part_width, part_width)
            out_ref[item] = turned[item % 2, pl.ds(first, part_width), :]


def turn_blocks(section, blocks, lead, sections):
    count, rows, width = blocks.shape[-3:]
    step = 8 if count % 8 == 0 else count
    part_width = width // sections
    block_shape = (1,) * (len(blocks.shape) - 3) + (step, rows, width)
    out_spec = pl.BlockSpec((step, part_width, rows), lambda i, *prefetched: (i, 0, 0))
    return pl.pallas_call(
        turn_kernel,
        grid_spec=pltpu.PrefetchScalarGridSpec(
            num_scalar_prefetch=1,
            grid=(count // step,),
            in_specs=[pl.BlockSpec(block_shape, lambda i, *prefetched: lead + (i, 0, 0))],
            out_specs=[out_spec] * sections,
            scratch_shapes=[pltpu.VMEM((2, width, rows), jnp.bfloat16)],
        ),
        out_shape=[in_hbm((count, part_width, rows))] * sections,
        compiler_params=params(),
        name="turn",
    )(section, pinned(blocks))


class Aggregate:
    def __init__(self, plan, columns, info, initial_ref, tiles_ref, source_refs, mixed_ref, scratch):
        self.stream, self.group_blocks, self.fanout, sources, home, sections = plan
        self.columns, self.tiles_ref, self.mixed_ref = columns, tiles_ref, mixed_ref
        self.table, self.tiles, self.initial, table_sem, self.tiles_sem, initial_sem = scratch
        self.rows = len(self.stream) * self.group_blocks
        self.first_row = self.stream[0] * self.group_blocks
        self.ahead = min(3, self.rows)
        self.initial_copy = pltpu.make_async_copy(initial_ref, self.initial, initial_sem)
        self.copies = []
        for index, (kind, target, detail) in enumerate(sources):
            ref = source_refs[index]
            source = ref.at[:, detail] if kind == "import" else ref
            condition = None
            if kind == "stale":
                condition = lax.rem(info[0] - home + 2 * sections, sections) == detail
            part = self.table.at[pl.ds(target, source.shape[0])]
            copy = pltpu.make_async_copy(source, part, table_sem.at[index])
            self.copies.append((condition, copy))

    def tile_copy(self, row):
        return pltpu.make_async_copy(
            self.tiles_ref.at[self.first_row + row], self.tiles.at[row], self.tiles_sem.at[row]
        )

    def begin(self):
        start_all(self.copies)
        for row in range(self.ahead):
            self.tile_copy(row).start()
        self.initial_copy.start()

    def run(self):
        wait_all(self.copies)
        self.initial_copy.wait()

        def one_row(row, carry):
            self.tile_copy(row).wait()

            @pl.when(row + self.ahead < self.rows)
            def _():
                self.tile_copy(row + self.ahead).start()

            base = (self.first_row + row) * self.fanout
            total = None
            for tile in range(0, self.fanout, 2):
                span = range(tile, min(tile + 2, self.fanout))
                left = jnp.concatenate([self.table[self.columns[base + t]] for t in span], 1)
                right = jnp.concatenate([self.tiles[row, t] for t in span], 1)
                term = lax.dot_general(
                    left, right, (((1,), (1,)), ((), ())), preferred_element_type=jnp.float32
                )
                total = term if total is None else total + term
            start = self.initial[row].astype(jnp.float32)
            self.mixed_ref[row] = ((1.0 - alpha_mix) * total + alpha_mix * start).astype(
                jnp.bfloat16
            )
            return carry

        lax.fori_loop(0, self.rows, one_row, 0)


def aggregate_kernel(plan, columns, info, initial_ref, tiles_ref, *refs):
    count = len(plan[3])
    work = Aggregate(plan, columns, info, initial_ref, tiles_ref, refs[:count], refs[-7], refs[-6:])
    work.begin()
    work.run()


def both_kernel(plan, aggregate_plan, columns, picks, info, mixed_ref, gathered_ref, *refs):
    parts = gathered_ref.shape[0]
    count = len(aggregate_plan[3])
    weight_refs, refs = refs[:parts], refs[parts:]
    initial_ref, tiles_ref = refs[:2]
    source_refs, refs = refs[2 : 2 + count], refs[2 + count :]
    own_ref, outgoing_ref, next_ref = refs[:3]
    scratch = refs[3:7]
    work = Aggregate(
        aggregate_plan, columns, info, initial_ref, tiles_ref, source_refs, next_ref, refs[7:]
    )
    copies = finish_begin(plan, info, mixed_ref, gathered_ref, weight_refs, scratch)
    work.begin()
    finish_run(plan, copies, picks, [own_ref, outgoing_ref], scratch)
    work.run()


def aggregate_parts(section, initial_blocks, tiles, own, imports, stale, home, stream, streams, group_blocks, part_count):
    rows, part_width, block = initial_blocks.shape
    blocks_dev, fanout = tiles.shape[:2]
    groups = blocks_dev // group_blocks
    sources, operands, specs = [], [], []
    for other, own_blocks, imported in zip(streams, own, imports):
        if other[0] > stream[-1]:
            continue
        sources.append(("own", other[0] * group_blocks, None))
        operands.append(pinned(own_blocks))
        specs.append(hbm)
        for local, group in enumerate(other):
            sources.append(("import", blocks_dev + group * part_count, local))
            operands.append(imported)
            specs.append(anywhere)
    if groups > 1 and stream[0] < groups - 1:
        for distance, stale_blocks in enumerate(stale):
            sources.append(("stale", blocks_dev + groups * part_count, distance))
            operands.append(pinned(stale_blocks))
            specs.append(hbm)
    table_size = blocks_dev + (2 * groups - 1) * part_count
    plan = (stream, group_blocks, fanout, sources, home, len(stale))
    scratch = [
        pltpu.VMEM((table_size, part_width, block), jnp.bfloat16),
        pltpu.VMEM((rows, fanout, block, block), jnp.bfloat16),
        pltpu.VMEM(initial_blocks.shape, jnp.bfloat16),
        pltpu.SemaphoreType.DMA((len(sources),)),
        pltpu.SemaphoreType.DMA((rows,)),
        pltpu.SemaphoreType.DMA,
    ]
    operands = [pinned(initial_blocks), pinned(tiles)] + operands
    return plan, operands, [hbm, hbm] + specs, scratch


def estimate(rows, fanout, block, part_width, width):
    return pl.CostEstimate(
        flops=2 * rows * block * part_width * (fanout * block + width),
        bytes_accessed=rows * fanout * block * block * 2,
        transcendentals=0,
    )


def aggregate(columns, section, parts, shape, after):
    plan, operands, specs, scratch = parts
    operands = operands + [pinned(value) for value in after]
    return pl.pallas_call(
        functools.partial(aggregate_kernel, plan),
        grid_spec=pltpu.PrefetchScalarGridSpec(
            num_scalar_prefetch=2,
            grid=(1,),
            in_specs=specs + [hbm] * len(after),
            out_specs=whole(shape),
            scratch_shapes=scratch,
        ),
        out_shape=jax.ShapeDtypeStruct(shape, jnp.bfloat16),
        cost_estimate=estimate(shape[0], plan[2], shape[2], shape[1], 0),
        compiler_params=params(),
        name="aggregate",
    )(columns, section, *operands)


def finish_and_aggregate(columns, picks, section, mixed, gathered, weights, layer, depth, stream, group_blocks, part_count, parts, shape):
    aggregate_plan, operands, specs, scratch = parts
    rows, part_width, block = mixed.shape
    width = weights[0].shape[2]
    plan = finish_plan(layer, depth, stream, group_blocks, part_count, False)
    outgoing = (part_count, len(stream), part_width, block)
    return pl.pallas_call(
        functools.partial(both_kernel, plan, aggregate_plan),
        grid_spec=pltpu.PrefetchScalarGridSpec(
            num_scalar_prefetch=3,
            grid=(1,),
            in_specs=[anywhere] * (2 + len(weights)) + specs,
            out_specs=[whole(mixed.shape), whole(outgoing), whole(shape)],
            scratch_shapes=finish_scratch(mixed, gathered, weights) + scratch,
        ),
        out_shape=[
            in_hbm(mixed.shape),
            jax.ShapeDtypeStruct(outgoing, jnp.bfloat16),
            jax.ShapeDtypeStruct(shape, jnp.bfloat16),
        ],
        cost_estimate=estimate(shape[0], aggregate_plan[2], block, part_width, width),
        compiler_params=params(),
        name="finish_aggregate",
    )(columns, picks, section, mixed, gathered, *weights, *operands)


def finish_begin(plan, info, mixed_ref, gathered_ref, weight_refs, scratch):
    parts = len(weight_refs)
    sub, home = plan[4:6]
    mixed, gathered, weight, sem = scratch
    copies = [
        (
            lax.rem(info[0] - home + 2 * parts, parts) == distance,
            pltpu.make_async_copy(weight_ref.at[sub], weight, sem.at[distance]),
        )
        for distance, weight_ref in enumerate(weight_refs)
    ]
    copies.append((None, pltpu.make_async_copy(gathered_ref, gathered, sem.at[parts])))
    copies.append((None, pltpu.make_async_copy(mixed_ref, mixed, sem.at[parts + 1])))
    start_all(copies)
    return copies


def finish_run(plan, copies, picks, refs, scratch):
    beta_layer, stream, group_blocks, part_count, sub, home, last = plan
    mixed_ref, gathered_ref, weight, sem = scratch
    rows, part_width, block = mixed_ref.shape
    parts = gathered_ref.shape[0]
    wait_all(copies)
    for row in range(0, rows, 2):
        span = range(row, min(row + 2, rows))
        right = jnp.concatenate(
            [jnp.concatenate([gathered_ref[p, r] for p in range(parts)], 0) for r in span], 1
        )
        product = jnp.dot(weight[...], right, preferred_element_type=jnp.float32)
        for place, r in enumerate(span):
            value = (1.0 - beta_layer) * mixed_ref[r].astype(jnp.float32) + beta_layer * product[
                :, place * block : (place + 1) * block
            ]
            value = jnp.maximum(value, 0.0).astype(jnp.bfloat16)
            if last:
                low = (stream[0] * group_blocks + r) * block
                refs[0][low : low + block, :] = value.T
            else:
                refs[0][r] = value
    if not last:
        pick_outgoing(picks, refs[0], refs[1], stream, group_blocks, part_count)


def finish_kernel(plan, picks, info, mixed_ref, gathered_ref, *refs):
    parts = gathered_ref.shape[0]
    weight_refs, out_refs, scratch = refs[:parts], refs[parts:-4], refs[-4:]
    copies = finish_begin(plan, info, mixed_ref, gathered_ref, weight_refs, scratch)
    finish_run(plan, copies, picks, out_refs, scratch)
    out_refs[2][...] = jnp.zeros_like(out_refs[2])


def last_kernel(plans, picks, info, *refs):
    parts = refs[1].shape[0]
    weight_refs, out_ref = refs[4 : 4 + parts], refs[4 + parts]
    scratches = [refs[5 + parts : 9 + parts], refs[9 + parts :]]
    begun = [
        finish_begin(plan, info, refs[2 * i], refs[2 * i + 1], weight_refs, scratches[i])
        for i, plan in enumerate(plans)
    ]
    for plan, copies, scratch in zip(plans, begun, scratches):
        finish_run(plan, copies, picks, [out_ref], scratch)


def finish_plan(layer, depth, stream, group_blocks, part_count, last):
    beta_layer = math.log(lambda_decay / (layer + 1) + 1.0)
    return (beta_layer, stream, group_blocks, part_count, layer % depth, layer // depth, last)


def finish_scratch(mixed, gathered, weights):
    return [
        pltpu.VMEM(mixed.shape, jnp.bfloat16),
        pltpu.VMEM(gathered.shape, jnp.bfloat16),
        pltpu.VMEM(weights[0].shape[1:], jnp.bfloat16),
        pltpu.SemaphoreType.DMA((len(weights) + 2,)),
    ]


def finish_last(picks, section, pairs, weights, layer, depth, streams, group_blocks, part_count):
    plans = [finish_plan(layer, depth, s, group_blocks, part_count, True) for s in streams]
    rows = sum(mixed.shape[0] * mixed.shape[2] for mixed, gathered in pairs)
    shape = (rows, pairs[0][0].shape[1])
    return pl.pallas_call(
        functools.partial(last_kernel, plans),
        grid_spec=pltpu.PrefetchScalarGridSpec(
            num_scalar_prefetch=2,
            grid=(1,),
            in_specs=[anywhere] * (2 * len(pairs) + len(weights)),
            out_specs=whole(shape),
            scratch_shapes=sum([finish_scratch(*pair, weights) for pair in pairs], []),
        ),
        out_shape=jax.ShapeDtypeStruct(shape, jnp.bfloat16),
        compiler_params=params(),
        name="finish_last",
    )(picks, section, *[value for pair in pairs for value in pair], *weights)


def finish(picks, section, mixed, gathered, weights, layer, depth, stream, group_blocks, part_count):
    rows, part_width, block = mixed.shape
    width = weights[0].shape[2]
    plan = finish_plan(layer, depth, stream, group_blocks, part_count, False)
    outgoing = (part_count, len(stream), part_width, block)
    return pl.pallas_call(
        functools.partial(finish_kernel, plan),
        grid_spec=pltpu.PrefetchScalarGridSpec(
            num_scalar_prefetch=2,
            grid=(1,),
            in_specs=[anywhere] * (2 + len(weights)),
            out_specs=[whole(s) for s in [mixed.shape, outgoing, (16, 128)]],
            scratch_shapes=finish_scratch(mixed, gathered, weights),
        ),
        out_shape=[
            in_hbm(mixed.shape),
            jax.ShapeDtypeStruct(outgoing, jnp.bfloat16),
            in_hbm((16, 128)),
        ],
        cost_estimate=pl.CostEstimate(
            flops=2 * rows * block * width * part_width,
            bytes_accessed=rows * block * width * 2,
            transcendentals=0,
        ),
        compiler_params=params(),
        name="finish",
    )(picks, section, mixed, gathered, *weights)


def per_device(
    initial_features, layer_weights, adjacency_tiles, tile_columns, send_blocks, stale_imports
):
    section_count = lax.axis_size("section")
    part_count = lax.axis_size("dom")
    blocks_dev, fanout, block = adjacency_tiles.shape[:3]
    width = initial_features.shape[1]
    part_width = width // section_count
    groups = send_blocks.shape[1]
    group_blocks = blocks_dev // groups
    depth = layer_weights.shape[0]
    layers = depth * section_count
    streams = group_streams(groups)
    section = lax.axis_index("section").astype(jnp.int32).reshape(1)
    picks = send_blocks.reshape(-1)

    row_group = (jnp.arange(blocks_dev, dtype=jnp.int32) // group_blocks)[:, None]
    slot_group = (tile_columns - blocks_dev) // part_count
    is_stale = (tile_columns >= blocks_dev) & (slot_group > row_group)
    columns = jnp.where(
        is_stale, tile_columns + (groups - 1) * part_count, tile_columns
    ).reshape(-1)

    turned = [
        turn_blocks(section, stale_imports, (sub, 0), section_count) for sub in range(depth)
    ]
    started = prologue(
        initial_features, section, picks, turned[0][0], streams, group_blocks, block, part_width, part_count
    )
    own = started[: len(streams)]
    outgoing = started[len(streams) :]
    initial_blocks = own

    def exchange(value):
        return lax.all_to_all(value, "dom", split_axis=0, concat_axis=0, tiled=True)

    def spread(pieces):
        ring = range(section_count)
        return [pieces[0]] + [
            lax.ppermute(
                pieces[distance], "section", [(s, (s + distance) % section_count) for s in ring]
            )
            for distance in range(1, section_count)
        ]

    imports = [exchange(value) for value in outgoing]
    stale = [spread(pieces) for pieces in turned]
    weights = spread(turn_blocks(section, layer_weights[None], (0,), section_count))

    front, back = streams
    turned_late = [pieces[0] for pieces in turned[1:]]

    def parts_of(index, layer):
        return aggregate_parts(
            section, initial_blocks[index], adjacency_tiles, own, imports, stale[layer % depth],
            layer // depth, streams[index], streams, group_blocks, part_count,
        )

    own, imports = list(own), list(imports)
    shapes = [value.shape for value in initial_blocks]
    mixed_front = aggregate(columns, section, parts_of(0, 0), shapes[0], turned_late)
    for layer in range(layers):
        last = layer == layers - 1
        gathered_front = lax.all_gather(mixed_front, "section", axis=0, tiled=False)
        after = []
        if not last:
            front_result = finish(
                picks, section, mixed_front, gathered_front, weights, layer, depth, front,
                group_blocks, part_count,
            )
            after = [front_result[2]]
        mixed_back = aggregate(columns, section, parts_of(1, layer), shapes[1], after)
        gathered = lax.all_gather(mixed_back, "section", axis=0, tiled=False)
        if last:
            pairs = [(mixed_front, gathered_front), (mixed_back, gathered)]
            return finish_last(
                picks, section, pairs, weights, layer, depth, streams, group_blocks, part_count
            )
        own[0], imports[0] = front_result[0], exchange(front_result[1])
        own[1], outgoing, mixed_front = finish_and_aggregate(
            columns, picks, section, mixed_back, gathered, weights, layer, depth, back,
            group_blocks, part_count, parts_of(0, layer + 1), shapes[0],
        )
        imports[1] = exchange(outgoing)


def solution(mesh):
    return jax.shard_map(
        per_device,
        mesh=mesh,
        in_specs=(
            P("dom", None),
            P("section", None, None),
            P("dom", None, None, None),
            P("dom", None),
            P("dom", None, None),
            P("section", "dom", None, None, None),
        ),
        out_specs=P("dom", "section"),
        check_vma=False,
    )
```

```python
import functools
import math

import jax
import jax.numpy as jnp
from jax import lax
from jax.experimental import pallas as pl
from jax.experimental.pallas import tpu as pltpu
from jax.sharding import PartitionSpec as P

alpha_mix = 0.1
lambda_decay = 0.5
vmem_bytes = 48 * 1024 * 1024


def group_streams(groups):
    return [list(range(groups - 1)), [groups - 1]]


def params():
    return pltpu.CompilerParams(vmem_limit_bytes=vmem_bytes)


def in_hbm(shape):
    return pltpu.HBM(shape, jnp.bfloat16)


hbm = pl.BlockSpec(memory_space=pltpu.HBM)
anywhere = pl.BlockSpec(memory_space=pl.ANY)


def pinned(value):
    return pltpu.with_memory_space_constraint(value, pltpu.HBM)


def start_all(copies):
    for condition, copy in copies:
        if condition is None:
            copy.start()
        else:
            pl.when(condition)(copy.start)


def wait_all(copies):
    for condition, copy in copies:
        if condition is None:
            copy.wait()
        else:
            pl.when(condition)(copy.wait)


def whole(shape):
    return pl.BlockSpec(shape, lambda i, *prefetched: (0,) * len(shape))


def pick_outgoing(picks, blocks_ref, outgoing_ref, stream, group_blocks, part_count):
    for local, group in enumerate(stream):

        def pick(dest, carry):
            chosen = jnp.maximum(picks[group * part_count + dest], 0)
            outgoing_ref[dest, local] = blocks_ref[local * group_blocks + chosen]
            return carry

        lax.fori_loop(0, part_count, pick, 0)


def prologue_kernel(streams, group_blocks, part_count, info, picks, rows_ref, unused, *refs):
    own_refs = refs[: len(streams)]
    outgoing_refs = refs[len(streams) : 2 * len(streams)]
    turned = refs[-1]
    block = own_refs[0].shape[2]
    part_width = own_refs[0].shape[1]
    first = pl.multiple_of(info[0] * part_width, part_width)
    for stream, own_ref, outgoing_ref in zip(streams, own_refs, outgoing_refs):
        for local in range(len(stream) * group_blocks):
            row = (stream[0] * group_blocks + local) * block
            turned[local % 2] = rows_ref[row : row + block, :].T
            own_ref[local] = turned[local % 2, pl.ds(first, part_width), :]
        pick_outgoing(picks, own_ref, outgoing_ref, stream, group_blocks, part_count)


def prologue(initial_features, section, picks, after, streams, group_blocks, block, part_width, part_count):
    rows, width = initial_features.shape
    own_shapes = [(len(s) * group_blocks, part_width, block) for s in streams]
    out_shapes = [(part_count, len(s), part_width, block) for s in streams]
    return pl.pallas_call(
        functools.partial(prologue_kernel, streams, group_blocks, part_count),
        grid_spec=pltpu.PrefetchScalarGridSpec(
            num_scalar_prefetch=2,
            grid=(1,),
            in_specs=[whole((rows, width)), hbm],
            out_specs=[whole(s) for s in own_shapes + out_shapes],
            scratch_shapes=[pltpu.VMEM((2, width, block), jnp.bfloat16)],
        ),
        out_shape=[in_hbm(s) for s in own_shapes]
        + [jax.ShapeDtypeStruct(s, jnp.bfloat16) for s in out_shapes],
        compiler_params=params(),
        name="prologue",
    )(section, picks, pinned(initial_features), pinned(after))


def turn_kernel(info, in_ref, *refs):
    *out_refs, turned = refs
    count = in_ref.shape[-3]
    sections, part_width = len(out_refs), out_refs[0].shape[1]
    for item in range(count):
        turned[item % 2] = in_ref[0, item].T if len(in_ref.shape) == 4 else in_ref[0, 0, item].T
        for distance, out_ref in enumerate(out_refs):
            owner = lax.rem(info[0] + distance, sections)
            first = pl.multiple_of(owner * part_width, part_width)
            out_ref[item] = turned[item % 2, pl.ds(first, part_width), :]


def turn_blocks(section, blocks, lead, sections):
    count, rows, width = blocks.shape[-3:]
    step = 8 if count % 8 == 0 else count
    part_width = width // sections
    block_shape = (1,) * (len(blocks.shape) - 3) + (step, rows, width)
    out_spec = pl.BlockSpec((step, part_width, rows), lambda i, *prefetched: (i, 0, 0))
    return pl.pallas_call(
        turn_kernel,
        grid_spec=pltpu.PrefetchScalarGridSpec(
            num_scalar_prefetch=1,
            grid=(count // step,),
            in_specs=[pl.BlockSpec(block_shape, lambda i, *prefetched: lead + (i, 0, 0))],
            out_specs=[out_spec] * sections,
            scratch_shapes=[pltpu.VMEM((2, width, rows), jnp.bfloat16)],
        ),
        out_shape=[in_hbm((count, part_width, rows))] * sections,
        compiler_params=params(),
        name="turn",
    )(section, pinned(blocks))


class Aggregate:
    def __init__(self, plan, columns, info, initial_ref, tiles_ref, source_refs, mixed_ref, scratch):
        self.stream, self.group_blocks, self.fanout, sources, home, sections = plan
        self.columns, self.tiles_ref, self.mixed_ref = columns, tiles_ref, mixed_ref
        self.table, self.tiles, self.initial, table_sem, self.tiles_sem, initial_sem = scratch
        self.rows = len(self.stream) * self.group_blocks
        self.first_row = self.stream[0] * self.group_blocks
        self.ahead = min(3, self.rows)
        self.initial_copy = pltpu.make_async_copy(initial_ref, self.initial, initial_sem)
        self.copies = []
        for index, (kind, target, detail) in enumerate(sources):
            ref = source_refs[index]
            source = ref.at[:, detail] if kind == "import" else ref
            condition = None
            if kind == "stale":
                condition = lax.rem(info[0] - home + 2 * sections, sections) == detail
            part = self.table.at[pl.ds(target, source.shape[0])]
            copy = pltpu.make_async_copy(source, part, table_sem.at[index])
            self.copies.append((condition, copy))

    def tile_copy(self, row):
        return pltpu.make_async_copy(
            self.tiles_ref.at[self.first_row + row], self.tiles.at[row], self.tiles_sem.at[row]
        )

    def begin(self):
        start_all(self.copies)
        for row in range(self.ahead):
            self.tile_copy(row).start()
        self.initial_copy.start()

    def run(self):
        wait_all(self.copies)
        self.initial_copy.wait()

        def one_row(row, carry):
            self.tile_copy(row).wait()

            @pl.when(row + self.ahead < self.rows)
            def _():
                self.tile_copy(row + self.ahead).start()

            base = (self.first_row + row) * self.fanout
            total = None
            for tile in range(0, self.fanout, 2):
                span = range(tile, min(tile + 2, self.fanout))
                left = jnp.concatenate([self.table[self.columns[base + t]] for t in span], 1)
                right = jnp.concatenate([self.tiles[row, t] for t in span], 1)
                term = lax.dot_general(
                    left, right, (((1,), (1,)), ((), ())), preferred_element_type=jnp.float32
                )
                total = term if total is None else total + term
            start = self.initial[row].astype(jnp.float32)
            self.mixed_ref[row] = ((1.0 - alpha_mix) * total + alpha_mix * start).astype(
                jnp.bfloat16
            )
            return carry

        lax.fori_loop(0, self.rows, one_row, 0)


def aggregate_kernel(plan, columns, info, initial_ref, tiles_ref, *refs):
    count = len(plan[3])
    work = Aggregate(plan, columns, info, initial_ref, tiles_ref, refs[:count], refs[-7], refs[-6:])
    work.begin()
    work.run()


def both_kernel(plan, aggregate_plan, columns, picks, info, mixed_ref, gathered_ref, *refs):
    parts = gathered_ref.shape[0]
    count = len(aggregate_plan[3])
    weight_refs, refs = refs[:parts], refs[parts:]
    initial_ref, tiles_ref = refs[:2]
    source_refs, refs = refs[2 : 2 + count], refs[2 + count :]
    own_ref, outgoing_ref, next_ref = refs[:3]
    scratch = refs[3:5]
    work = Aggregate(
        aggregate_plan, columns, info, initial_ref, tiles_ref, source_refs, next_ref, refs[5:]
    )
    copies = finish_begin(plan, info, weight_refs, scratch)
    work.begin()
    finish_run(plan, copies, picks, mixed_ref, gathered_ref, [own_ref, outgoing_ref], scratch)
    work.run()


def aggregate_parts(section, initial_blocks, tiles, own, imports, stale, home, stream, streams, group_blocks, part_count):
    rows, part_width, block = initial_blocks.shape
    blocks_dev, fanout = tiles.shape[:2]
    groups = blocks_dev // group_blocks
    sources, operands, specs = [], [], []
    for other, own_blocks, imported in zip(streams, own, imports):
        if other[0] > stream[-1]:
            continue
        sources.append(("own", other[0] * group_blocks, None))
        operands.append(pinned(own_blocks))
        specs.append(hbm)
        for local, group in enumerate(other):
            sources.append(("import", blocks_dev + group * part_count, local))
            operands.append(imported)
            specs.append(anywhere)
    if groups > 1 and stream[0] < groups - 1:
        for distance, stale_blocks in enumerate(stale):
            sources.append(("stale", blocks_dev + groups * part_count, distance))
            operands.append(pinned(stale_blocks))
            specs.append(hbm)
    table_size = blocks_dev + (2 * groups - 1) * part_count
    plan = (stream, group_blocks, fanout, sources, home, len(stale))
    scratch = [
        pltpu.VMEM((table_size, part_width, block), jnp.bfloat16),
        pltpu.VMEM((rows, fanout, block, block), jnp.bfloat16),
        pltpu.VMEM(initial_blocks.shape, jnp.bfloat16),
        pltpu.SemaphoreType.DMA((len(sources),)),
        pltpu.SemaphoreType.DMA((rows,)),
        pltpu.SemaphoreType.DMA,
    ]
    operands = [pinned(initial_blocks), pinned(tiles)] + operands
    return plan, operands, [hbm, hbm] + specs, scratch


def estimate(rows, fanout, block, part_width, width):
    return pl.CostEstimate(
        flops=2 * rows * block * part_width * (fanout * block + width),
        bytes_accessed=rows * fanout * block * block * 2,
        transcendentals=0,
    )


def aggregate(columns, section, parts, shape, after):
    plan, operands, specs, scratch = parts
    operands = operands + [pinned(value) for value in after]
    return pl.pallas_call(
        functools.partial(aggregate_kernel, plan),
        grid_spec=pltpu.PrefetchScalarGridSpec(
            num_scalar_prefetch=2,
            grid=(1,),
            in_specs=specs + [hbm] * len(after),
            out_specs=whole(shape),
            scratch_shapes=scratch,
        ),
        out_shape=jax.ShapeDtypeStruct(shape, jnp.bfloat16),
        cost_estimate=estimate(shape[0], plan[2], shape[2], shape[1], 0),
        compiler_params=params(),
        name="aggregate",
    )(columns, section, *operands)


def finish_and_aggregate(columns, picks, section, mixed, gathered, weights, layer, depth, stream, group_blocks, part_count, parts, shape):
    aggregate_plan, operands, specs, scratch = parts
    rows, part_width, block = mixed.shape
    width = weights[0].shape[2]
    plan = finish_plan(layer, depth, stream, group_blocks, part_count, False)
    outgoing = (part_count, len(stream), part_width, block)
    return pl.pallas_call(
        functools.partial(both_kernel, plan, aggregate_plan),
        grid_spec=pltpu.PrefetchScalarGridSpec(
            num_scalar_prefetch=3,
            grid=(1,),
            in_specs=[whole(mixed.shape), whole(gathered.shape)]
            + [anywhere] * len(weights)
            + specs,
            out_specs=[whole(mixed.shape), whole(outgoing), whole(shape)],
            scratch_shapes=finish_scratch(weights) + scratch,
        ),
        out_shape=[
            in_hbm(mixed.shape),
            jax.ShapeDtypeStruct(outgoing, jnp.bfloat16),
            jax.ShapeDtypeStruct(shape, jnp.bfloat16),
        ],
        cost_estimate=estimate(shape[0], aggregate_plan[2], block, part_width, width),
        compiler_params=params(),
        name="finish_aggregate",
    )(columns, picks, section, mixed, gathered, *weights, *operands)


def finish_begin(plan, info, weight_refs, scratch):
    parts = len(weight_refs)
    sub, home = plan[4:6]
    weight, sem = scratch
    copies = [
        (
            lax.rem(info[0] - home + 2 * parts, parts) == distance,
            pltpu.make_async_copy(weight_ref.at[sub], weight, sem.at[distance]),
        )
        for distance, weight_ref in enumerate(weight_refs)
    ]
    start_all(copies)
    return copies


def finish_run(plan, copies, picks, mixed_ref, gathered_ref, refs, scratch):
    beta_layer, stream, group_blocks, part_count, sub, home, last = plan
    weight = scratch[0]
    rows, part_width, block = mixed_ref.shape
    parts = gathered_ref.shape[0]
    wait_all(copies)
    for row in range(0, rows, 2):
        span = range(row, min(row + 2, rows))
        right = jnp.concatenate(
            [jnp.concatenate([gathered_ref[p, r] for p in range(parts)], 0) for r in span], 1
        )
        product = jnp.dot(weight[...], right, preferred_element_type=jnp.float32)
        for place, r in enumerate(span):
            value = (1.0 - beta_layer) * mixed_ref[r].astype(jnp.float32) + beta_layer * product[
                :, place * block : (place + 1) * block
            ]
            value = jnp.maximum(value, 0.0).astype(jnp.bfloat16)
            if last:
                low = (stream[0] * group_blocks + r) * block
                refs[0][low : low + block, :] = value.T
            else:
                refs[0][r] = value
    if not last:
        pick_outgoing(picks, refs[0], refs[1], stream, group_blocks, part_count)


def finish_kernel(plan, picks, info, mixed_ref, gathered_ref, *refs):
    parts = gathered_ref.shape[0]
    weight_refs, out_refs, scratch = refs[:parts], refs[parts:-2], refs[-2:]
    copies = finish_begin(plan, info, weight_refs, scratch)
    finish_run(plan, copies, picks, mixed_ref, gathered_ref, out_refs, scratch)
    out_refs[2][...] = jnp.zeros_like(out_refs[2])


def last_kernel(plans, picks, info, *refs):
    parts = refs[1].shape[0]
    weight_refs, out_ref = refs[4 : 4 + parts], refs[4 + parts]
    scratch = refs[5 + parts :]
    copies = finish_begin(plans[0], info, weight_refs, scratch)
    for index, plan in enumerate(plans):
        mixed_ref, gathered_ref = refs[2 * index : 2 * index + 2]
        finish_run(plan, copies, picks, mixed_ref, gathered_ref, [out_ref], scratch)
        copies = []


def finish_plan(layer, depth, stream, group_blocks, part_count, last):
    beta_layer = math.log(lambda_decay / (layer + 1) + 1.0)
    return (beta_layer, stream, group_blocks, part_count, layer % depth, layer // depth, last)


def finish_scratch(weights):
    return [
        pltpu.VMEM(weights[0].shape[1:], jnp.bfloat16),
        pltpu.SemaphoreType.DMA((len(weights),)),
    ]


def finish_last(picks, section, pairs, weights, layer, depth, streams, group_blocks, part_count):
    plans = [finish_plan(layer, depth, s, group_blocks, part_count, True) for s in streams]
    rows = sum(mixed.shape[0] * mixed.shape[2] for mixed, gathered in pairs)
    shape = (rows, pairs[0][0].shape[1])
    return pl.pallas_call(
        functools.partial(last_kernel, plans),
        grid_spec=pltpu.PrefetchScalarGridSpec(
            num_scalar_prefetch=2,
            grid=(1,),
            in_specs=[whole(value.shape) for pair in pairs for value in pair]
            + [anywhere] * len(weights),
            out_specs=whole(shape),
            scratch_shapes=finish_scratch(weights),
        ),
        out_shape=jax.ShapeDtypeStruct(shape, jnp.bfloat16),
        compiler_params=params(),
        name="finish_last",
    )(picks, section, *[value for pair in pairs for value in pair], *weights)


def finish(picks, section, mixed, gathered, weights, layer, depth, stream, group_blocks, part_count):
    rows, part_width, block = mixed.shape
    width = weights[0].shape[2]
    plan = finish_plan(layer, depth, stream, group_blocks, part_count, False)
    outgoing = (part_count, len(stream), part_width, block)
    return pl.pallas_call(
        functools.partial(finish_kernel, plan),
        grid_spec=pltpu.PrefetchScalarGridSpec(
            num_scalar_prefetch=2,
            grid=(1,),
            in_specs=[whole(mixed.shape), whole(gathered.shape)] + [anywhere] * len(weights),
            out_specs=[whole(s) for s in [mixed.shape, outgoing, (16, 128)]],
            scratch_shapes=finish_scratch(weights),
        ),
        out_shape=[
            in_hbm(mixed.shape),
            jax.ShapeDtypeStruct(outgoing, jnp.bfloat16),
            in_hbm((16, 128)),
        ],
        cost_estimate=pl.CostEstimate(
            flops=2 * rows * block * width * part_width,
            bytes_accessed=rows * block * width * 2,
            transcendentals=0,
        ),
        compiler_params=params(),
        name="finish",
    )(picks, section, mixed, gathered, *weights)


def per_device(
    initial_features, layer_weights, adjacency_tiles, tile_columns, send_blocks, stale_imports
):
    section_count = lax.axis_size("section")
    part_count = lax.axis_size("dom")
    blocks_dev, fanout, block = adjacency_tiles.shape[:3]
    width = initial_features.shape[1]
    part_width = width // section_count
    groups = send_blocks.shape[1]
    group_blocks = blocks_dev // groups
    depth = layer_weights.shape[0]
    layers = depth * section_count
    streams = group_streams(groups)
    section = lax.axis_index("section").astype(jnp.int32).reshape(1)
    picks = send_blocks.reshape(-1)

    row_group = (jnp.arange(blocks_dev, dtype=jnp.int32) // group_blocks)[:, None]
    slot_group = (tile_columns - blocks_dev) // part_count
    is_stale = (tile_columns >= blocks_dev) & (slot_group > row_group)
    columns = jnp.where(
        is_stale, tile_columns + (groups - 1) * part_count, tile_columns
    ).reshape(-1)

    turned = [
        turn_blocks(section, stale_imports, (sub, 0), section_count) for sub in range(depth)
    ]
    started = prologue(
        initial_features, section, picks, turned[0][0], streams, group_blocks, block, part_width, part_count
    )
    own = started[: len(streams)]
    outgoing = started[len(streams) :]
    initial_blocks = own

    def exchange(value):
        return lax.all_to_all(value, "dom", split_axis=0, concat_axis=0, tiled=True)

    def spread(pieces):
        ring = range(section_count)
        return [pieces[0]] + [
            lax.ppermute(
                pieces[distance], "section", [(s, (s + distance) % section_count) for s in ring]
            )
            for distance in range(1, section_count)
        ]

    imports = [exchange(value) for value in outgoing]
    stale = [spread(pieces) for pieces in turned]
    weights = spread(turn_blocks(section, layer_weights[None], (0,), section_count))

    front, back = streams
    turned_late = [pieces[0] for pieces in turned[1:]]

    def parts_of(index, layer):
        return aggregate_parts(
            section, initial_blocks[index], adjacency_tiles, own, imports, stale[layer % depth],
            layer // depth, streams[index], streams, group_blocks, part_count,
        )

    own, imports = list(own), list(imports)
    shapes = [value.shape for value in initial_blocks]
    mixed_front = aggregate(columns, section, parts_of(0, 0), shapes[0], turned_late)
    for layer in range(layers):
        last = layer == layers - 1
        gathered_front = lax.all_gather(mixed_front, "section", axis=0, tiled=False)
        after = []
        if not last:
            front_result = finish(
                picks, section, mixed_front, gathered_front, weights, layer, depth, front,
                group_blocks, part_count,
            )
            after = [front_result[2]]
        mixed_back = aggregate(columns, section, parts_of(1, layer), shapes[1], after)
        gathered = lax.all_gather(mixed_back, "section", axis=0, tiled=False)
        if last:
            pairs = [(mixed_front, gathered_front), (mixed_back, gathered)]
            return finish_last(
                picks, section, pairs, weights, layer, depth, streams, group_blocks, part_count
            )
        own[0], imports[0] = front_result[0], exchange(front_result[1])
        own[1], outgoing, mixed_front = finish_and_aggregate(
            columns, picks, section, mixed_back, gathered, weights, layer, depth, back,
            group_blocks, part_count, parts_of(0, layer + 1), shapes[0],
        )
        imports[1] = exchange(outgoing)


def solution(mesh):
    return jax.shard_map(
        per_device,
        mesh=mesh,
        in_specs=(
            P("dom", None),
            P("section", None, None),
            P("dom", None, None, None),
            P("dom", None),
            P("dom", None, None),
            P("section", "dom", None, None, None),
        ),
        out_specs=P("dom", "section"),
        check_vma=False,
    )
```

```python
import functools
import math

import jax
import jax.numpy as jnp
from jax import lax
from jax.experimental import pallas as pl
from jax.experimental.pallas import tpu as pltpu
from jax.sharding import PartitionSpec as P

alpha_mix = 0.1
lambda_decay = 0.5
vmem_bytes = 48 * 1024 * 1024


def group_streams(groups):
    return [list(range(groups - 1)), [groups - 1]]


def params():
    return pltpu.CompilerParams(vmem_limit_bytes=vmem_bytes)


def in_hbm(shape):
    return pltpu.HBM(shape, jnp.bfloat16)


hbm = pl.BlockSpec(memory_space=pltpu.HBM)
anywhere = pl.BlockSpec(memory_space=pl.ANY)


def pinned(value):
    return pltpu.with_memory_space_constraint(value, pltpu.HBM)


def start_all(copies):
    for condition, copy in copies:
        if condition is None:
            copy.start()
        else:
            pl.when(condition)(copy.start)


def wait_all(copies):
    for condition, copy in copies:
        if condition is None:
            copy.wait()
        else:
            pl.when(condition)(copy.wait)


def whole(shape):
    return pl.BlockSpec(shape, lambda i, *prefetched: (0,) * len(shape))


def pick_outgoing(picks, blocks_ref, outgoing_ref, stream, group_blocks, part_count):
    for local, group in enumerate(stream):

        def pick(dest, carry):
            chosen = jnp.maximum(picks[group * part_count + dest], 0)
            outgoing_ref[dest, local] = blocks_ref[local * group_blocks + chosen]
            return carry

        lax.fori_loop(0, part_count, pick, 0)


def prologue_kernel(streams, group_blocks, part_count, info, picks, rows_ref, unused, *refs):
    own_refs = refs[: len(streams)]
    outgoing_refs = refs[len(streams) : 2 * len(streams)]
    turned = refs[-1]
    block = own_refs[0].shape[2]
    part_width = own_refs[0].shape[1]
    first = pl.multiple_of(info[0] * part_width, part_width)
    for stream, own_ref, outgoing_ref in zip(streams, own_refs, outgoing_refs):
        for local in range(len(stream) * group_blocks):
            row = (stream[0] * group_blocks + local) * block
            turned[local % 2] = rows_ref[row : row + block, :].T
            own_ref[local] = turned[local % 2, pl.ds(first, part_width), :]
        pick_outgoing(picks, own_ref, outgoing_ref, stream, group_blocks, part_count)


def prologue(initial_features, section, picks, after, streams, group_blocks, block, part_width, part_count):
    rows, width = initial_features.shape
    own_shapes = [(len(s) * group_blocks, part_width, block) for s in streams]
    out_shapes = [(part_count, len(s), part_width, block) for s in streams]
    return pl.pallas_call(
        functools.partial(prologue_kernel, streams, group_blocks, part_count),
        grid_spec=pltpu.PrefetchScalarGridSpec(
            num_scalar_prefetch=2,
            grid=(1,),
            in_specs=[whole((rows, width)), hbm],
            out_specs=[whole(s) for s in own_shapes + out_shapes],
            scratch_shapes=[pltpu.VMEM((2, width, block), jnp.bfloat16)],
        ),
        out_shape=[in_hbm(s) for s in own_shapes]
        + [jax.ShapeDtypeStruct(s, jnp.bfloat16) for s in out_shapes],
        compiler_params=params(),
        name="prologue",
    )(section, picks, pinned(initial_features), pinned(after))


def turn_kernel(info, in_ref, *refs):
    *out_refs, turned = refs
    count = in_ref.shape[-3]
    sections, part_width = len(out_refs), out_refs[0].shape[1]
    for item in range(count):
        turned[item % 2] = in_ref[0, item].T if len(in_ref.shape) == 4 else in_ref[0, 0, item].T
        for distance, out_ref in enumerate(out_refs):
            owner = lax.rem(info[0] + distance, sections)
            first = pl.multiple_of(owner * part_width, part_width)
            out_ref[item] = turned[item % 2, pl.ds(first, part_width), :]


def turn_blocks(section, blocks, lead, sections):
    count, rows, width = blocks.shape[-3:]
    step = 8 if count % 8 == 0 else count
    part_width = width // sections
    block_shape = (1,) * (len(blocks.shape) - 3) + (step, rows, width)
    out_spec = pl.BlockSpec((step, part_width, rows), lambda i, *prefetched: (i, 0, 0))
    return pl.pallas_call(
        turn_kernel,
        grid_spec=pltpu.PrefetchScalarGridSpec(
            num_scalar_prefetch=1,
            grid=(count // step,),
            in_specs=[pl.BlockSpec(block_shape, lambda i, *prefetched: lead + (i, 0, 0))],
            out_specs=[out_spec] * sections,
            scratch_shapes=[pltpu.VMEM((2, width, rows), jnp.bfloat16)],
        ),
        out_shape=[in_hbm((count, part_width, rows))] * sections,
        compiler_params=params(),
        name="turn",
    )(section, pinned(blocks))


class Aggregate:
    def __init__(self, plan, columns, info, initial_ref, tiles_ref, source_refs, mixed_ref, scratch):
        self.stream, self.group_blocks, self.fanout, sources, home, sections = plan
        self.columns, self.tiles_ref, self.mixed_ref = columns, tiles_ref, mixed_ref
        self.table, self.tiles, self.initial, table_sem, self.tiles_sem, initial_sem = scratch
        self.rows = len(self.stream) * self.group_blocks
        self.first_row = self.stream[0] * self.group_blocks
        self.ahead = min(4, self.rows)
        self.initial_copy = pltpu.make_async_copy(initial_ref, self.initial, initial_sem)
        self.copies = []
        for index, (kind, target, detail) in enumerate(sources):
            ref = source_refs[index]
            source = ref.at[:, detail] if kind == "import" else ref
            condition = None
            if kind == "stale":
                condition = lax.rem(info[0] - home + 2 * sections, sections) == detail
            part = self.table.at[pl.ds(target, source.shape[0])]
            copy = pltpu.make_async_copy(source, part, table_sem.at[index])
            self.copies.append((condition, copy))

    def tile_copy(self, row):
        return pltpu.make_async_copy(
            self.tiles_ref.at[self.first_row + row], self.tiles.at[row], self.tiles_sem.at[row]
        )

    def begin(self):
        start_all(self.copies)
        for row in range(self.ahead):
            self.tile_copy(row).start()
        self.initial_copy.start()

    def run(self):
        wait_all(self.copies)
        self.initial_copy.wait()

        def one_row(row, carry):
            self.tile_copy(row).wait()

            @pl.when(row + self.ahead < self.rows)
            def _():
                self.tile_copy(row + self.ahead).start()

            base = (self.first_row + row) * self.fanout
            total = None
            for tile in range(0, self.fanout, 2):
                span = range(tile, min(tile + 2, self.fanout))
                left = jnp.concatenate([self.table[self.columns[base + t]] for t in span], 1)
                right = jnp.concatenate([self.tiles[row, t] for t in span], 1)
                term = lax.dot_general(
                    left, right, (((1,), (1,)), ((), ())), preferred_element_type=jnp.float32
                )
                total = term if total is None else total + term
            start = self.initial[row].astype(jnp.float32)
            self.mixed_ref[row] = ((1.0 - alpha_mix) * total + alpha_mix * start).astype(
                jnp.bfloat16
            )
            return carry

        lax.fori_loop(0, self.rows, one_row, 0, unroll=2 if self.rows % 2 == 0 else 1)


def aggregate_kernel(plan, columns, info, initial_ref, tiles_ref, *refs):
    count = len(plan[3])
    work = Aggregate(plan, columns, info, initial_ref, tiles_ref, refs[:count], refs[-7], refs[-6:])
    work.begin()
    work.run()


def both_kernel(plan, aggregate_plan, columns, picks, info, mixed_ref, gathered_ref, *refs):
    parts = gathered_ref.shape[0]
    count = len(aggregate_plan[3])
    weight_refs, refs = refs[:parts], refs[parts:]
    initial_ref, tiles_ref = refs[:2]
    source_refs, refs = refs[2 : 2 + count], refs[2 + count :]
    own_ref, outgoing_ref, next_ref = refs[:3]
    scratch = refs[3:5]
    work = Aggregate(
        aggregate_plan, columns, info, initial_ref, tiles_ref, source_refs, next_ref, refs[5:]
    )
    work.begin()
    copies = finish_begin(plan, info, weight_refs, scratch)
    finish_run(plan, copies, picks, mixed_ref, gathered_ref, [own_ref, outgoing_ref], scratch)
    work.run()


def aggregate_parts(section, initial_blocks, tiles, own, imports, stale, home, stream, streams, group_blocks, part_count):
    rows, part_width, block = initial_blocks.shape
    blocks_dev, fanout = tiles.shape[:2]
    groups = blocks_dev // group_blocks
    sources, operands, specs = [], [], []
    for other, own_blocks, imported in zip(streams, own, imports):
        if other[0] > stream[-1]:
            continue
        sources.append(("own", other[0] * group_blocks, None))
        operands.append(pinned(own_blocks))
        specs.append(hbm)
        for local, group in enumerate(other):
            sources.append(("import", blocks_dev + group * part_count, local))
            operands.append(imported)
            specs.append(anywhere)
    if groups > 1 and stream[0] < groups - 1:
        for distance, stale_blocks in enumerate(stale):
            sources.append(("stale", blocks_dev + groups * part_count, distance))
            operands.append(pinned(stale_blocks))
            specs.append(hbm)
    table_size = blocks_dev + (2 * groups - 1) * part_count
    plan = (stream, group_blocks, fanout, sources, home, len(stale))
    scratch = [
        pltpu.VMEM((table_size, part_width, block), jnp.bfloat16),
        pltpu.VMEM((rows, fanout, block, block), jnp.bfloat16),
        pltpu.VMEM(initial_blocks.shape, jnp.bfloat16),
        pltpu.SemaphoreType.DMA((len(sources),)),
        pltpu.SemaphoreType.DMA((rows,)),
        pltpu.SemaphoreType.DMA,
    ]
    operands = [pinned(initial_blocks), pinned(tiles)] + operands
    return plan, operands, [hbm, hbm] + specs, scratch


def estimate(rows, fanout, block, part_width, width):
    return pl.CostEstimate(
        flops=2 * rows * block * part_width * (fanout * block + width),
        bytes_accessed=rows * fanout * block * block * 2,
        transcendentals=0,
    )


def aggregate(columns, section, parts, shape, after):
    plan, operands, specs, scratch = parts
    operands = operands + [pinned(value) for value in after]
    return pl.pallas_call(
        functools.partial(aggregate_kernel, plan),
        grid_spec=pltpu.PrefetchScalarGridSpec(
            num_scalar_prefetch=2,
            grid=(1,),
            in_specs=specs + [hbm] * len(after),
            out_specs=whole(shape),
            scratch_shapes=scratch,
        ),
        out_shape=jax.ShapeDtypeStruct(shape, jnp.bfloat16),
        cost_estimate=estimate(shape[0], plan[2], shape[2], shape[1], 0),
        compiler_params=params(),
        name="aggregate",
    )(columns, section, *operands)


def finish_and_aggregate(columns, picks, section, mixed, gathered, weights, layer, depth, stream, group_blocks, part_count, parts, shape):
    aggregate_plan, operands, specs, scratch = parts
    rows, part_width, block = mixed.shape
    width = weights[0].shape[2]
    plan = finish_plan(layer, depth, stream, group_blocks, part_count, False)
    outgoing = (part_count, len(stream), part_width, block)
    return pl.pallas_call(
        functools.partial(both_kernel, plan, aggregate_plan),
        grid_spec=pltpu.PrefetchScalarGridSpec(
            num_scalar_prefetch=3,
            grid=(1,),
            in_specs=[whole(mixed.shape), whole(gathered.shape)]
            + [anywhere] * len(weights)
            + specs,
            out_specs=[whole(mixed.shape), whole(outgoing), whole(shape)],
            scratch_shapes=finish_scratch(weights) + scratch,
        ),
        out_shape=[
            in_hbm(mixed.shape),
            jax.ShapeDtypeStruct(outgoing, jnp.bfloat16),
            jax.ShapeDtypeStruct(shape, jnp.bfloat16),
        ],
        cost_estimate=estimate(shape[0], aggregate_plan[2], block, part_width, width),
        compiler_params=params(),
        name="finish_aggregate",
    )(columns, picks, section, mixed, gathered, *weights, *operands)


def finish_begin(plan, info, weight_refs, scratch):
    parts = len(weight_refs)
    sub, home = plan[4:6]
    weight, sem = scratch
    copies = [
        (
            lax.rem(info[0] - home + 2 * parts, parts) == distance,
            pltpu.make_async_copy(weight_ref.at[sub], weight, sem.at[distance]),
        )
        for distance, weight_ref in enumerate(weight_refs)
    ]
    start_all(copies)
    return copies


def finish_run(plan, copies, picks, mixed_ref, gathered_ref, refs, scratch):
    beta_layer, stream, group_blocks, part_count, sub, home, last = plan
    weight = scratch[0]
    rows, part_width, block = mixed_ref.shape
    parts = gathered_ref.shape[0]
    wait_all(copies)
    for row in range(0, rows, 2):
        span = range(row, min(row + 2, rows))
        right = jnp.concatenate(
            [jnp.concatenate([gathered_ref[p, r] for p in range(parts)], 0) for r in span], 1
        )
        product = jnp.dot(weight[...], right, preferred_element_type=jnp.float32)
        for place, r in enumerate(span):
            value = (1.0 - beta_layer) * mixed_ref[r].astype(jnp.float32) + beta_layer * product[
                :, place * block : (place + 1) * block
            ]
            value = jnp.maximum(value, 0.0).astype(jnp.bfloat16)
            if last:
                low = (stream[0] * group_blocks + r) * block
                refs[0][low : low + block, :] = value.T
            else:
                refs[0][r] = value
    if not last:
        pick_outgoing(picks, refs[0], refs[1], stream, group_blocks, part_count)


def finish_kernel(plan, picks, info, mixed_ref, gathered_ref, *refs):
    parts = gathered_ref.shape[0]
    weight_refs, out_refs, scratch = refs[:parts], refs[parts:-2], refs[-2:]
    copies = finish_begin(plan, info, weight_refs, scratch)
    finish_run(plan, copies, picks, mixed_ref, gathered_ref, out_refs, scratch)
    out_refs[2][...] = jnp.zeros_like(out_refs[2])


def last_kernel(plans, picks, info, *refs):
    parts = refs[1].shape[0]
    weight_refs, out_ref = refs[4 : 4 + parts], refs[4 + parts]
    scratch = refs[5 + parts :]
    copies = finish_begin(plans[0], info, weight_refs, scratch)
    for index, plan in enumerate(plans):
        mixed_ref, gathered_ref = refs[2 * index : 2 * index + 2]
        finish_run(plan, copies, picks, mixed_ref, gathered_ref, [out_ref], scratch)
        copies = []


def finish_plan(layer, depth, stream, group_blocks, part_count, last):
    beta_layer = math.log(lambda_decay / (layer + 1) + 1.0)
    return (beta_layer, stream, group_blocks, part_count, layer % depth, layer // depth, last)


def finish_scratch(weights):
    return [
        pltpu.VMEM(weights[0].shape[1:], jnp.bfloat16),
        pltpu.SemaphoreType.DMA((len(weights),)),
    ]


def finish_last(picks, section, pairs, weights, layer, depth, streams, group_blocks, part_count):
    plans = [finish_plan(layer, depth, s, group_blocks, part_count, True) for s in streams]
    rows = sum(mixed.shape[0] * mixed.shape[2] for mixed, gathered in pairs)
    shape = (rows, pairs[0][0].shape[1])
    return pl.pallas_call(
        functools.partial(last_kernel, plans),
        grid_spec=pltpu.PrefetchScalarGridSpec(
            num_scalar_prefetch=2,
            grid=(1,),
            in_specs=[whole(value.shape) for pair in pairs for value in pair]
            + [anywhere] * len(weights),
            out_specs=whole(shape),
            scratch_shapes=finish_scratch(weights),
        ),
        out_shape=jax.ShapeDtypeStruct(shape, jnp.bfloat16),
        compiler_params=params(),
        name="finish_last",
    )(picks, section, *[value for pair in pairs for value in pair], *weights)


def finish(picks, section, mixed, gathered, weights, layer, depth, stream, group_blocks, part_count):
    rows, part_width, block = mixed.shape
    width = weights[0].shape[2]
    plan = finish_plan(layer, depth, stream, group_blocks, part_count, False)
    outgoing = (part_count, len(stream), part_width, block)
    return pl.pallas_call(
        functools.partial(finish_kernel, plan),
        grid_spec=pltpu.PrefetchScalarGridSpec(
            num_scalar_prefetch=2,
            grid=(1,),
            in_specs=[whole(mixed.shape), whole(gathered.shape)] + [anywhere] * len(weights),
            out_specs=[whole(s) for s in [mixed.shape, outgoing, (16, 128)]],
            scratch_shapes=finish_scratch(weights),
        ),
        out_shape=[
            in_hbm(mixed.shape),
            jax.ShapeDtypeStruct(outgoing, jnp.bfloat16),
            in_hbm((16, 128)),
        ],
        cost_estimate=pl.CostEstimate(
            flops=2 * rows * block * width * part_width,
            bytes_accessed=rows * block * width * 2,
            transcendentals=0,
        ),
        compiler_params=params(),
        name="finish",
    )(picks, section, mixed, gathered, *weights)


def per_device(
    initial_features, layer_weights, adjacency_tiles, tile_columns, send_blocks, stale_imports
):
    section_count = lax.axis_size("section")
    part_count = lax.axis_size("dom")
    blocks_dev, fanout, block = adjacency_tiles.shape[:3]
    width = initial_features.shape[1]
    part_width = width // section_count
    groups = send_blocks.shape[1]
    group_blocks = blocks_dev // groups
    depth = layer_weights.shape[0]
    layers = depth * section_count
    streams = group_streams(groups)
    section = lax.axis_index("section").astype(jnp.int32).reshape(1)
    picks = send_blocks.reshape(-1)

    row_group = (jnp.arange(blocks_dev, dtype=jnp.int32) // group_blocks)[:, None]
    slot_group = (tile_columns - blocks_dev) // part_count
    is_stale = (tile_columns >= blocks_dev) & (slot_group > row_group)
    columns = jnp.where(
        is_stale, tile_columns + (groups - 1) * part_count, tile_columns
    ).reshape(-1)

    turned = [
        turn_blocks(section, stale_imports, (sub, 0), section_count) for sub in range(depth)
    ]
    started = prologue(
        initial_features, section, picks, turned[0][0], streams, group_blocks, block, part_width, part_count
    )
    own = started[: len(streams)]
    outgoing = started[len(streams) :]
    initial_blocks = own

    def exchange(value):
        return lax.all_to_all(value, "dom", split_axis=0, concat_axis=0, tiled=True)

    def spread(pieces):
        ring = range(section_count)
        return [pieces[0]] + [
            lax.ppermute(
                pieces[distance], "section", [(s, (s + distance) % section_count) for s in ring]
            )
            for distance in range(1, section_count)
        ]

    imports = [exchange(value) for value in outgoing]
    stale = [spread(pieces) for pieces in turned]
    weights = spread(turn_blocks(section, layer_weights[None], (0,), section_count))

    front, back = streams
    turned_late = [pieces[0] for pieces in turned[1:]]

    def parts_of(index, layer):
        return aggregate_parts(
            section, initial_blocks[index], adjacency_tiles, own, imports, stale[layer % depth],
            layer // depth, streams[index], streams, group_blocks, part_count,
        )

    own, imports = list(own), list(imports)
    shapes = [value.shape for value in initial_blocks]
    mixed_front = aggregate(columns, section, parts_of(0, 0), shapes[0], turned_late)
    for layer in range(layers):
        last = layer == layers - 1
        gathered_front = lax.all_gather(mixed_front, "section", axis=0, tiled=False)
        after = []
        if not last:
            front_result = finish(
                picks, section, mixed_front, gathered_front, weights, layer, depth, front,
                group_blocks, part_count,
            )
            after = [front_result[2]]
        mixed_back = aggregate(columns, section, parts_of(1, layer), shapes[1], after)
        gathered = lax.all_gather(mixed_back, "section", axis=0, tiled=False)
        if last:
            pairs = [(mixed_front, gathered_front), (mixed_back, gathered)]
            return finish_last(
                picks, section, pairs, weights, layer, depth, streams, group_blocks, part_count
            )
        own[0], imports[0] = front_result[0], exchange(front_result[1])
        own[1], outgoing, mixed_front = finish_and_aggregate(
            columns, picks, section, mixed_back, gathered, weights, layer, depth, back,
            group_blocks, part_count, parts_of(0, layer + 1), shapes[0],
        )
        imports[1] = exchange(outgoing)


def solution(mesh):
    return jax.shard_map(
        per_device,
        mesh=mesh,
        in_specs=(
            P("dom", None),
            P("section", None, None),
            P("dom", None, None, None),
            P("dom", None),
            P("dom", None, None),
            P("section", "dom", None, None, None),
        ),
        out_specs=P("dom", "section"),
        check_vma=False,
    )
```

```python
import functools
import math

import jax
import jax.numpy as jnp
from jax import lax
from jax.experimental import pallas as pl
from jax.experimental.pallas import tpu as pltpu
from jax.sharding import PartitionSpec as P

alpha_mix = 0.1
lambda_decay = 0.5
vmem_bytes = 48 * 1024 * 1024


def group_streams(groups):
    return [list(range(groups - 1)), [groups - 1]]


def params():
    return pltpu.CompilerParams(vmem_limit_bytes=vmem_bytes)


def in_hbm(shape):
    return pltpu.HBM(shape, jnp.bfloat16)


hbm = pl.BlockSpec(memory_space=pltpu.HBM)
anywhere = pl.BlockSpec(memory_space=pl.ANY)


def pinned(value):
    return pltpu.with_memory_space_constraint(value, pltpu.HBM)


def start_all(copies):
    for condition, copy in copies:
        if condition is None:
            copy.start()
        else:
            pl.when(condition)(copy.start)


def wait_all(copies):
    for condition, copy in copies:
        if condition is None:
            copy.wait()
        else:
            pl.when(condition)(copy.wait)


def whole(shape):
    return pl.BlockSpec(shape, lambda i, *prefetched: (0,) * len(shape))


def pick_outgoing(picks, blocks_ref, outgoing_ref, stream, group_blocks, part_count):
    for local, group in enumerate(stream):

        def pick(dest, carry):
            chosen = jnp.maximum(picks[group * part_count + dest], 0)
            outgoing_ref[dest, local] = blocks_ref[local * group_blocks + chosen]
            return carry

        lax.fori_loop(0, part_count, pick, 0)


def prologue_kernel(streams, group_blocks, part_count, info, picks, rows_ref, unused, *refs):
    own_refs = refs[: len(streams)]
    outgoing_refs = refs[len(streams) : 2 * len(streams)]
    turned = refs[-1]
    block = own_refs[0].shape[2]
    part_width = own_refs[0].shape[1]
    first = pl.multiple_of(info[0] * part_width, part_width)
    for stream, own_ref, outgoing_ref in zip(streams, own_refs, outgoing_refs):
        for local in range(len(stream) * group_blocks):
            row = (stream[0] * group_blocks + local) * block
            turned[local % 2] = rows_ref[row : row + block, :].T
            own_ref[local] = turned[local % 2, pl.ds(first, part_width), :]
        pick_outgoing(picks, own_ref, outgoing_ref, stream, group_blocks, part_count)


def prologue(initial_features, section, picks, after, streams, group_blocks, block, part_width, part_count):
    rows, width = initial_features.shape
    own_shapes = [(len(s) * group_blocks, part_width, block) for s in streams]
    out_shapes = [(part_count, len(s), part_width, block) for s in streams]
    return pl.pallas_call(
        functools.partial(prologue_kernel, streams, group_blocks, part_count),
        grid_spec=pltpu.PrefetchScalarGridSpec(
            num_scalar_prefetch=2,
            grid=(1,),
            in_specs=[whole((rows, width)), hbm],
            out_specs=[whole(s) for s in own_shapes + out_shapes],
            scratch_shapes=[pltpu.VMEM((2, width, block), jnp.bfloat16)],
        ),
        out_shape=[in_hbm(s) for s in own_shapes]
        + [jax.ShapeDtypeStruct(s, jnp.bfloat16) for s in out_shapes],
        compiler_params=params(),
        name="prologue",
    )(section, picks, pinned(initial_features), pinned(after))


def turn_kernel(info, in_ref, *refs):
    *out_refs, turned = refs
    count = in_ref.shape[-3]
    sections, part_width = len(out_refs), out_refs[0].shape[1]
    for item in range(count):
        turned[item % 2] = in_ref[0, item].T if len(in_ref.shape) == 4 else in_ref[0, 0, item].T
        for distance, out_ref in enumerate(out_refs):
            owner = lax.rem(info[0] + distance, sections)
            first = pl.multiple_of(owner * part_width, part_width)
            out_ref[item] = turned[item % 2, pl.ds(first, part_width), :]


def turn_blocks(section, blocks, lead, sections):
    count, rows, width = blocks.shape[-3:]
    step = 8 if count % 8 == 0 else count
    part_width = width // sections
    block_shape = (1,) * (len(blocks.shape) - 3) + (step, rows, width)
    out_spec = pl.BlockSpec((step, part_width, rows), lambda i, *prefetched: (i, 0, 0))
    return pl.pallas_call(
        turn_kernel,
        grid_spec=pltpu.PrefetchScalarGridSpec(
            num_scalar_prefetch=1,
            grid=(count // step,),
            in_specs=[pl.BlockSpec(block_shape, lambda i, *prefetched: lead + (i, 0, 0))],
            out_specs=[out_spec] * sections,
            scratch_shapes=[pltpu.VMEM((2, width, rows), jnp.bfloat16)],
        ),
        out_shape=[in_hbm((count, part_width, rows))] * sections,
        compiler_params=params(),
        name="turn",
    )(section, pinned(blocks))


class Aggregate:
    def __init__(self, plan, columns, info, initial_ref, tiles_ref, source_refs, mixed_ref, scratch):
        self.stream, self.group_blocks, self.fanout, sources, home, sections = plan
        self.columns, self.tiles_ref, self.mixed_ref = columns, tiles_ref, mixed_ref
        self.table, self.tiles, self.initial, table_sem, self.tiles_sem, initial_sem = scratch
        self.rows = len(self.stream) * self.group_blocks
        self.first_row = self.stream[0] * self.group_blocks
        self.ahead = min(3, self.rows)
        self.initial_copy = pltpu.make_async_copy(initial_ref, self.initial, initial_sem)
        self.copies = []
        for index, (kind, target, detail) in enumerate(sources):
            ref = source_refs[index]
            source = ref.at[:, detail] if kind == "import" else ref
            condition = None
            if kind == "stale":
                condition = lax.rem(info[0] - home + 2 * sections, sections) == detail
            part = self.table.at[pl.ds(target, source.shape[0])]
            copy = pltpu.make_async_copy(source, part, table_sem.at[index])
            self.copies.append((condition, copy))

    def tile_copy(self, row):
        return pltpu.make_async_copy(
            self.tiles_ref.at[self.first_row + row], self.tiles.at[row], self.tiles_sem.at[row]
        )

    def begin(self):
        start_all(self.copies)
        for row in range(self.ahead):
            self.tile_copy(row).start()
        self.initial_copy.start()

    def run(self):
        wait_all(self.copies)
        self.initial_copy.wait()

        def one_row(row, carry):
            self.tile_copy(row).wait()

            @pl.when(row + self.ahead < self.rows)
            def _():
                self.tile_copy(row + self.ahead).start()

            base = (self.first_row + row) * self.fanout
            span = range(self.fanout)
            left = jnp.concatenate([self.table[self.columns[base + t]] for t in span], 1)
            right = jnp.concatenate([self.tiles[row, t] for t in span], 1)
            total = lax.dot_general(
                left, right, (((1,), (1,)), ((), ())), preferred_element_type=jnp.float32
            )
            start = self.initial[row].astype(jnp.float32)
            self.mixed_ref[row] = ((1.0 - alpha_mix) * total + alpha_mix * start).astype(
                jnp.bfloat16
            )
            return carry

        lax.fori_loop(0, self.rows, one_row, 0)


def aggregate_kernel(plan, columns, info, initial_ref, tiles_ref, *refs):
    count = len(plan[3])
    work = Aggregate(plan, columns, info, initial_ref, tiles_ref, refs[:count], refs[-7], refs[-6:])
    work.begin()
    work.run()


def both_kernel(plan, aggregate_plan, columns, picks, info, mixed_ref, gathered_ref, *refs):
    parts = gathered_ref.shape[0]
    count = len(aggregate_plan[3])
    weight_refs, refs = refs[:parts], refs[parts:]
    initial_ref, tiles_ref = refs[:2]
    source_refs, refs = refs[2 : 2 + count], refs[2 + count :]
    own_ref, outgoing_ref, next_ref = refs[:3]
    scratch = refs[3:5]
    work = Aggregate(
        aggregate_plan, columns, info, initial_ref, tiles_ref, source_refs, next_ref, refs[5:]
    )
    copies = finish_begin(plan, info, weight_refs, scratch)
    work.begin()
    finish_run(plan, copies, picks, mixed_ref, gathered_ref, [own_ref, outgoing_ref], scratch)
    work.run()


def aggregate_parts(section, initial_blocks, tiles, own, imports, stale, home, stream, streams, group_blocks, part_count):
    rows, part_width, block = initial_blocks.shape
    blocks_dev, fanout = tiles.shape[:2]
    groups = blocks_dev // group_blocks
    sources, operands, specs = [], [], []
    for other, own_blocks, imported in zip(streams, own, imports):
        if other[0] > stream[-1]:
            continue
        sources.append(("own", other[0] * group_blocks, None))
        operands.append(pinned(own_blocks))
        specs.append(hbm)
        for local, group in enumerate(other):
            sources.append(("import", blocks_dev + group * part_count, local))
            operands.append(imported)
            specs.append(anywhere)
    if groups > 1 and stream[0] < groups - 1:
        for distance, stale_blocks in enumerate(stale):
            sources.append(("stale", blocks_dev + groups * part_count, distance))
            operands.append(pinned(stale_blocks))
            specs.append(hbm)
    table_size = blocks_dev + (2 * groups - 1) * part_count
    plan = (stream, group_blocks, fanout, sources, home, len(stale))
    scratch = [
        pltpu.VMEM((table_size, part_width, block), jnp.bfloat16),
        pltpu.VMEM((rows, fanout, block, block), jnp.bfloat16),
        pltpu.VMEM(initial_blocks.shape, jnp.bfloat16),
        pltpu.SemaphoreType.DMA((len(sources),)),
        pltpu.SemaphoreType.DMA((rows,)),
        pltpu.SemaphoreType.DMA,
    ]
    operands = [pinned(initial_blocks), pinned(tiles)] + operands
    return plan, operands, [hbm, hbm] + specs, scratch


def estimate(rows, fanout, block, part_width, width):
    return pl.CostEstimate(
        flops=2 * rows * block * part_width * (fanout * block + width),
        bytes_accessed=rows * fanout * block * block * 2,
        transcendentals=0,
    )


def aggregate(columns, section, parts, shape, after):
    plan, operands, specs, scratch = parts
    operands = operands + [pinned(value) for value in after]
    return pl.pallas_call(
        functools.partial(aggregate_kernel, plan),
        grid_spec=pltpu.PrefetchScalarGridSpec(
            num_scalar_prefetch=2,
            grid=(1,),
            in_specs=specs + [hbm] * len(after),
            out_specs=whole(shape),
            scratch_shapes=scratch,
        ),
        out_shape=jax.ShapeDtypeStruct(shape, jnp.bfloat16),
        cost_estimate=estimate(shape[0], plan[2], shape[2], shape[1], 0),
        compiler_params=params(),
        name="aggregate",
    )(columns, section, *operands)


def finish_and_aggregate(columns, picks, section, mixed, gathered, weights, layer, depth, stream, group_blocks, part_count, parts, shape):
    aggregate_plan, operands, specs, scratch = parts
    rows, part_width, block = mixed.shape
    width = weights[0].shape[2]
    plan = finish_plan(layer, depth, stream, group_blocks, part_count, False)
    outgoing = (part_count, len(stream), part_width, block)
    return pl.pallas_call(
        functools.partial(both_kernel, plan, aggregate_plan),
        grid_spec=pltpu.PrefetchScalarGridSpec(
            num_scalar_prefetch=3,
            grid=(1,),
            in_specs=[whole(mixed.shape), whole(gathered.shape)]
            + [anywhere] * len(weights)
            + specs,
            out_specs=[whole(mixed.shape), whole(outgoing), whole(shape)],
            scratch_shapes=finish_scratch(weights) + scratch,
        ),
        out_shape=[
            in_hbm(mixed.shape),
            jax.ShapeDtypeStruct(outgoing, jnp.bfloat16),
            jax.ShapeDtypeStruct(shape, jnp.bfloat16),
        ],
        cost_estimate=estimate(shape[0], aggregate_plan[2], block, part_width, width),
        compiler_params=params(),
        name="finish_aggregate",
    )(columns, picks, section, mixed, gathered, *weights, *operands)


def finish_begin(plan, info, weight_refs, scratch):
    parts = len(weight_refs)
    sub, home = plan[4:6]
    weight, sem = scratch
    copies = [
        (
            lax.rem(info[0] - home + 2 * parts, parts) == distance,
            pltpu.make_async_copy(weight_ref.at[sub], weight, sem.at[distance]),
        )
        for distance, weight_ref in enumerate(weight_refs)
    ]
    start_all(copies)
    return copies


def finish_run(plan, copies, picks, mixed_ref, gathered_ref, refs, scratch):
    beta_layer, stream, group_blocks, part_count, sub, home, last = plan
    weight = scratch[0]
    rows, part_width, block = mixed_ref.shape
    parts = gathered_ref.shape[0]
    wait_all(copies)
    for row in range(0, rows, 2):
        span = range(row, min(row + 2, rows))
        right = jnp.concatenate(
            [jnp.concatenate([gathered_ref[p, r] for p in range(parts)], 0) for r in span], 1
        )
        product = jnp.dot(weight[...], right, preferred_element_type=jnp.float32)
        for place, r in enumerate(span):
            value = (1.0 - beta_layer) * mixed_ref[r].astype(jnp.float32) + beta_layer * product[
                :, place * block : (place + 1) * block
            ]
            value = jnp.maximum(value, 0.0).astype(jnp.bfloat16)
            if last:
                low = (stream[0] * group_blocks + r) * block
                refs[0][low : low + block, :] = value.T
            else:
                refs[0][r] = value
    if not last:
        pick_outgoing(picks, refs[0], refs[1], stream, group_blocks, part_count)


def finish_kernel(plan, picks, info, mixed_ref, gathered_ref, *refs):
    parts = gathered_ref.shape[0]
    weight_refs, out_refs, scratch = refs[:parts], refs[parts:-2], refs[-2:]
    copies = finish_begin(plan, info, weight_refs, scratch)
    finish_run(plan, copies, picks, mixed_ref, gathered_ref, out_refs, scratch)
    out_refs[2][...] = jnp.zeros_like(out_refs[2])


def last_kernel(plans, picks, info, *refs):
    parts = refs[1].shape[0]
    weight_refs, out_ref = refs[4 : 4 + parts], refs[4 + parts]
    scratch = refs[5 + parts :]
    copies = finish_begin(plans[0], info, weight_refs, scratch)
    for index, plan in enumerate(plans):
        mixed_ref, gathered_ref = refs[2 * index : 2 * index + 2]
        finish_run(plan, copies, picks, mixed_ref, gathered_ref, [out_ref], scratch)
        copies = []


def finish_plan(layer, depth, stream, group_blocks, part_count, last):
    beta_layer = math.log(lambda_decay / (layer + 1) + 1.0)
    return (beta_layer, stream, group_blocks, part_count, layer % depth, layer // depth, last)


def finish_scratch(weights):
    return [
        pltpu.VMEM(weights[0].shape[1:], jnp.bfloat16),
        pltpu.SemaphoreType.DMA((len(weights),)),
    ]


def finish_last(picks, section, pairs, weights, layer, depth, streams, group_blocks, part_count):
    plans = [finish_plan(layer, depth, s, group_blocks, part_count, True) for s in streams]
    rows = sum(mixed.shape[0] * mixed.shape[2] for mixed, gathered in pairs)
    shape = (rows, pairs[0][0].shape[1])
    return pl.pallas_call(
        functools.partial(last_kernel, plans),
        grid_spec=pltpu.PrefetchScalarGridSpec(
            num_scalar_prefetch=2,
            grid=(1,),
            in_specs=[whole(value.shape) for pair in pairs for value in pair]
            + [anywhere] * len(weights),
            out_specs=whole(shape),
            scratch_shapes=finish_scratch(weights),
        ),
        out_shape=jax.ShapeDtypeStruct(shape, jnp.bfloat16),
        compiler_params=params(),
        name="finish_last",
    )(picks, section, *[value for pair in pairs for value in pair], *weights)


def finish(picks, section, mixed, gathered, weights, layer, depth, stream, group_blocks, part_count):
    rows, part_width, block = mixed.shape
    width = weights[0].shape[2]
    plan = finish_plan(layer, depth, stream, group_blocks, part_count, False)
    outgoing = (part_count, len(stream), part_width, block)
    return pl.pallas_call(
        functools.partial(finish_kernel, plan),
        grid_spec=pltpu.PrefetchScalarGridSpec(
            num_scalar_prefetch=2,
            grid=(1,),
            in_specs=[whole(mixed.shape), whole(gathered.shape)] + [anywhere] * len(weights),
            out_specs=[whole(s) for s in [mixed.shape, outgoing, (16, 128)]],
            scratch_shapes=finish_scratch(weights),
        ),
        out_shape=[
            in_hbm(mixed.shape),
            jax.ShapeDtypeStruct(outgoing, jnp.bfloat16),
            in_hbm((16, 128)),
        ],
        cost_estimate=pl.CostEstimate(
            flops=2 * rows * block * width * part_width,
            bytes_accessed=rows * block * width * 2,
            transcendentals=0,
        ),
        compiler_params=params(),
        name="finish",
    )(picks, section, mixed, gathered, *weights)


def per_device(
    initial_features, layer_weights, adjacency_tiles, tile_columns, send_blocks, stale_imports
):
    section_count = lax.axis_size("section")
    part_count = lax.axis_size("dom")
    blocks_dev, fanout, block = adjacency_tiles.shape[:3]
    width = initial_features.shape[1]
    part_width = width // section_count
    groups = send_blocks.shape[1]
    group_blocks = blocks_dev // groups
    depth = layer_weights.shape[0]
    layers = depth * section_count
    streams = group_streams(groups)
    section = lax.axis_index("section").astype(jnp.int32).reshape(1)
    picks = send_blocks.reshape(-1)

    row_group = (jnp.arange(blocks_dev, dtype=jnp.int32) // group_blocks)[:, None]
    slot_group = (tile_columns - blocks_dev) // part_count
    is_stale = (tile_columns >= blocks_dev) & (slot_group > row_group)
    columns = jnp.where(
        is_stale, tile_columns + (groups - 1) * part_count, tile_columns
    ).reshape(-1)

    turned = [
        turn_blocks(section, stale_imports, (sub, 0), section_count) for sub in range(depth)
    ]
    started = prologue(
        initial_features, section, picks, turned[0][0], streams, group_blocks, block, part_width, part_count
    )
    own = started[: len(streams)]
    outgoing = started[len(streams) :]
    initial_blocks = own

    def exchange(value):
        return lax.all_to_all(value, "dom", split_axis=0, concat_axis=0, tiled=True)

    def spread(pieces):
        ring = range(section_count)
        return [pieces[0]] + [
            lax.ppermute(
                pieces[distance], "section", [(s, (s + distance) % section_count) for s in ring]
            )
            for distance in range(1, section_count)
        ]

    imports = [exchange(value) for value in outgoing]
    stale = [spread(pieces) for pieces in turned]
    weights = spread(turn_blocks(section, layer_weights[None], (0,), section_count))

    front, back = streams
    turned_late = [pieces[0] for pieces in turned[1:]]

    def parts_of(index, layer):
        return aggregate_parts(
            section, initial_blocks[index], adjacency_tiles, own, imports, stale[layer % depth],
            layer // depth, streams[index], streams, group_blocks, part_count,
        )

    own, imports = list(own), list(imports)
    shapes = [value.shape for value in initial_blocks]
    mixed_front = aggregate(columns, section, parts_of(0, 0), shapes[0], turned_late)
    for layer in range(layers):
        last = layer == layers - 1
        gathered_front = lax.all_gather(mixed_front, "section", axis=0, tiled=False)
        after = []
        if not last:
            front_result = finish(
                picks, section, mixed_front, gathered_front, weights, layer, depth, front,
                group_blocks, part_count,
            )
            after = [front_result[2]]
        mixed_back = aggregate(columns, section, parts_of(1, layer), shapes[1], after)
        gathered = lax.all_gather(mixed_back, "section", axis=0, tiled=False)
        if last:
            pairs = [(mixed_front, gathered_front), (mixed_back, gathered)]
            return finish_last(
                picks, section, pairs, weights, layer, depth, streams, group_blocks, part_count
            )
        own[0], imports[0] = front_result[0], exchange(front_result[1])
        own[1], outgoing, mixed_front = finish_and_aggregate(
            columns, picks, section, mixed_back, gathered, weights, layer, depth, back,
            group_blocks, part_count, parts_of(0, layer + 1), shapes[0],
        )
        imports[1] = exchange(outgoing)


def solution(mesh):
    return jax.shard_map(
        per_device,
        mesh=mesh,
        in_specs=(
            P("dom", None),
            P("section", None, None),
            P("dom", None, None, None),
            P("dom", None),
            P("dom", None, None),
            P("section", "dom", None, None, None),
        ),
        out_specs=P("dom", "section"),
        check_vma=False,
    )
```

```python
import functools
import math

import jax
import jax.numpy as jnp
from jax import lax
from jax.experimental import pallas as pl
from jax.experimental.pallas import tpu as pltpu
from jax.sharding import PartitionSpec as P

alpha_mix = 0.1
lambda_decay = 0.5
vmem_bytes = 48 * 1024 * 1024


def group_streams(groups):
    return [list(range(groups - 1)), [groups - 1]]


def params():
    return pltpu.CompilerParams(vmem_limit_bytes=vmem_bytes)


def in_hbm(shape):
    return pltpu.HBM(shape, jnp.bfloat16)


hbm = pl.BlockSpec(memory_space=pltpu.HBM)
anywhere = pl.BlockSpec(memory_space=pl.ANY)


def pinned(value):
    return pltpu.with_memory_space_constraint(value, pltpu.HBM)


def start_all(copies):
    for condition, copy in copies:
        if condition is None:
            copy.start()
        else:
            pl.when(condition)(copy.start)


def wait_all(copies):
    for condition, copy in copies:
        if condition is None:
            copy.wait()
        else:
            pl.when(condition)(copy.wait)


def whole(shape):
    return pl.BlockSpec(shape, lambda i, *prefetched: (0,) * len(shape))


def pick_outgoing(picks, blocks_ref, outgoing_ref, stream, group_blocks, part_count):
    for local, group in enumerate(stream):

        def pick(dest, carry):
            chosen = jnp.maximum(picks[group * part_count + dest], 0)
            outgoing_ref[dest, local] = blocks_ref[local * group_blocks + chosen]
            return carry

        lax.fori_loop(0, part_count, pick, 0)


def prologue_kernel(streams, group_blocks, part_count, info, picks, rows_ref, unused, *refs):
    own_refs = refs[: len(streams)]
    outgoing_refs = refs[len(streams) : 2 * len(streams)]
    turned = refs[-1]
    block = own_refs[0].shape[2]
    part_width = own_refs[0].shape[1]
    first = pl.multiple_of(info[0] * part_width, part_width)
    for stream, own_ref, outgoing_ref in zip(streams, own_refs, outgoing_refs):
        for local in range(len(stream) * group_blocks):
            row = (stream[0] * group_blocks + local) * block
            turned[local % 2] = rows_ref[row : row + block, :].T
            own_ref[local] = turned[local % 2, pl.ds(first, part_width), :]
        pick_outgoing(picks, own_ref, outgoing_ref, stream, group_blocks, part_count)


def prologue(initial_features, section, picks, after, streams, group_blocks, block, part_width, part_count):
    rows, width = initial_features.shape
    own_shapes = [(len(s) * group_blocks, part_width, block) for s in streams]
    out_shapes = [(part_count, len(s), part_width, block) for s in streams]
    return pl.pallas_call(
        functools.partial(prologue_kernel, streams, group_blocks, part_count),
        grid_spec=pltpu.PrefetchScalarGridSpec(
            num_scalar_prefetch=2,
            grid=(1,),
            in_specs=[whole((rows, width)), hbm],
            out_specs=[whole(s) for s in own_shapes + out_shapes],
            scratch_shapes=[pltpu.VMEM((2, width, block), jnp.bfloat16)],
        ),
        out_shape=[in_hbm(s) for s in own_shapes]
        + [jax.ShapeDtypeStruct(s, jnp.bfloat16) for s in out_shapes],
        compiler_params=params(),
        name="prologue",
    )(section, picks, pinned(initial_features), pinned(after))


def turn_kernel(info, in_ref, *refs):
    *out_refs, turned = refs
    count = in_ref.shape[-3]
    sections, part_width = len(out_refs), out_refs[0].shape[1]
    for item in range(count):
        turned[item % 2] = in_ref[0, item].T if len(in_ref.shape) == 4 else in_ref[0, 0, item].T
        for distance, out_ref in enumerate(out_refs):
            owner = lax.rem(info[0] + distance, sections)
            first = pl.multiple_of(owner * part_width, part_width)
            out_ref[item] = turned[item % 2, pl.ds(first, part_width), :]


def turn_blocks(section, blocks, lead, sections):
    count, rows, width = blocks.shape[-3:]
    step = 8 if count % 8 == 0 else count
    part_width = width // sections
    block_shape = (1,) * (len(blocks.shape) - 3) + (step, rows, width)
    out_spec = pl.BlockSpec((step, part_width, rows), lambda i, *prefetched: (i, 0, 0))
    return pl.pallas_call(
        turn_kernel,
        grid_spec=pltpu.PrefetchScalarGridSpec(
            num_scalar_prefetch=1,
            grid=(count // step,),
            in_specs=[pl.BlockSpec(block_shape, lambda i, *prefetched: lead + (i, 0, 0))],
            out_specs=[out_spec] * sections,
            scratch_shapes=[pltpu.VMEM((2, width, rows), jnp.bfloat16)],
        ),
        out_shape=[in_hbm((count, part_width, rows))] * sections,
        compiler_params=params(),
        name="turn",
    )(section, pinned(blocks))


class Aggregate:
    def __init__(self, plan, columns, info, initial_ref, tiles_ref, source_refs, mixed_ref, scratch):
        self.stream, self.group_blocks, self.fanout, sources, home, sections = plan
        self.columns, self.tiles_ref, self.mixed_ref = columns, tiles_ref, mixed_ref
        self.table, self.tiles, self.initial, table_sem, self.tiles_sem, initial_sem = scratch
        self.rows = len(self.stream) * self.group_blocks
        self.first_row = self.stream[0] * self.group_blocks
        self.ahead = min(4, self.rows)
        self.initial_copy = pltpu.make_async_copy(initial_ref, self.initial, initial_sem)
        self.copies = []
        for index, (kind, target, detail) in enumerate(sources):
            ref = source_refs[index]
            source = ref.at[:, detail] if kind == "import" else ref
            condition = None
            if kind == "stale":
                condition = lax.rem(info[0] - home + 2 * sections, sections) == detail
            part = self.table.at[pl.ds(target, source.shape[0])]
            copy = pltpu.make_async_copy(source, part, table_sem.at[index])
            self.copies.append((condition, copy))

    def tile_copy(self, row):
        return pltpu.make_async_copy(
            self.tiles_ref.at[self.first_row + row], self.tiles.at[row], self.tiles_sem.at[row]
        )

    def begin(self):
        start_all(self.copies)
        for row in range(self.ahead):
            self.tile_copy(row).start()
        self.initial_copy.start()

    def run(self):
        wait_all(self.copies)
        self.initial_copy.wait()

        def one_row(row, carry):
            self.tile_copy(row).wait()

            @pl.when(row + self.ahead < self.rows)
            def _():
                self.tile_copy(row + self.ahead).start()

            base = (self.first_row + row) * self.fanout
            total = None
            for tile in range(0, self.fanout, 2):
                span = range(tile, min(tile + 2, self.fanout))
                left = jnp.concatenate([self.table[self.columns[base + t]] for t in span], 1)
                right = jnp.concatenate([self.tiles[row, t] for t in span], 1)
                term = lax.dot_general(
                    left, right, (((1,), (1,)), ((), ())), preferred_element_type=jnp.float32
                )
                total = term if total is None else total + term
            start = self.initial[row].astype(jnp.float32)
            self.mixed_ref[row] = ((1.0 - alpha_mix) * total + alpha_mix * start).astype(
                jnp.bfloat16
            )
            return carry

        lax.fori_loop(0, self.rows, one_row, 0)


def aggregate_kernel(plan, columns, info, initial_ref, tiles_ref, *refs):
    count = len(plan[3])
    work = Aggregate(plan, columns, info, initial_ref, tiles_ref, refs[:count], refs[-7], refs[-6:])
    work.begin()
    work.run()


def both_kernel(plan, aggregate_plan, columns, picks, info, mixed_ref, gathered_ref, *refs):
    parts = gathered_ref.shape[0]
    count = len(aggregate_plan[3])
    weight_refs, refs = refs[:parts], refs[parts:]
    initial_ref, tiles_ref = refs[:2]
    source_refs, refs = refs[2 : 2 + count], refs[2 + count :]
    own_ref, outgoing_ref, next_ref = refs[:3]
    scratch = refs[3:5]
    work = Aggregate(
        aggregate_plan, columns, info, initial_ref, tiles_ref, source_refs, next_ref, refs[5:]
    )
    work.begin()
    copies = finish_begin(plan, info, weight_refs, scratch)
    finish_run(plan, copies, picks, mixed_ref, gathered_ref, [own_ref, outgoing_ref], scratch)
    work.run()


def aggregate_parts(section, initial_blocks, tiles, own, imports, stale, home, stream, streams, group_blocks, part_count):
    rows, part_width, block = initial_blocks.shape
    blocks_dev, fanout = tiles.shape[:2]
    groups = blocks_dev // group_blocks
    sources, operands, specs = [], [], []
    for other, own_blocks, imported in zip(streams, own, imports):
        if other[0] > stream[-1]:
            continue
        sources.append(("own", other[0] * group_blocks, None))
        operands.append(pinned(own_blocks))
        specs.append(hbm)
        for local, group in enumerate(other):
            sources.append(("import", blocks_dev + group * part_count, local))
            operands.append(imported)
            specs.append(anywhere)
    if groups > 1 and stream[0] < groups - 1:
        for distance, stale_blocks in enumerate(stale):
            sources.append(("stale", blocks_dev + groups * part_count, distance))
            operands.append(pinned(stale_blocks))
            specs.append(hbm)
    table_size = blocks_dev + (2 * groups - 1) * part_count
    plan = (stream, group_blocks, fanout, sources, home, len(stale))
    scratch = [
        pltpu.VMEM((table_size, part_width, block), jnp.bfloat16),
        pltpu.VMEM((rows, fanout, block, block), jnp.bfloat16),
        pltpu.VMEM(initial_blocks.shape, jnp.bfloat16),
        pltpu.SemaphoreType.DMA((len(sources),)),
        pltpu.SemaphoreType.DMA((rows,)),
        pltpu.SemaphoreType.DMA,
    ]
    operands = [pinned(initial_blocks), pinned(tiles)] + operands
    return plan, operands, [hbm, hbm] + specs, scratch


def estimate(rows, fanout, block, part_width, width):
    return pl.CostEstimate(
        flops=2 * rows * block * part_width * (fanout * block + width),
        bytes_accessed=rows * fanout * block * block * 2,
        transcendentals=0,
    )


def aggregate(columns, section, parts, shape, after):
    plan, operands, specs, scratch = parts
    operands = operands + [pinned(value) for value in after]
    return pl.pallas_call(
        functools.partial(aggregate_kernel, plan),
        grid_spec=pltpu.PrefetchScalarGridSpec(
            num_scalar_prefetch=2,
            grid=(1,),
            in_specs=specs + [hbm] * len(after),
            out_specs=whole(shape),
            scratch_shapes=scratch,
        ),
        out_shape=jax.ShapeDtypeStruct(shape, jnp.bfloat16),
        cost_estimate=estimate(shape[0], plan[2], shape[2], shape[1], 0),
        compiler_params=params(),
        name="aggregate",
    )(columns, section, *operands)


def finish_and_aggregate(columns, picks, section, mixed, gathered, weights, layer, depth, stream, group_blocks, part_count, parts, shape):
    aggregate_plan, operands, specs, scratch = parts
    rows, part_width, block = mixed.shape
    width = weights[0].shape[2]
    plan = finish_plan(layer, depth, stream, group_blocks, part_count, False)
    outgoing = (part_count, len(stream), part_width, block)
    return pl.pallas_call(
        functools.partial(both_kernel, plan, aggregate_plan),
        grid_spec=pltpu.PrefetchScalarGridSpec(
            num_scalar_prefetch=3,
            grid=(1,),
            in_specs=[whole(mixed.shape), whole(gathered.shape)]
            + [anywhere] * len(weights)
            + specs,
            out_specs=[whole(mixed.shape), whole(outgoing), whole(shape)],
            scratch_shapes=finish_scratch(weights) + scratch,
        ),
        out_shape=[
            in_hbm(mixed.shape),
            jax.ShapeDtypeStruct(outgoing, jnp.bfloat16),
            jax.ShapeDtypeStruct(shape, jnp.bfloat16),
        ],
        cost_estimate=estimate(shape[0], aggregate_plan[2], block, part_width, width),
        compiler_params=params(),
        name="finish_aggregate",
    )(columns, picks, section, mixed, gathered, *weights, *operands)


def finish_begin(plan, info, weight_refs, scratch):
    parts = len(weight_refs)
    sub, home = plan[4:6]
    weight, sem = scratch
    copies = [
        (
            lax.rem(info[0] - home + 2 * parts, parts) == distance,
            pltpu.make_async_copy(weight_ref.at[sub], weight, sem.at[distance]),
        )
        for distance, weight_ref in enumerate(weight_refs)
    ]
    start_all(copies)
    return copies


def finish_run(plan, copies, picks, mixed_ref, gathered_ref, refs, scratch):
    beta_layer, stream, group_blocks, part_count, sub, home, last = plan
    weight = scratch[0]
    rows, part_width, block = mixed_ref.shape
    parts = gathered_ref.shape[0]
    wait_all(copies)
    for row in range(0, rows, 2):
        span = range(row, min(row + 2, rows))
        right = jnp.concatenate(
            [jnp.concatenate([gathered_ref[p, r] for p in range(parts)], 0) for r in span], 1
        )
        product = jnp.dot(weight[...], right, preferred_element_type=jnp.float32)
        for place, r in enumerate(span):
            value = (1.0 - beta_layer) * mixed_ref[r].astype(jnp.float32) + beta_layer * product[
                :, place * block : (place + 1) * block
            ]
            value = jnp.maximum(value, 0.0).astype(jnp.bfloat16)
            if last:
                low = (stream[0] * group_blocks + r) * block
                refs[0][low : low + block, :] = value.T
            else:
                refs[0][r] = value
    if not last:
        pick_outgoing(picks, refs[0], refs[1], stream, group_blocks, part_count)


def finish_kernel(plan, picks, info, mixed_ref, gathered_ref, *refs):
    parts = gathered_ref.shape[0]
    weight_refs, out_refs, scratch = refs[:parts], refs[parts:-2], refs[-2:]
    copies = finish_begin(plan, info, weight_refs, scratch)
    finish_run(plan, copies, picks, mixed_ref, gathered_ref, out_refs, scratch)
    out_refs[2][...] = jnp.zeros_like(out_refs[2])


def last_kernel(plans, picks, info, *refs):
    parts = refs[1].shape[0]
    weight_refs, out_ref = refs[4 : 4 + parts], refs[4 + parts]
    scratch = refs[5 + parts :]
    copies = finish_begin(plans[0], info, weight_refs, scratch)
    for index, plan in enumerate(plans):
        mixed_ref, gathered_ref = refs[2 * index : 2 * index + 2]
        finish_run(plan, copies, picks, mixed_ref, gathered_ref, [out_ref], scratch)
        copies = []


def finish_plan(layer, depth, stream, group_blocks, part_count, last):
    beta_layer = math.log(lambda_decay / (layer + 1) + 1.0)
    return (beta_layer, stream, group_blocks, part_count, layer % depth, layer // depth, last)


def finish_scratch(weights):
    return [
        pltpu.VMEM(weights[0].shape[1:], jnp.bfloat16),
        pltpu.SemaphoreType.DMA((len(weights),)),
    ]


def finish_last(picks, section, pairs, weights, layer, depth, streams, group_blocks, part_count):
    plans = [finish_plan(layer, depth, s, group_blocks, part_count, True) for s in streams]
    rows = sum(mixed.shape[0] * mixed.shape[2] for mixed, gathered in pairs)
    shape = (rows, pairs[0][0].shape[1])
    return pl.pallas_call(
        functools.partial(last_kernel, plans),
        grid_spec=pltpu.PrefetchScalarGridSpec(
            num_scalar_prefetch=2,
            grid=(1,),
            in_specs=[whole(value.shape) for pair in pairs for value in pair]
            + [anywhere] * len(weights),
            out_specs=whole(shape),
            scratch_shapes=finish_scratch(weights),
        ),
        out_shape=jax.ShapeDtypeStruct(shape, jnp.bfloat16),
        compiler_params=params(),
        name="finish_last",
    )(picks, section, *[value for pair in pairs for value in pair], *weights)


def finish(picks, section, mixed, gathered, weights, layer, depth, stream, group_blocks, part_count):
    rows, part_width, block = mixed.shape
    width = weights[0].shape[2]
    plan = finish_plan(layer, depth, stream, group_blocks, part_count, False)
    outgoing = (part_count, len(stream), part_width, block)
    return pl.pallas_call(
        functools.partial(finish_kernel, plan),
        grid_spec=pltpu.PrefetchScalarGridSpec(
            num_scalar_prefetch=2,
            grid=(1,),
            in_specs=[whole(mixed.shape), whole(gathered.shape)] + [anywhere] * len(weights),
            out_specs=[whole(s) for s in [mixed.shape, outgoing, (16, 128)]],
            scratch_shapes=finish_scratch(weights),
        ),
        out_shape=[
            in_hbm(mixed.shape),
            jax.ShapeDtypeStruct(outgoing, jnp.bfloat16),
            in_hbm((16, 128)),
        ],
        cost_estimate=pl.CostEstimate(
            flops=2 * rows * block * width * part_width,
            bytes_accessed=rows * block * width * 2,
            transcendentals=0,
        ),
        compiler_params=params(),
        name="finish",
    )(picks, section, mixed, gathered, *weights)


def per_device(
    initial_features, layer_weights, adjacency_tiles, tile_columns, send_blocks, stale_imports
):
    section_count = lax.axis_size("section")
    part_count = lax.axis_size("dom")
    blocks_dev, fanout, block = adjacency_tiles.shape[:3]
    width = initial_features.shape[1]
    part_width = width // section_count
    groups = send_blocks.shape[1]
    group_blocks = blocks_dev // groups
    depth = layer_weights.shape[0]
    layers = depth * section_count
    streams = group_streams(groups)
    section = lax.axis_index("section").astype(jnp.int32).reshape(1)
    picks = send_blocks.reshape(-1)

    row_group = (jnp.arange(blocks_dev, dtype=jnp.int32) // group_blocks)[:, None]
    slot_group = (tile_columns - blocks_dev) // part_count
    is_stale = (tile_columns >= blocks_dev) & (slot_group > row_group)
    columns = jnp.where(
        is_stale, tile_columns + (groups - 1) * part_count, tile_columns
    ).reshape(-1)

    turned = [
        turn_blocks(section, stale_imports, (sub, 0), section_count) for sub in range(depth)
    ]
    started = prologue(
        initial_features, section, picks, turned[0][0], streams, group_blocks, block, part_width, part_count
    )
    own = started[: len(streams)]
    outgoing = started[len(streams) :]
    initial_blocks = own

    def exchange(value):
        return lax.all_to_all(value, "dom", split_axis=0, concat_axis=0, tiled=True)

    def spread(pieces):
        ring = range(section_count)
        return [pieces[0]] + [
            lax.ppermute(
                pieces[distance], "section", [(s, (s + distance) % section_count) for s in ring]
            )
            for distance in range(1, section_count)
        ]

    imports = [exchange(value) for value in outgoing]
    stale = [spread(pieces) for pieces in turned]
    weights = spread(turn_blocks(section, layer_weights[None], (0,), section_count))

    front, back = streams
    turned_late = [pieces[0] for pieces in turned[1:]]

    def parts_of(index, layer):
        return aggregate_parts(
            section, initial_blocks[index], adjacency_tiles, own, imports, stale[layer % depth],
            layer // depth, streams[index], streams, group_blocks, part_count,
        )

    own, imports = list(own), list(imports)
    shapes = [value.shape for value in initial_blocks]
    mixed_front = aggregate(columns, section, parts_of(0, 0), shapes[0], turned_late)
    for layer in range(layers):
        last = layer == layers - 1
        gathered_front = lax.all_gather(mixed_front, "section", axis=0, tiled=False)
        after = []
        if not last:
            front_result = finish(
                picks, section, mixed_front, gathered_front, weights, layer, depth, front,
                group_blocks, part_count,
            )
            after = [front_result[2]]
        mixed_back = aggregate(columns, section, parts_of(1, layer), shapes[1], after)
        gathered = lax.all_gather(mixed_back, "section", axis=0, tiled=False)
        if last:
            pairs = [(mixed_front, gathered_front), (mixed_back, gathered)]
            return finish_last(
                picks, section, pairs, weights, layer, depth, streams, group_blocks, part_count
            )
        own[0], imports[0] = front_result[0], exchange(front_result[1])
        own[1], outgoing, mixed_front = finish_and_aggregate(
            columns, picks, section, mixed_back, gathered, weights, layer, depth, back,
            group_blocks, part_count, parts_of(0, layer + 1), shapes[0],
        )
        imports[1] = exchange(outgoing)


def solution(mesh):
    return jax.shard_map(
        per_device,
        mesh=mesh,
        in_specs=(
            P("dom", None),
            P("section", None, None),
            P("dom", None, None, None),
            P("dom", None),
            P("dom", None, None),
            P("section", "dom", None, None, None),
        ),
        out_specs=P("dom", "section"),
        check_vma=False,
    )
```
